256 devices in a mesh: tok: 16 (over y, x), gr: 2 (over z_hi), gc: 8 (over z_lo, core).
Axes of the slice: x: 4, y: 4, z: 8 (z_hi: 2, z_lo: 4; z = z_hi * 4 + z_lo), core: 2. Of those that a mesh axis runs over, the one named last changes fastest.
Arguments:
- acts: bfloat16 [2048, 16384], P('tok', ('gr', 'gc')), may hold values from -24 to 24
- init_basis: float32 [16, 1024, 512], P(('gr', 'gc'), 'tok'), may hold values from -6 to 6
- kept: int32 [16, 16], replicated, may hold values from 0 to 1, as said below
- member: int32 [16], replicated, may hold values from 0 to 1, as said below
Outputs:
- bases: float32 [16, 1024, 512], P(('gr', 'gc'), 'tok')
- latent: bfloat16 [2048, 1024], P(('tok', 'gr', 'gc'))
The draws below stay inside these ranges and needn't reach their ends.
Inputs may be any that keep to these rules, and one draw needn't show every extreme that they name: kept is symmetric with ones on the diagonal. `member`: each of the 2 group numbers names exactly 8 blocks.
All inputs are finite; a program needn't handle non-finite values.
Results may differ from the reference program's by a relative error of at most 0.0095.
Values may be sent and summed in bfloat16 or wider, within the bound.
A program may use at most 64 MiB of HBM per device.

```python
import math
import jax
import jax.numpy as jnp
from jax import lax

BLK = 1024
RANK = 512
NBLK = 16
GBLK = 8
ITERS = 2
TOKENS = 2048
COLS = 16384
NGRP = 2
GCOLS = 8192


def draw_acts(key, part):
    key = jax.random.fold_in(key, 37)
    noise_key, order_key = jax.random.split(key)
    noise = jnp.clip(jax.random.normal(noise_key, (TOKENS, COLS), jnp.float32), -6.0, 6.0)
    order = jax.random.permutation(order_key, NBLK).astype(jnp.float32)
    block_scale = jnp.exp(jnp.log(4.0) * order / (NBLK - 1))
    within = jnp.arange(BLK, dtype=jnp.float32) / (BLK - 1)
    row_scale = jnp.exp(jnp.log(16.0) * within)
    column_scale = (block_scale[:, None] * row_scale[None, :]).reshape(COLS) / 16.0
    return (noise * column_scale[None, :]).astype(jnp.bfloat16)


def draw_kept(key, part):
    key = jax.random.fold_in(key, 23)
    coins = jax.random.randint(key, (NBLK, NBLK), 0, 2, dtype=jnp.int32)
    upper = jnp.triu(coins, 1)
    return (upper + upper.T + jnp.eye(NBLK, dtype=jnp.int32)).astype(jnp.int32)


def draw_member(key, part):
    key = jax.random.fold_in(key, 11)
    labels = jnp.arange(NBLK, dtype=jnp.int32) // GBLK
    return jax.random.permutation(key, labels).astype(jnp.int32)


def level_of(stream_key, shape, pieces, low, top_value):
    factor_of = 1.0
    for dim, blocks in pieces:
        steps = jax.random.uniform(jax.random.fold_in(jax.random.fold_in(stream_key, 6), dim), (blocks,), jnp.float32, low / len(pieces), top_value / len(pieces))
        factor_of = factor_of * jnp.repeat(jnp.exp(steps), shape[dim] // blocks).reshape((-1,) + (1,) * (len(shape) - 1 - dim))
    return factor_of


def normal_values(key, dims, deviation, bound, cuts=(), kind=jnp.bfloat16):
    values = deviation * jax.random.normal(key, dims, jnp.float32)
    if cuts:
        values = values * level_of(key, dims, cuts, -0.22, 0.18)
    return jnp.clip(values, -bound, bound).astype(kind)


def setup_inputs(seed: int = 0) -> dict:
    splits = jax.random.split(jax.random.key(seed), 5)
    acts = draw_acts(jax.random.fold_in(splits[4], 71), 0)
    init_basis = normal_values(splits[1], (NBLK, BLK, RANK), 1.0, 6.0, ((0, 16), (1, 16)), jnp.float32)
    kept = draw_kept(jax.random.fold_in(splits[4], 71), 0)
    member = draw_member(jax.random.fold_in(splits[4], 71), 0)
    return {"acts": acts, "init_basis": init_basis, "kept": kept, "member": member}


def project(pair):
    return jnp.dot(pair[0].astype(jnp.float32), pair[1].astype(jnp.float32), preferred_element_type=jnp.float32)

def reference(acts, init_basis, kept, member):
    highest = lax.Precision.HIGHEST
    blocks_x = acts.reshape(TOKENS, NBLK, BLK).transpose(1, 0, 2)
    links = ((member[:, None] == member[None, :]).astype(jnp.int32) * kept).astype(jnp.float32)
    selector = (member[:, None] == jnp.arange(NGRP, dtype=jnp.int32)[None, :]).astype(jnp.float32)
    basis = init_basis
    for step in range(ITERS):
        basis_bf = basis.astype(jnp.bfloat16)
        proj = lax.map(project, (blocks_x, basis_bf)).astype(jnp.bfloat16)
        proj_wide = proj.astype(jnp.float32)

        def combine_row(row):
            return jnp.tensordot(row, proj_wide, axes=1, precision=highest).astype(jnp.bfloat16)
        mixed = lax.map(combine_row, links)

        def cover(pair):
            return jnp.dot(pair[0].T.astype(jnp.float32), pair[1].astype(jnp.float32), preferred_element_type=jnp.float32)
        image = lax.map(cover, (blocks_x, mixed)) / TOKENS + 2.0 * basis_bf.astype(jnp.float32)
        grams = jnp.einsum('irb,irs->ibs', image, image, precision=highest)
        gram = jnp.einsum('ig,ibs->gbs', selector, grams, precision=highest)
        lower = jnp.linalg.cholesky(gram / GCOLS)
        own_lower = jnp.einsum('ig,gbs->ibs', selector, lower, precision=highest)

        def solve_one(pair):
            return jax.scipy.linalg.solve_triangular(pair[0], pair[1].T, lower=True).T
        basis = lax.map(solve_one, (own_lower, image))
    codes = lax.map(project, (blocks_x, basis.astype(jnp.bfloat16)))
    latent = jnp.einsum('jg,jtr->tgr', selector, codes, precision=highest).reshape(TOKENS, NGRP * RANK)
    latent = latent * (1.0 / math.sqrt(GCOLS))
    return (basis, latent.astype(jnp.bfloat16))
```

```python
import functools
import math

import jax
import jax.numpy as jnp
from jax import lax
from jax.experimental import pallas as pl
from jax.experimental.pallas import tpu as pltpu
from jax.sharding import PartitionSpec as P

GBLK = 8
ITERS = 2
RIDGE = 2.0
LEAF = 128
MESH = pl.DeviceIdType.MESH
HIGHEST = lax.Precision.HIGHEST
VMEM_LIMIT = 48 * 2**20
F32 = jnp.float32
BF16 = jnp.bfloat16


def vmem():
    return pl.BlockSpec(memory_space=pltpu.VMEM)


def smem():
    return pl.BlockSpec(memory_space=pltpu.SMEM)


def params(collective_id=None):
    if collective_id is None:
        return pltpu.CompilerParams(vmem_limit_bytes=VMEM_LIMIT)
    return pltpu.CompilerParams(
        vmem_limit_bytes=VMEM_LIMIT, collective_id=collective_id, has_side_effects=True
    )


class Place:
    def __init__(self):
        self.tok = lax.axis_size("tok")
        self.gc = lax.axis_size("gc")
        self.line = lax.axis_size("gr") * self.gc
        self.side = math.isqrt(self.tok)
        self.p = lax.axis_index("tok")
        self.gr_at = lax.axis_index("gr")
        self.gc_at = lax.axis_index("gc")
        self.k = self.gr_at * self.gc + self.gc_at
        self.y = self.p // self.side
        self.x = self.p % self.side

    def in_plane(self, p):
        return (p, self.gr_at, self.gc_at)

    def in_line(self, k):
        return (self.p, k // self.gc, k % self.gc)

    def at_axis(self, axis, at):
        if axis == "x":
            return self.in_plane(self.y * self.side + at)
        return self.in_plane(at * self.side + self.x)


def greet(devices):
    barrier = pltpu.get_barrier_semaphore()
    for device in devices:
        pl.semaphore_signal(barrier, inc=1, device_id=device, device_id_type=MESH)
    if devices:
        pl.semaphore_wait(barrier, len(devices))


def line_devices(here):
    return [here.in_line((here.k + d) % here.line) for d in range(1, here.line)]


def plane_devices(here):
    return [here.in_plane((here.p + d) % here.tok) for d in range(1, here.tok)]


def ring_devices(here):
    if here.tok == 1:
        return []
    side = here.side
    return [
        here.at_axis(axis, (at + d) % side)
        for axis, at in (("x", here.x), ("y", here.y))
        for d in (1, side - 1)
    ]


def rcopy(src, dst, send, recv, device):
    return pltpu.make_async_remote_copy(
        src_ref=src, dst_ref=dst, send_sem=send, recv_sem=recv, device_id=device, device_id_type=MESH
    )


class Ring:
    def __init__(self, here, axis, piece, send, recv):
        at = here.x if axis == "x" else here.y
        side = here.side
        self.me, self.right, self.left = at, (at + 1) % side, (at + side - 1) % side
        self.opp = (at + 2) % side
        self.to_right = here.at_axis(axis, self.right)
        self.to_left = here.at_axis(axis, self.left)
        self.piece, self.send, self.recv = piece, send, recv

    def copy(self, slot, owner, part, device):
        ref = self.piece(owner, part)
        return rcopy(ref, ref, self.send.at[slot], self.recv.at[slot], device)

    def start(self):
        self.copy(0, self.me, 0, self.to_right).start()
        self.copy(1, self.me, 1, self.to_left).start()
        self.copy(2, self.me, 1, self.to_right).start()
        self.copy(3, self.me, 0, self.to_left).start()

    def forward(self):
        self.copy(0, self.left, 0, self.to_right).wait_recv()
        self.copy(4, self.left, 0, self.to_right).start()
        self.copy(1, self.right, 1, self.to_left).wait_recv()
        self.copy(5, self.right, 1, self.to_left).start()

    def finish(self):
        self.copy(2, self.left, 1, self.to_right).wait_recv()
        self.copy(3, self.right, 0, self.to_left).wait_recv()
        self.copy(4, self.opp, 0, self.to_right).wait_recv()
        self.copy(5, self.opp, 1, self.to_left).wait_recv()

    def sent(self):
        self.copy(0, self.me, 0, self.to_right).wait_send()
        self.copy(1, self.me, 1, self.to_left).wait_send()
        self.copy(2, self.me, 1, self.to_right).wait_send()
        self.copy(3, self.me, 0, self.to_left).wait_send()
        self.copy(4, self.left, 0, self.to_right).wait_send()
        self.copy(5, self.right, 1, self.to_left).wait_send()


def plane_rings(here, buf, send, recv):
    y, x = here.y, here.x
    return (
        Ring(here, "x", lambda at, part: buf.at[y, at, part], send.at[0], recv.at[0]),
        Ring(here, "y", lambda at, part: buf.at[at, x, 2 + part], send.at[1], recv.at[1]),
        Ring(here, "y", lambda at, part: buf.at[at, :, part], send.at[2], recv.at[2]),
        Ring(here, "x", lambda at, part: buf.at[:, at, 2 + part], send.at[3], recv.at[3]),
    )


def plane_gather_start(here, buf, send, recv):
    if here.tok > 1:
        one_a, one_b, _, _ = plane_rings(here, buf, send, recv)
        one_a.start()
        one_b.start()


def plane_gather_finish(here, buf, send, recv):
    if here.tok > 1:
        one_a, one_b, two_a, two_b = plane_rings(here, buf, send, recv)
        one_a.forward()
        one_b.forward()
        one_a.finish()
        two_a.start()
        one_b.finish()
        two_b.start()
        two_a.forward()
        two_b.forward()
        two_a.finish()
        two_b.finish()


def plane_gather_sent(here, buf, send, recv):
    if here.tok > 1:
        for ring in plane_rings(here, buf, send, recv):
            ring.sent()


def ring_semaphores():
    return [pltpu.SemaphoreType.DMA((4, 6)), pltpu.SemaphoreType.DMA((4, 6))]


def line_semaphores(count):
    return [pltpu.SemaphoreType.DMA((count,)), pltpu.SemaphoreType.DMA((count,))]


def line_copy(here, src, dst, send, recv, to):
    return rcopy(src.at[to], dst.at[here.k], send.at[to], recv.at[here.k], here.in_line(to))


def line_received(here, src, dst, send, recv):
    def body(d, carry):
        other = (here.k + here.line - d) % here.line
        rcopy(
            src.at[other], dst.at[other], send.at[other], recv.at[other], here.in_line(other)
        ).wait_recv()
        return carry

    lax.fori_loop(1, here.line, body, 0)


def line_sent(here, src, dst, send, recv):
    def body(d, carry):
        line_copy(here, src, dst, send, recv, (here.k + d) % here.line).wait_send()
        return carry

    lax.fori_loop(1, here.line, body, 0)


def start_kernel(acts_ref, init_ref, full_ref, basis_ref, out_tiles, in_tiles, xs, xr, bs, br):
    here = Place()
    rows = init_ref.shape[0]
    rank = init_ref.shape[1] // here.tok
    full_ref[here.y, here.x] = acts_ref[...].reshape(full_ref.shape[2:])
    turned = init_ref[...].T
    if here.tok == 1:
        basis_ref[...] = turned.astype(BF16)
        return
    wide = jnp.concatenate([turned, jnp.zeros((turned.shape[0], 128 - rows), F32)], axis=1)
    out_tiles[...] = wide.astype(BF16).reshape(out_tiles.shape)
    greet(plane_devices(here))
    plane_gather_start(here, full_ref, xs, xr)

    def copy(to):
        return rcopy(
            out_tiles.at[to], in_tiles.at[here.p], bs.at[to], br.at[here.p], here.in_plane(to)
        )

    def send(d, carry):
        copy((here.p + d) % here.tok).start()
        return carry

    lax.fori_loop(1, here.tok, send, 0)
    in_tiles[here.p] = out_tiles[here.p]
    plane_gather_finish(here, full_ref, xs, xr)

    def received(d, carry):
        other = (here.p + here.tok - d) % here.tok
        rcopy(
            out_tiles.at[other], in_tiles.at[other], bs.at[other], br.at[other], here.in_plane(other)
        ).wait_recv()
        copy((here.p + d) % here.tok).wait_send()
        return carry

    lax.fori_loop(1, here.tok, received, 0)
    per = 128 // rows
    for c in range(here.tok // per):
        total = in_tiles[c * per].astype(F32)
        for d in range(1, per):
            total += pltpu.roll(in_tiles[c * per + d].astype(F32), d * rows, 1)
        basis_ref[:, c * 128 : c * 128 + 128] = total.astype(BF16)
    plane_gather_sent(here, full_ref, xs, xr)


def start(acts, init):
    tok = lax.axis_size("tok")
    side = math.isqrt(tok)
    tokens, cols = acts.shape
    rows, rank = init.shape
    return pl.pallas_call(
        start_kernel,
        out_shape=(
            jax.ShapeDtypeStruct((side, side, 4, tokens // 4, cols), BF16),
            jax.ShapeDtypeStruct((rank // tok, cols), BF16),
        ),
        in_specs=[vmem(), vmem()],
        out_specs=(vmem(), vmem()),
        scratch_shapes=[
            pltpu.VMEM((tok, rank // tok, 128), BF16),
            pltpu.VMEM((tok, rank // tok, 128), BF16),
            *ring_semaphores(),
            *line_semaphores(tok),
        ],
        compiler_params=params(0),
    )(acts, init)


def step_kernel(
    links_ref, same_ref, acts_ref, basis_ref,
    image_ref, gram_ref,
    proj_out, proj_in, mixed_out, mixed_in, wide, part_out, part_in, sum_out, sum_in,
    ps, pr, ms, mr, is_, ir, gs, gr, ss, sr, hs, hr,
):
    here = Place()
    line = here.line
    tokens, cols = acts_ref.shape
    rank = basis_ref.shape[0]
    chunk = tokens // line
    greet(line_devices(here) + ring_devices(here))

    per = 2 if line % 2 == 0 else 1
    groups = line // per

    def project(d, carry):
        u = (here.k // per + 1 + d) % groups
        at = pl.multiple_of(u * (per * chunk), per * chunk)
        proj = lax.dot_general(
            basis_ref[...], acts_ref[pl.ds(at, per * chunk), :],
            (((1,), (1,)), ((), ())), preferred_element_type=F32,
        ).astype(BF16)
        for v in range(per):
            c = u * per + v
            proj_out[c] = proj[:, v * chunk : (v + 1) * chunk]

            @pl.when(c != here.k)
            def _():
                line_copy(here, proj_out, proj_in, ps, pr, c).start()

        return carry

    lax.fori_loop(0, groups, project, 0)
    proj_in[here.k] = proj_out[here.k]
    line_received(here, proj_out, proj_in, ps, pr)
    for j in range(line):
        wide[j] = proj_in[j].astype(F32)

    def mix(d, carry):
        i = (here.k + 1 + d) % line
        total = links_ref[i, 0] * wide[0]
        for j in range(1, line):
            total += links_ref[i, j] * wide[j]
        mixed_out[i] = total.astype(BF16)

        @pl.when(i != here.k)
        def _():
            line_copy(here, mixed_out, mixed_in, ms, mr, i).start()

        return carry

    lax.fori_loop(0, line, mix, 0)
    mixed_in[here.k] = mixed_out[here.k]
    line_received(here, mixed_out, mixed_in, ms, mr)
    mixed = jnp.concatenate([mixed_in[c] for c in range(line)], axis=1)
    image = jnp.dot(mixed, acts_ref[...], preferred_element_type=F32)
    image = image * (1.0 / tokens) + RIDGE * basis_ref[...].astype(F32)
    image_ref[here.y, here.x] = image.reshape(image_ref.shape[2:])
    plane_gather_start(here, image_ref, is_, ir)
    plane_gather_finish(here, image_ref, is_, ir)

    whole = image_ref[...].reshape(rank * here.tok, cols)
    gram = lax.dot_general(
        image, whole, (((1,), (1,)), ((), ())), precision=HIGHEST, preferred_element_type=F32
    )
    high, across = part_out.shape[1:]
    down = rank // high
    over = gram.shape[1] // across
    for a in range(down):
        for b in range(over):
            part_out[a * over + b] = gram[a * high : (a + 1) * high, b * across : (b + 1) * across]

    def send_part(d, carry):
        line_copy(here, part_out, part_in, gs, gr, (here.k + d) % line).start()
        return carry

    lax.fori_loop(1, line, send_part, 0)
    part_in[here.k] = part_out[here.k]
    line_received(here, part_out, part_in, gs, gr)

    def add(d, carry):
        i = (here.k + 1 + d) % line
        total = same_ref[i, 0] * part_in[0]
        for j in range(1, line):
            total += same_ref[i, j] * part_in[j]
        sum_out[i] = total

        @pl.when(i != here.k)
        def _():
            line_copy(here, sum_out, sum_in, ss, sr, i).start()

        return carry

    lax.fori_loop(0, line, add, 0)
    sum_in[here.k] = sum_out[here.k]
    line_received(here, sum_out, sum_in, ss, sr)
    rows = [
        jnp.concatenate([sum_in[a * over + b] for b in range(over)], axis=1) for a in range(down)
    ]
    gram_ref[here.y, here.x] = jnp.concatenate(rows, axis=0).reshape(gram_ref.shape[2:])
    plane_gather_start(here, gram_ref, hs, hr)
    plane_gather_finish(here, gram_ref, hs, hr)

    line_sent(here, proj_out, proj_in, ps, pr)
    line_sent(here, mixed_out, mixed_in, ms, mr)
    line_sent(here, part_out, part_in, gs, gr)
    line_sent(here, sum_out, sum_in, ss, sr)
    plane_gather_sent(here, image_ref, is_, ir)
    plane_gather_sent(here, gram_ref, hs, hr)


def step(links, same, acts, basis):
    tok = lax.axis_size("tok")
    line = lax.axis_size("gr") * lax.axis_size("gc")
    side = math.isqrt(tok)
    tokens, cols = acts.shape
    rank = basis.shape[0]
    chunk = tokens // line
    high = max(8, rank // line)
    across = rank * rank * tok // line // high
    pieces = (line, rank, chunk)
    tiles = (line, high, across)
    image, gram = pl.pallas_call(
        step_kernel,
        out_shape=(
            jax.ShapeDtypeStruct((side, side, 4, rank // 4, cols), F32),
            jax.ShapeDtypeStruct((side, side, 4, rank // 4, rank * tok), F32),
        ),
        in_specs=[smem(), smem(), vmem(), vmem()],
        out_specs=(vmem(), vmem()),
        scratch_shapes=[
            pltpu.VMEM(pieces, BF16),
            pltpu.VMEM(pieces, BF16),
            pltpu.VMEM(pieces, BF16),
            pltpu.VMEM(pieces, BF16),
            pltpu.VMEM(pieces, F32),
            pltpu.VMEM(tiles, F32),
            pltpu.VMEM(tiles, F32),
            pltpu.VMEM(tiles, F32),
            pltpu.VMEM(tiles, F32),
            *line_semaphores(line),
            *line_semaphores(line),
            *ring_semaphores(),
            *line_semaphores(line),
            *line_semaphores(line),
            *ring_semaphores(),
        ],
        compiler_params=params(1),
    )(links, same, acts, basis)
    return image.reshape(rank * tok, cols), gram.reshape(rank * tok, rank * tok)


def leaf_inverse(tiles):
    shape = tiles[0].shape
    lane = lax.broadcasted_iota(jnp.int32, shape, 1)
    sub = lax.broadcasted_iota(jnp.int32, shape, 0)
    tiles = list(tiles)
    count = len(tiles)
    for s in range(count):
        c0 = 8 * s
        here = tiles[s]
        cols = [jnp.broadcast_to(here[:, c0 + j : c0 + j + 1], shape) for j in range(8)]
        diag = (lane >= c0) & (lane < c0 + 8)
        first = jnp.where(diag, jnp.where(lane - c0 == sub, 1.0, 0.0), here)
        full, low = first, first
        pivots = jnp.ones(shape, F32)
        for j in range(8):
            pivot = jnp.broadcast_to(cols[j][j : j + 1, :], shape)
            ratio = cols[j] * (1.0 / pivot)
            others = jnp.where(sub == j, 0.0, ratio)
            below = jnp.where(sub > j, ratio, 0.0)
            for k in range(j + 1, 8):
                cols[k] = cols[k] - others * jnp.broadcast_to(cols[k][j : j + 1, :], shape)
            full = full - others * jnp.broadcast_to(full[j : j + 1, :], shape)
            low = low - below * jnp.broadcast_to(low[j : j + 1, :], shape)
            pivots = jnp.where(sub == j, pivot, pivots)
        solved = full / pivots
        tiles[s] = jnp.where(lane < c0 + 8, low * lax.rsqrt(pivots), 0.0)
        rows = [jnp.broadcast_to(solved[k : k + 1, :], shape) for k in range(8)]
        for t in range(s + 1, count):
            old = tiles[t]
            new = jnp.where(diag, 0.0, old)
            for k in range(8):
                new = new - jnp.broadcast_to(old[:, c0 + k : c0 + k + 1], shape) * rows[k]
            tiles[t] = new
    return jnp.concatenate(tiles, axis=0)


def dot(a, b):
    return jnp.dot(a, b, precision=HIGHEST, preferred_element_type=F32)


def factor_inverse(m_ref, w_ref):
    size = m_ref.shape[0]
    for r0 in range(0, size, LEAF):
        r1 = r0 + LEAF
        inv = leaf_inverse([m_ref[r0 + 8 * t : r0 + 8 * t + 8, r0:r1] for t in range(LEAF // 8)])
        w_ref[r0:r1, r0:r1] = inv
        if r0:
            left = dot(inv, m_ref[r0:r1, :r0])
            w_ref[r0:r1, :r0] = left
        if r1 < size:
            w_ref[r0:r1, r1:] = jnp.zeros((LEAF, size - r1), F32)
            right = dot(inv, m_ref[r0:r1, r1:])
            back = right.T
            m_ref[r1:, r1:] = m_ref[r1:, r1:] - dot(back, right)
            m_ref[r1:, r0:r1] = -dot(back, inv)
            if r0:
                m_ref[r1:, :r0] = m_ref[r1:, :r0] - dot(back, left)


def slice_kernel(scale, gram_ref, image_ref, basis_ref, m_ref, w_ref):
    rank = basis_ref.shape[0]
    m_ref[...] = gram_ref[...] * scale
    factor_inverse(m_ref, w_ref)
    at = pl.multiple_of(lax.axis_index("tok") * rank, rank)
    basis_ref[...] = dot(w_ref[pl.ds(at, rank), :], image_ref[...]).astype(BF16)


def next_basis(gram, image, group_cols):
    rank = gram.shape[0]
    return pl.pallas_call(
        functools.partial(slice_kernel, 1.0 / group_cols),
        out_shape=jax.ShapeDtypeStruct((rank // lax.axis_size("tok"), image.shape[1]), BF16),
        in_specs=[vmem(), vmem()],
        out_specs=vmem(),
        scratch_shapes=[pltpu.VMEM((rank, rank), F32), pltpu.VMEM((rank, rank), F32)],
        compiler_params=params(),
    )(gram, image)


def last_kernel(scale, gram_ref, image_ref, acts_ref, bases_ref, codes_ref, m_ref, w_ref, turned):
    rows = bases_ref.shape[0]
    cols = image_ref.shape[1]
    m_ref[...] = gram_ref[...] * scale
    factor_inverse(m_ref, w_ref)
    basis = dot(w_ref[...], image_ref[...])
    codes_ref[...] = lax.dot_general(
        acts_ref[...], basis.astype(BF16), (((1,), (1,)), ((), ())), preferred_element_type=F32
    )
    wide = turned.shape[0]
    per = wide // rows
    p = lax.axis_index("tok")
    at = pl.multiple_of(p // per * wide, wide)
    turned[...] = dot(w_ref[...], image_ref[:, pl.ds(at, wide)]).T
    bases_ref[...] = turned[pl.ds(pl.multiple_of(p % per * rows, rows), rows), :]


def last(gram, image, acts, rows, group_cols):
    rank = gram.shape[0]
    return pl.pallas_call(
        functools.partial(last_kernel, 1.0 / group_cols),
        out_shape=(
            jax.ShapeDtypeStruct((rows, rank), F32),
            jax.ShapeDtypeStruct((acts.shape[0], rank), F32),
        ),
        in_specs=[vmem(), vmem(), vmem()],
        out_specs=(vmem(), vmem()),
        scratch_shapes=[
            pltpu.VMEM((rank, rank), F32),
            pltpu.VMEM((rank, rank), F32),
            pltpu.VMEM((max(rows, 128), rank), F32),
        ],
        compiler_params=params(),
    )(gram, image, acts)


def latent_kernel(scale, groups, select_ref, codes_ref, out_ref, in_tiles, send, recv):
    here = Place()
    rank = codes_ref.shape[2]
    greet(line_devices(here))

    def go(d, carry):
        line_copy(here, codes_ref, in_tiles, send, recv, (here.k + d) % here.line).start()
        return carry

    lax.fori_loop(1, here.line, go, 0)
    in_tiles[here.k] = codes_ref[here.k]
    line_received(here, codes_ref, in_tiles, send, recv)
    for g in range(groups):
        total = select_ref[g, 0] * in_tiles[0]
        for j in range(1, here.line):
            total += select_ref[g, j] * in_tiles[j]
        out_ref[:, g * rank : (g + 1) * rank] = (total * scale).astype(BF16)
    line_sent(here, codes_ref, in_tiles, send, recv)


def latent_of(select, codes, group_cols):
    groups, line = select.shape
    tokens, rank = codes.shape
    tiles = (line, tokens // line, rank)
    return pl.pallas_call(
        functools.partial(latent_kernel, 1.0 / math.sqrt(group_cols), groups),
        out_shape=jax.ShapeDtypeStruct((tokens // line, groups * rank), BF16),
        in_specs=[smem(), vmem()],
        out_specs=vmem(),
        scratch_shapes=[pltpu.VMEM(tiles, F32), *line_semaphores(line)],
        compiler_params=params(2),
    )(select, codes.reshape(tiles))


def per_device(acts, init_basis, kept, member):
    tok = lax.axis_size("tok")
    groups = kept.shape[0] // GBLK
    rows = init_basis.shape[1]
    group_cols = GBLK * rows * tok
    equal = member[:, None] == member[None, :]
    same = equal.astype(F32)
    links = jnp.where(equal, kept, 0).astype(F32)
    select = (member[None, :] == jnp.arange(groups, dtype=jnp.int32)[:, None]).astype(F32)
    full, basis = start(acts, init_basis[0])
    full = full.reshape(acts.shape[0] * tok, acts.shape[1])
    for turn in range(ITERS):
        image, gram = step(links, same, full, basis)
        if turn < ITERS - 1:
            basis = next_basis(gram, image, group_cols)
    bases, codes = last(gram, image, acts, rows, group_cols)
    return bases[None], latent_of(select, codes, group_cols)


def solution(mesh):
    placed = (P("tok", ("gr", "gc")), P(("gr", "gc"), "tok", None), P(), P())
    return jax.shard_map(
        per_device,
        mesh=mesh,
        in_specs=placed,
        out_specs=(P(("gr", "gc"), "tok", None), P(("tok", "gr", "gc"), None)),
        check_vma=False,
    )
```

```python
import functools
import math

import jax
import jax.numpy as jnp
from jax import lax
from jax.experimental import pallas as pl
from jax.experimental.pallas import tpu as pltpu
from jax.sharding import PartitionSpec as P

GBLK = 8
ITERS = 2
RIDGE = 2.0
LEAF = 128
MESH = pl.DeviceIdType.MESH
HIGHEST = lax.Precision.HIGHEST
VMEM_LIMIT = 48 * 2**20
F32 = jnp.float32
BF16 = jnp.bfloat16


def vmem():
    return pl.BlockSpec(memory_space=pltpu.VMEM)


def smem():
    return pl.BlockSpec(memory_space=pltpu.SMEM)


def params(collective_id=None):
    if collective_id is None:
        return pltpu.CompilerParams(vmem_limit_bytes=VMEM_LIMIT)
    return pltpu.CompilerParams(
        vmem_limit_bytes=VMEM_LIMIT, collective_id=collective_id, has_side_effects=True
    )


class Place:
    def __init__(self):
        self.tok = lax.axis_size("tok")
        self.gc = lax.axis_size("gc")
        self.line = lax.axis_size("gr") * self.gc
        self.side = math.isqrt(self.tok)
        self.p = lax.axis_index("tok")
        self.gr_at = lax.axis_index("gr")
        self.gc_at = lax.axis_index("gc")
        self.k = self.gr_at * self.gc + self.gc_at
        self.y = self.p // self.side
        self.x = self.p % self.side

    def in_plane(self, p):
        return (p, self.gr_at, self.gc_at)

    def in_line(self, k):
        return (self.p, k // self.gc, k % self.gc)

    def at_axis(self, axis, at):
        if axis == "x":
            return self.in_plane(self.y * self.side + at)
        return self.in_plane(at * self.side + self.x)


def greet(devices):
    barrier = pltpu.get_barrier_semaphore()
    for device in devices:
        pl.semaphore_signal(barrier, inc=1, device_id=device, device_id_type=MESH)
    if devices:
        pl.semaphore_wait(barrier, len(devices))


def line_devices(here):
    return [here.in_line((here.k + d) % here.line) for d in range(1, here.line)]


def plane_devices(here):
    return [here.in_plane((here.p + d) % here.tok) for d in range(1, here.tok)]


def ring_devices(here):
    if here.tok == 1:
        return []
    side = here.side
    return [
        here.at_axis(axis, (at + d) % side)
        for axis, at in (("x", here.x), ("y", here.y))
        for d in (1, side - 1)
    ]


def rcopy(src, dst, send, recv, device):
    return pltpu.make_async_remote_copy(
        src_ref=src, dst_ref=dst, send_sem=send, recv_sem=recv, device_id=device, device_id_type=MESH
    )


class Ring:
    def __init__(self, here, axis, piece, send, recv):
        at = here.x if axis == "x" else here.y
        side = here.side
        self.me, self.right, self.left = at, (at + 1) % side, (at + side - 1) % side
        self.opp = (at + 2) % side
        self.to_right = here.at_axis(axis, self.right)
        self.to_left = here.at_axis(axis, self.left)
        self.piece, self.send, self.recv = piece, send, recv

    def copy(self, slot, owner, part, device):
        ref = self.piece(owner, part)
        return rcopy(ref, ref, self.send.at[slot], self.recv.at[slot], device)

    def start(self):
        self.copy(0, self.me, 0, self.to_right).start()
        self.copy(1, self.me, 1, self.to_left).start()
        self.copy(2, self.me, 1, self.to_right).start()
        self.copy(3, self.me, 0, self.to_left).start()

    def forward(self):
        self.copy(0, self.left, 0, self.to_right).wait_recv()
        self.copy(4, self.left, 0, self.to_right).start()
        self.copy(1, self.right, 1, self.to_left).wait_recv()
        self.copy(5, self.right, 1, self.to_left).start()

    def finish(self):
        self.copy(2, self.left, 1, self.to_right).wait_recv()
        self.copy(3, self.right, 0, self.to_left).wait_recv()
        self.copy(4, self.opp, 0, self.to_right).wait_recv()
        self.copy(5, self.opp, 1, self.to_left).wait_recv()

    def sent(self):
        self.copy(0, self.me, 0, self.to_right).wait_send()
        self.copy(1, self.me, 1, self.to_left).wait_send()
        self.copy(2, self.me, 1, self.to_right).wait_send()
        self.copy(3, self.me, 0, self.to_left).wait_send()
        self.copy(4, self.left, 0, self.to_right).wait_send()
        self.copy(5, self.right, 1, self.to_left).wait_send()


def plane_rings(here, buf, send, recv):
    y, x = here.y, here.x
    return (
        Ring(here, "x", lambda at, part: buf.at[y, at, part], send.at[0], recv.at[0]),
        Ring(here, "y", lambda at, part: buf.at[at, x, 2 + part], send.at[1], recv.at[1]),
        Ring(here, "y", lambda at, part: buf.at[at, :, part], send.at[2], recv.at[2]),
        Ring(here, "x", lambda at, part: buf.at[:, at, 2 + part], send.at[3], recv.at[3]),
    )


def plane_gather_start(here, buf, send, recv):
    if here.tok > 1:
        one_a, one_b, _, _ = plane_rings(here, buf, send, recv)
        one_a.start()
        one_b.start()


def plane_gather_finish(here, buf, send, recv):
    if here.tok > 1:
        one_a, one_b, two_a, two_b = plane_rings(here, buf, send, recv)
        one_a.forward()
        one_b.forward()
        one_a.finish()
        two_a.start()
        one_b.finish()
        two_b.start()
        two_a.forward()
        two_b.forward()
        two_a.finish()
        two_b.finish()


def plane_gather_sent(here, buf, send, recv):
    if here.tok > 1:
        for ring in plane_rings(here, buf, send, recv):
            ring.sent()


def group_copy(src, dst, sems, which, device):
    return rcopy(src, dst, sems.at[0, which], sems.at[1, which], device)


class Exchange:
    def __init__(self, at, count, device, src, dst, sems, which):
        self.at, self.count, self.device = at, count, device
        self.src, self.dst, self.sems, self.which = src, dst, sems, which

    def send(self, to):
        group_copy(
            self.src.at[to], self.dst.at[self.at], self.sems, self.which, self.device(to)
        ).start()

    def send_all(self):
        def body(d, carry):
            self.send(lax.rem(self.at + d, self.count))
            return carry

        lax.fori_loop(1, self.count, body, 0)

    def keep(self):
        self.dst[self.at] = self.src[self.at]

    def all_of(self, ref, number):
        other = lax.rem(self.at + 1, self.count)
        return group_copy(
            ref.at[pl.ds(0, number)], ref.at[pl.ds(0, number)], self.sems, self.which, self.device(other)
        )

    def received(self, number=None):
        number = self.count - 1 if number is None else number
        if number:
            self.all_of(self.dst, number).wait_recv()

    def sent(self, number=None):
        number = self.count - 1 if number is None else number
        if number:
            self.all_of(self.src, number).wait_send()


def leaf_inverse(block):
    count, high, wide = block.shape
    shape = (high, wide)
    lane = lax.broadcasted_iota(jnp.int32, shape, 1)
    sub = lax.broadcasted_iota(jnp.int32, shape, 0)

    def down(v, r):
        return jnp.broadcast_to(v[r : r + 1, :], shape)

    done = []
    rest = block
    for s in range(count):
        c0 = 8 * s
        here = rest[0]
        cols = [jnp.broadcast_to(here[:, c0 + j : c0 + j + 1], shape) for j in range(8)]
        diag = (lane >= c0) & (lane < c0 + 8)
        first = jnp.where(diag, jnp.where(lane - c0 == sub, 1.0, 0.0), here)
        full, low = first, first
        pivots = jnp.ones(shape, F32)
        for j in range(8):
            pivot = down(cols[j], j)
            inverse = 1.0 / pivot
            others = jnp.where(sub == j, 0.0, cols[j])
            below = jnp.where(sub > j, cols[j], 0.0)
            for k in range(j + 1, 8):
                cols[k] = cols[k] - (others * down(cols[k], j)) * inverse
            full = full - (others * down(full, j)) * inverse
            low = low - (below * down(low, j)) * inverse
            pivots = jnp.where(sub == j, pivot, pivots)
        solved = full / pivots
        done.append(jnp.where(lane < c0 + 8, low * lax.rsqrt(pivots), 0.0))
        if s + 1 < count:
            old = rest[1:]
            terms = [
                jnp.broadcast_to(old[:, :, c0 + k : c0 + k + 1], old.shape) * down(solved, k)[None]
                for k in range(8)
            ]
            while len(terms) > 1:
                terms = [terms[i] + terms[i + 1] for i in range(0, len(terms), 2)]
            rest = jnp.where(diag[None], 0.0, old) - terms[0]
    return jnp.stack(done)


def dot(a, b):
    return jnp.dot(a, b, precision=HIGHEST, preferred_element_type=F32)


def dot_t(a, b):
    return lax.dot_general(
        a, b, (((1,), (1,)), ((), ())), precision=HIGHEST, preferred_element_type=F32
    )


def factor_inverse(m_ref, w_ref):
    size = m_ref.shape[0]
    w_ref[...] = jnp.zeros(w_ref.shape, F32)

    def turn(step, carry):
        at = pl.ds(pl.multiple_of(step * LEAF, LEAF), LEAF)
        w_ref[at, at] = leaf_inverse(m_ref[at, at].reshape(LEAF // 8, 8, LEAF)).reshape(LEAF, LEAF)
        for b in range(size // LEAF):
            r0, r1 = b * LEAF, (b + 1) * LEAF

            @pl.when(step == b)
            def _():
                inv = w_ref[r0:r1, r0:r1]
                if r0:
                    left = dot(inv, m_ref[r0:r1, :r0])
                    w_ref[r0:r1, :r0] = left
                if r1 < size:
                    back = dot_t(m_ref[r1:, r0:r1], inv)
                    for c in range(r1, size, LEAF):
                        m_ref[c:, c : c + LEAF] -= dot_t(
                            back[c - r1 :], back[c - r1 : c - r1 + LEAF]
                        )
                    m_ref[r1:, r0:r1] = -dot(back, inv)
                    if r0:
                        m_ref[r1:, :r0] -= dot(back, left)

        return carry

    lax.fori_loop(0, size // LEAF, turn, 0)


def tokens_at(full_ref, u, size):
    side, _, _, quarter, cols = full_ref.shape
    shard = 4 * quarter
    if size >= shard:
        m = size // shard
        if m <= side:
            part = full_ref[u * m // side, pl.ds(u * m % side, m)]
        else:
            part = full_ref[pl.ds(u * (m // side), m // side)]
    else:
        per = quarter // size
        part = full_ref[0, 0, u // per, pl.ds(u % per * size, size)]
    return part.reshape(size, cols)


def eight_rows(image_ref, row):
    side, _, _, quarter, _ = image_ref.shape
    shard, within = row // (4 * quarter), row % (4 * quarter)
    place = (shard // side, shard % side, within // quarter)
    if quarter == 8:
        return image_ref[place]
    return image_ref[(*place, pl.ds(pl.multiple_of(within % quarter, 8), 8))]


def masks(member_ref, line, groups):
    rows = lax.broadcasted_iota(jnp.int32, (line, line), 0)
    across = lax.broadcasted_iota(jnp.int32, (line, line), 1)
    row = jnp.broadcast_to(member_ref[...].astype(F32), (line, line))
    column = jnp.sum(jnp.where(rows == across, row, 0.0), axis=1, keepdims=True)
    wide = jnp.broadcast_to(column, (line, 128))
    spread = jnp.broadcast_to(wide[:, None, :], (line, 8, 128))
    return (row == column), [jnp.where(spread == g, 1.0, 0.0) for g in range(groups)]


def mixing(linked, rank):
    line = linked.shape[0]
    size = line * rank
    owner = lax.broadcasted_iota(jnp.int32, (size, line), 0) // rank
    block = lax.broadcasted_iota(jnp.int32, (size, line), 1)
    spread = jnp.where(owner == block, 1.0, 0.0).astype(BF16)
    tall = jnp.dot(spread, linked.astype(BF16), preferred_element_type=F32).astype(BF16)
    big = lax.dot_general(tall, spread, (((1,), (1,)), ((), ())), preferred_element_type=F32)
    rows = lax.broadcasted_iota(jnp.int32, (size, size), 0)
    across = lax.broadcasted_iota(jnp.int32, (size, size), 1)
    return jnp.where(rows % rank == across % rank, big, 0.0).astype(BF16)


def whole_kernel(
    groups, group_cols,
    acts_ref, init_ref, kept_ref, member_ref,
    bases_ref, latent_ref,
    full_ref, image_all, gram_ref, basis_ref, init_v, init_out, init_in,
    proj_out, proj_in, mixed_out, mixed_in, part_out, part_in, sum_out, sum_in,
    m_ref, w_ref, mix_ref, codes_out, codes_in, turned,
    local_sems, sems, xs, xr, is_, ir,
):
    here = Place()
    line, tok = here.line, here.tok
    rows = init_v.shape[0]
    rank, cols = basis_ref.shape
    total_rank = rank * tok
    tokens = line * proj_out.shape[2]
    reducers, per_tile = part_out.shape[:2]

    acts_copy = pltpu.make_async_copy(acts_ref, turned_acts(full_ref, here), local_sems.at[0])
    init_copy = pltpu.make_async_copy(init_ref, init_v, local_sems.at[1])
    acts_copy.start()
    init_copy.start()
    greet_start(line_devices(here) + plane_devices(here))
    init_copy.wait()
    turned_init = init_v[...].T
    if tok > 1:
        wide = jnp.concatenate([turned_init, jnp.zeros((total_rank, 128 - rows), F32)], axis=1)
        init_out[...] = wide.astype(BF16).reshape(init_out.shape)
    else:
        basis_ref[...] = turned_init.astype(BF16)
    acts_copy.wait()
    greet_finish(line + tok - 2)

    plane_gather_start(here, full_ref, xs, xr)
    spread = Exchange(here.p, tok, here.in_plane, init_out, init_in, sems, 0)
    if tok > 1:
        spread.send_all()
        spread.keep()
    same, member_masks = masks(member_ref, line, groups)
    linked = jnp.where(same, kept_ref[...].astype(F32), 0.0)
    mix_ref[...] = mixing(linked, rank)
    plane_gather_finish(here, full_ref, xs, xr)
    if tok > 1:
        spread.received()
        spread.sent()
        per = 128 // rows
        for c in range(tok // per):
            total = init_in[c * per].astype(F32)
            for d in range(1, per):
                total += pltpu.roll(init_in[c * per + d].astype(F32), d * rows, 1)
            basis_ref[:, c * 128 : c * 128 + 128] = total.astype(BF16)
    plane_gather_sent(here, full_ref, xs, xr)

    chunk = tokens // line
    per_step = 2 if line % 2 == 0 else 1
    steps = line // per_step
    proj_x = Exchange(here.k, line, here.in_line, proj_out, proj_in, sems, 1)
    mixed_x = Exchange(here.k, line, here.in_line, mixed_out, mixed_in, sems, 2)
    part_x = Exchange(here.k, line, here.in_line, part_out, part_in, sems, 3)
    sum_x = Exchange(here.k, line, here.in_line, sum_out, sum_in, sems, 4)
    gram_x = Exchange(here.p, tok, here.in_plane, gram_ref, gram_ref, sems, 5)
    codes_x = Exchange(here.k, line, here.in_line, codes_out, codes_in, sems, 6)
    reducing = here.k < reducers

    def iteration(turn, carry):
        image_ref = image_all.at[turn]

        def project(d, carry):
            u = (here.k // per_step + 1 + d) % steps
            proj = lax.dot_general(
                basis_ref[...], tokens_at(full_ref, u, per_step * chunk),
                (((1,), (1,)), ((), ())), preferred_element_type=F32,
            ).astype(BF16)
            for v in range(per_step):
                c = u * per_step + v
                proj_out[c] = proj[:, v * chunk : (v + 1) * chunk]

                @pl.when(c != here.k)
                def _():
                    proj_x.send(c)

            return carry

        lax.fori_loop(0, steps, project, 0)
        proj_x.keep()
        proj_x.received()
        stacked = proj_in[...].reshape(line * rank, chunk)
        mixed_out[...] = (
            jnp.dot(mix_ref[...], stacked, preferred_element_type=F32)
            .astype(BF16)
            .reshape(mixed_out.shape)
        )
        mixed_x.send_all()
        mixed_x.keep()
        mixed_x.received()
        mixed = jnp.concatenate([mixed_in[c] for c in range(line)], axis=1)
        acts = full_ref[...].reshape(tokens, cols)
        image = jnp.dot(mixed, acts, preferred_element_type=F32)
        image = image * (1.0 / tokens) + RIDGE * basis_ref[...].astype(F32)
        image_ref[here.y, here.x] = image.reshape(image_ref.shape[2:])
        plane_gather_start(here, image_ref, is_, ir)
        plane_gather_finish(here, image_ref, is_, ir)

        whole = image_ref[...].reshape(total_rank, cols)
        tiles = []
        for c in range(0, total_rank, LEAF):
            high = (total_rank - c) // tok
            mine = [eight_rows(image_ref, c + here.p * high + r) for r in range(0, high, 8)]
            tile = dot_t(jnp.concatenate(mine, axis=0), whole[c : c + LEAF])
            tiles.append(tile.reshape(high // 8, 8, LEAF))
        part_out[...] = jnp.concatenate(tiles, axis=0).reshape(part_out.shape)

        def send_part(d, carry):
            to = lax.rem(here.k + d, line)

            @pl.when(to < reducers)
            def _():
                part_x.send(to)

            return carry

        lax.fori_loop(1, line, send_part, 0)

        @pl.when(reducing)
        def _():
            part_x.keep()
            part_x.received()
            totals = [
                jnp.sum(part_in[...] * mask[:, None], axis=0) for mask in member_masks
            ]
            for i in range(line):
                mine = member_masks[0][i][None] * totals[0]
                for g in range(1, groups):
                    mine += member_masks[g][i][None] * totals[g]
                sum_out[i] = mine
            sum_x.send_all()
            sum_x.keep()
            sum_x.received(reducers - 1)

        @pl.when(jnp.logical_not(reducing))
        def _():
            sum_x.received(reducers)

        gram_ref[here.p] = sum_in[...].reshape(gram_ref.shape[1:])
        if tok > 1:
            def send_gram(d, carry):
                to = lax.rem(here.p + d, tok)
                mine = gram_ref.at[here.p]
                group_copy(mine, mine, sems, 5, here.in_plane(to)).start()
                return carry

            lax.fori_loop(1, tok, send_gram, 0)
            gram_x.received()
        first = 0
        for c in range(0, total_rank, LEAF):
            count = (total_rank - c) // tok // 8
            panel = gram_ref[:, first : first + count].reshape(total_rank - c, LEAF)
            m_ref[c:, c : c + LEAF] = panel * (1.0 / group_cols)
            first += count

        proj_x.sent()
        mixed_x.sent()
        plane_gather_sent(here, image_ref, is_, ir)

        @pl.when(reducing)
        def _():
            part_x.sent(reducers - 1)
            sum_x.sent()

        @pl.when(jnp.logical_not(reducing))
        def _():
            part_x.sent(reducers)

        if tok > 1:
            gram_x.sent()
        factor_inverse(m_ref, w_ref)

        @pl.when(turn < ITERS - 1)
        def _():
            at = pl.multiple_of(here.p * rank, rank)
            image = image_ref[...].reshape(total_rank, cols)
            basis_ref[...] = dot(w_ref[pl.ds(at, rank), :], image).astype(BF16)

        return carry

    lax.fori_loop(0, ITERS, iteration, 0)

    image = image_all[ITERS - 1].reshape(total_rank, cols)
    basis = dot(w_ref[...], image).astype(BF16)
    own = full_ref[here.y, here.x].reshape(tokens // tok, cols)
    codes = lax.dot_general(own, basis, (((1,), (1,)), ((), ())), preferred_element_type=F32)
    codes_out[...] = codes.reshape(codes_out.shape)
    codes_x.send_all()
    codes_x.keep()
    wide = turned.shape[0]
    per = wide // rows
    at = pl.multiple_of(here.p // per * wide, wide)
    part = image_all[ITERS - 1, :, :, :, :, pl.ds(at, wide)].reshape(total_rank, wide)
    turned[...] = dot(w_ref[...], part).T
    bases_ref[...] = turned[pl.ds(pl.multiple_of(here.p % per * rows, rows), rows), :]
    codes_x.received()
    scale = 1.0 / math.sqrt(group_cols)
    for g in range(groups):
        for c in range(0, total_rank, 128):
            total = jnp.sum(codes_in[:, :, c : c + 128] * member_masks[g][:, :1], axis=0)
            latent_ref[:, g * total_rank + c : g * total_rank + c + 128] = (total * scale).astype(BF16)
    codes_x.sent()


def turned_acts(full_ref, here):
    return full_ref.at[here.y, here.x]


def greet_start(devices):
    barrier = pltpu.get_barrier_semaphore()
    for device in devices:
        pl.semaphore_signal(barrier, inc=1, device_id=device, device_id_type=MESH)


def greet_finish(count):
    pl.semaphore_wait(pltpu.get_barrier_semaphore(), count)


def per_device(acts, init_basis, kept, member):
    tok = lax.axis_size("tok")
    line = lax.axis_size("gr") * lax.axis_size("gc")
    side = math.isqrt(tok)
    groups = kept.shape[0] // GBLK
    rows, total_rank = init_basis.shape[1:]
    shard, cols = acts.shape
    tokens = shard * tok
    rank = total_rank // tok
    group_cols = GBLK * rows * tok
    tiles = sum((total_rank - c) // tok // 8 for c in range(0, total_rank, LEAF))
    reducers = max(d for d in range(1, line + 1) if tiles % d == 0)
    per_tile = tiles // reducers
    pieces = (line, rank, tokens // line)
    init_pieces = (tok, rank, 128)
    codes = (line, shard // line, total_rank)
    bases, latent = pl.pallas_call(
        functools.partial(whole_kernel, groups, group_cols),
        out_shape=(
            jax.ShapeDtypeStruct((rows, total_rank), F32),
            jax.ShapeDtypeStruct((shard // line, groups * total_rank), BF16),
        ),
        in_specs=[pl.BlockSpec(memory_space=pl.ANY), pl.BlockSpec(memory_space=pl.ANY), vmem(), vmem()],
        out_specs=(vmem(), vmem()),
        scratch_shapes=[
            pltpu.VMEM((side, side, 4, shard // 4, cols), BF16),
            pltpu.VMEM((ITERS, side, side, 4, rank // 4, cols), F32),
            pltpu.VMEM((tok, tiles, 8, LEAF), F32),
            pltpu.VMEM((rank, cols), BF16),
            pltpu.VMEM((rows, total_rank), F32),
            pltpu.VMEM(init_pieces, BF16),
            pltpu.VMEM(init_pieces, BF16),
            pltpu.VMEM(pieces, BF16),
            pltpu.VMEM(pieces, BF16),
            pltpu.VMEM(pieces, BF16),
            pltpu.VMEM(pieces, BF16),
            pltpu.VMEM((reducers, per_tile, 8, LEAF), F32),
            pltpu.VMEM((line, per_tile, 8, LEAF), F32),
            pltpu.VMEM((line, per_tile, 8, LEAF), F32),
            pltpu.VMEM((reducers, per_tile, 8, LEAF), F32),
            pltpu.VMEM((total_rank, total_rank), F32),
            pltpu.VMEM((total_rank, total_rank), F32),
            pltpu.VMEM((line * rank, line * rank), BF16),
            pltpu.VMEM(codes, F32),
            pltpu.VMEM(codes, F32),
            pltpu.VMEM((max(rows, 128), total_rank), F32),
            pltpu.SemaphoreType.DMA((2,)),
            pltpu.SemaphoreType.DMA((2, 7)),
            pltpu.SemaphoreType.DMA((4, 6)),
            pltpu.SemaphoreType.DMA((4, 6)),
            pltpu.SemaphoreType.DMA((4, 6)),
            pltpu.SemaphoreType.DMA((4, 6)),
        ],
        compiler_params=params(0),
    )(acts.reshape(4, shard // 4, cols), init_basis[0], kept, member.reshape(1, -1))
    return bases[None], latent


def solution(mesh):
    placed = (P("tok", ("gr", "gc")), P(("gr", "gc"), "tok", None), P(), P())
    return jax.shard_map(
        per_device,
        mesh=mesh,
        in_specs=placed,
        out_specs=(P(("gr", "gc"), "tok", None), P(("tok", "gr", "gc"), None)),
        check_vma=False,
    )
```

```python
import functools
import math

import jax
import jax.numpy as jnp
from jax import lax
from jax.experimental import pallas as pl
from jax.experimental.pallas import tpu as pltpu
from jax.sharding import PartitionSpec as P

GBLK = 8
ITERS = 2
RIDGE = 2.0
LEAF = 128
HIGH = 16
MESH = pl.DeviceIdType.MESH
HIGHEST = lax.Precision.HIGHEST
VMEM_LIMIT = 60 * 2**20
F32 = jnp.float32
BF16 = jnp.bfloat16


def vmem():
    return pl.BlockSpec(memory_space=pltpu.VMEM)


def smem():
    return pl.BlockSpec(memory_space=pltpu.SMEM)


def params(collective_id=None):
    if collective_id is None:
        return pltpu.CompilerParams(vmem_limit_bytes=VMEM_LIMIT)
    return pltpu.CompilerParams(
        vmem_limit_bytes=VMEM_LIMIT, collective_id=collective_id, has_side_effects=True
    )


class Place:
    def __init__(self):
        self.tok = lax.axis_size("tok")
        self.gc = lax.axis_size("gc")
        self.line = lax.axis_size("gr") * self.gc
        self.side = math.isqrt(self.tok)
        self.p = lax.axis_index("tok")
        self.gr_at = lax.axis_index("gr")
        self.gc_at = lax.axis_index("gc")
        self.k = self.gr_at * self.gc + self.gc_at
        self.y = self.p // self.side
        self.x = self.p % self.side

    def in_plane(self, p):
        return (p, self.gr_at, self.gc_at)

    def in_line(self, k):
        return (self.p, k // self.gc, k % self.gc)

    def at_axis(self, axis, at):
        if axis == "x":
            return self.in_plane(self.y * self.side + at)
        return self.in_plane(at * self.side + self.x)


def greet(devices):
    barrier = pltpu.get_barrier_semaphore()
    for device in devices:
        pl.semaphore_signal(barrier, inc=1, device_id=device, device_id_type=MESH)
    if devices:
        pl.semaphore_wait(barrier, len(devices))


def line_devices(here):
    return [here.in_line((here.k + d) % here.line) for d in range(1, here.line)]


def plane_devices(here):
    return [here.in_plane((here.p + d) % here.tok) for d in range(1, here.tok)]


def ring_devices(here):
    if here.tok == 1:
        return []
    side = here.side
    return [
        here.at_axis(axis, (at + d) % side)
        for axis, at in (("x", here.x), ("y", here.y))
        for d in (1, side - 1)
    ]


def rcopy(src, dst, send, recv, device):
    return pltpu.make_async_remote_copy(
        src_ref=src, dst_ref=dst, send_sem=send, recv_sem=recv, device_id=device, device_id_type=MESH
    )


class Gather:
    PARTS = ((0, 2), (0, 2), (0, 1), (1, 1))

    def __init__(self, here, buf, send, recv):
        self.here, self.buf, self.send, self.recv = here, buf, send, recv
        self.side = here.side
        self.axes = (("x", "y"), ("y", "x"))
        self.at = ((here.x, here.y), (here.y, here.x))

    def near(self, part, ring, step):
        return lax.rem(self.at[part][ring] + step, self.side)

    def copy(self, part, ring, kind, owner, rel, slot):
        low, number = self.PARTS[kind]
        first, second = (owner, self.at[part][1]) if ring == 0 else (self.near(part, 0, rel), owner)
        y, x = (second, first) if part == 0 else (first, second)
        ref = self.buf.at[y, x, pl.ds(2 * part + low, number)]
        to = self.near(part, ring, 1 if kind in (0, 2) else self.side - 1)
        device = self.here.at_axis(self.axes[part][ring], to)
        return rcopy(ref, ref, self.send.at[ring], self.recv.at[part, slot], device)

    def one(self, part, kind, step):
        return self.copy(part, 0, kind, self.near(part, 0, step), 0, kind)

    def two(self, part, rel, kind, step):
        return self.copy(part, 1, kind, self.near(part, 1, step), rel, 4 + 4 * rel + kind)

    def start(self):
        if self.here.tok == 1:
            return
        for part in (0, 1):
            self.one(part, 0, 0).start()
            self.one(part, 1, 0).start()
        for part in (0, 1):
            self.share(part, 0)

    def share(self, part, rel):
        self.two(part, rel, 0, 0).start()
        self.two(part, rel, 1, 0).start()

    def pass_on(self, part, rel):
        self.two(part, rel, 0, 3).wait_recv()
        self.two(part, rel, 2, 3).start()
        self.two(part, rel, 1, 1).wait_recv()
        self.two(part, rel, 3, 1).start()

    def finish(self):
        if self.here.tok == 1:
            return
        for part in (0, 1):
            self.one(part, 0, 3).wait_recv()
            self.one(part, 2, 3).start()
            self.share(part, 3)
        for part in (0, 1):
            self.one(part, 1, 1).wait_recv()
            self.one(part, 3, 1).start()
            self.share(part, 1)
        for part in (0, 1):
            self.pass_on(part, 0)
        for part in (0, 1):
            self.one(part, 2, 2).wait_recv()
            self.one(part, 3, 2).wait_recv()
            self.share(part, 2)
        for rel in (3, 1, 2):
            for part in (0, 1):
                self.pass_on(part, rel)
        for rel in (0, 3, 1, 2):
            for part in (0, 1):
                self.two(part, rel, 2, 2).wait_recv()
                self.two(part, rel, 3, 2).wait_recv()

    def sent(self):
        if self.here.tok == 1:
            return
        device = self.here.at_axis("x", self.near(0, 0, 1))
        for ring, ref in ((0, self.buf.at[0, pl.ds(0, 3)]), (1, self.buf.at[pl.ds(0, 3)])):
            rcopy(ref, ref, self.send.at[ring], self.recv.at[0, 0], device).wait_send()


def group_copy(src, dst, sems, which, device):
    return rcopy(src, dst, sems.at[0, which], sems.at[1, which], device)


class Exchange:
    def __init__(self, at, count, device, src, dst, sems, which):
        self.at, self.count, self.device = at, count, device
        self.src, self.dst, self.sems, self.which = src, dst, sems, which

    def send(self, to):
        group_copy(
            self.src.at[to], self.dst.at[self.at], self.sems, self.which, self.device(to)
        ).start()

    def send_all(self):
        def body(d, carry):
            self.send(lax.rem(self.at + d, self.count))
            return carry

        lax.fori_loop(1, self.count, body, 0)

    def keep(self):
        self.dst[self.at] = self.src[self.at]

    def all_of(self, ref, number):
        other = lax.rem(self.at + 1, self.count)
        return group_copy(
            ref.at[pl.ds(0, number)], ref.at[pl.ds(0, number)], self.sems, self.which, self.device(other)
        )

    def received(self, number=None):
        number = self.count - 1 if number is None else number
        if number:
            self.all_of(self.dst, number).wait_recv()

    def sent(self, number=None):
        number = self.count - 1 if number is None else number
        if number:
            self.all_of(self.src, number).wait_send()


def leaf_inverse(block):
    count = LEAF // HIGH
    shape = (HIGH, LEAF)
    lane = lax.broadcasted_iota(jnp.int32, shape, 1)
    sub = lax.broadcasted_iota(jnp.int32, shape, 0)

    def down(v, r):
        return jnp.broadcast_to(v[r : r + 1, :], shape)

    done = []
    rest = block.reshape(count, HIGH, LEAF)
    for s in range(count):
        c0 = HIGH * s
        here = rest[0]
        cols = [jnp.broadcast_to(here[:, c0 + j : c0 + j + 1], shape) for j in range(HIGH)]
        diag = (lane >= c0) & (lane < c0 + HIGH)
        first = jnp.where(diag, jnp.where(lane - c0 == sub, 1.0, 0.0), here)
        full, low = first, first
        pivots = jnp.ones(shape, F32)
        for j in range(HIGH):
            pivot = down(cols[j], j)
            inverse = 1.0 / pivot
            others = jnp.where(sub == j, 0.0, cols[j])
            below = jnp.where(sub > j, cols[j], 0.0)
            for k in range(j + 1, HIGH):
                cols[k] = cols[k] - (others * down(cols[k], j)) * inverse
            full = full - (others * down(full, j)) * inverse
            low = low - (below * down(low, j)) * inverse
            pivots = jnp.where(sub == j, pivot, pivots)
        solved = full / pivots
        done.append(jnp.where(lane < c0 + HIGH, low * lax.rsqrt(pivots), 0.0))
        if s + 1 < count:
            old = rest[1:]
            terms = [
                jnp.broadcast_to(old[:, :, c0 + k : c0 + k + 1], old.shape) * down(solved, k)[None]
                for k in range(HIGH)
            ]
            while len(terms) > 1:
                terms = [terms[i] + terms[i + 1] for i in range(0, len(terms), 2)]
            rest = jnp.where(diag[None], 0.0, old) - terms[0]
    return jnp.stack(done).reshape(LEAF, LEAF)


def dot(a, b):
    return jnp.dot(a, b, precision=HIGHEST, preferred_element_type=F32)


def dot_t(a, b):
    return lax.dot_general(
        a, b, (((1,), (1,)), ((), ())), precision=HIGHEST, preferred_element_type=F32
    )


def factor_inverse(m_ref, w_ref):
    size = m_ref.shape[0]
    w_ref[...] = jnp.zeros(w_ref.shape, F32)

    def turn(step, carry):
        at = pl.ds(pl.multiple_of(step * LEAF, LEAF), LEAF)
        w_ref[at, at] = leaf_inverse(m_ref[at, at])
        for b in range(size // LEAF):
            r0, r1 = b * LEAF, (b + 1) * LEAF

            @pl.when(step == b)
            def _():
                inv = w_ref[r0:r1, r0:r1]
                if r0:
                    left = dot(inv, m_ref[r0:r1, :r0])
                    w_ref[r0:r1, :r0] = left
                if r1 < size:
                    back = dot_t(m_ref[r1:, r0:r1], inv)
                    for c in range(r1, size, LEAF):
                        m_ref[c:, c : c + LEAF] -= dot_t(
                            back[c - r1 :], back[c - r1 : c - r1 + LEAF]
                        )
                    m_ref[r1:, r0:r1] = -dot(back, inv)
                    if r0:
                        m_ref[r1:, :r0] -= dot(back, left)

        return carry

    lax.fori_loop(0, size // LEAF, turn, 0)


def tokens_at(full_ref, u, size):
    side, _, _, quarter, cols = full_ref.shape
    shard = 4 * quarter
    if size >= shard:
        m = size // shard
        if m <= side:
            part = full_ref[u * m // side, pl.ds(u * m % side, m)]
        else:
            part = full_ref[pl.ds(u * (m // side), m // side)]
    else:
        per = quarter // size
        part = full_ref[0, 0, u // per, pl.ds(u % per * size, size)]
    return part.reshape(size, cols)


def eight_rows(image_ref, row):
    side, _, _, quarter, _ = image_ref.shape
    shard, within = row // (4 * quarter), row % (4 * quarter)
    place = (shard // side, shard % side, within // quarter)
    if quarter == 8:
        return image_ref[place]
    return image_ref[(*place, pl.ds(pl.multiple_of(within % quarter, 8), 8))]


def masks(member_ref, line, groups):
    rows = lax.broadcasted_iota(jnp.int32, (line, line), 0)
    across = lax.broadcasted_iota(jnp.int32, (line, line), 1)
    row = jnp.broadcast_to(member_ref[...].astype(F32), (line, line))
    column = jnp.sum(jnp.where(rows == across, row, 0.0), axis=1, keepdims=True)
    wide = jnp.broadcast_to(column, (line, 128))
    spread = jnp.broadcast_to(wide[:, None, :], (line, 8, 128))
    return (row == column), [jnp.where(spread == g, 1.0, 0.0) for g in range(groups)]


def mixing(linked, rank):
    line = linked.shape[0]
    size = line * rank
    owner = lax.broadcasted_iota(jnp.int32, (size, line), 0) // rank
    block = lax.broadcasted_iota(jnp.int32, (size, line), 1)
    spread = jnp.where(owner == block, 1.0, 0.0).astype(BF16)
    tall = jnp.dot(spread, linked.astype(BF16), preferred_element_type=F32).astype(BF16)
    big = lax.dot_general(tall, spread, (((1,), (1,)), ((), ())), preferred_element_type=F32)
    rows = lax.broadcasted_iota(jnp.int32, (size, size), 0)
    across = lax.broadcasted_iota(jnp.int32, (size, size), 1)
    return jnp.where(rows % rank == across % rank, big, 0.0).astype(BF16)


def whole_kernel(
    groups, group_cols,
    acts_ref, init_ref, kept_ref, member_ref,
    bases_ref, latent_ref,
    full_ref, image_all, gram_ref, basis_ref, init_v, init_out, init_in,
    proj_out, proj_in, mixed_out, mixed_in, part_out, part_in, sum_out, sum_in,
    m_ref, w_ref, mix_ref, codes_out, codes_in, mapped, turned,
    local_sems, sems, xs, xr, is_, ir,
):
    here = Place()
    line, tok = here.line, here.tok
    rows = init_v.shape[0]
    rank, cols = basis_ref.shape
    total_rank = rank * tok
    tokens = line * proj_out.shape[2]
    reducers, per_tile = part_out.shape[:2]

    acts_copy = pltpu.make_async_copy(acts_ref, turned_acts(full_ref, here), local_sems.at[0])
    init_copy = pltpu.make_async_copy(init_ref, init_v, local_sems.at[1])
    acts_copy.start()
    init_copy.start()
    greet_start(line_devices(here) + plane_devices(here))
    init_copy.wait()
    turned_init = init_v[...].T
    if tok > 1:
        wide = jnp.concatenate([turned_init, jnp.zeros((total_rank, 128 - rows), F32)], axis=1)
        init_out[...] = wide.astype(BF16).reshape(init_out.shape)
    else:
        basis_ref[...] = turned_init.astype(BF16)
    acts_copy.wait()
    greet_finish(line + tok - 2)

    acts_x = Gather(here, full_ref, xs, xr)
    acts_x.start()
    spread = Exchange(here.p, tok, here.in_plane, init_out, init_in, sems, 0)
    if tok > 1:
        spread.send_all()
        spread.keep()
    same, member_masks = masks(member_ref, line, groups)
    linked = jnp.where(same, kept_ref[...].astype(F32), 0.0)
    mix_ref[...] = mixing(linked, rank)
    acts_x.finish()
    if tok > 1:
        spread.received()
        spread.sent()
        per = 128 // rows
        for c in range(tok // per):
            total = init_in[c * per].astype(F32)
            for d in range(1, per):
                total += pltpu.roll(init_in[c * per + d].astype(F32), d * rows, 1)
            basis_ref[:, c * 128 : c * 128 + 128] = total.astype(BF16)
    acts_x.sent()

    chunk = tokens // line
    per_step = 2 if line % 2 == 0 else 1
    steps = line // per_step
    proj_x = Exchange(here.k, line, here.in_line, proj_out, proj_in, sems, 1)
    mixed_x = Exchange(here.k, line, here.in_line, mixed_out, mixed_in, sems, 2)
    part_x = Exchange(here.k, line, here.in_line, part_out, part_in, sems, 3)
    sum_x = Exchange(here.k, line, here.in_line, sum_out, sum_in, sems, 4)
    gram_x = Exchange(here.p, tok, here.in_plane, gram_ref, gram_ref, sems, 5)
    codes_x = Exchange(here.k, line, here.in_line, codes_out, codes_in, sems, 6)
    reducing = here.k < reducers

    def iteration(turn, carry):
        image_ref = image_all.at[turn]

        def project(d, carry):
            u = (here.k // per_step + 1 + d) % steps
            proj = lax.dot_general(
                basis_ref[...], tokens_at(full_ref, u, per_step * chunk),
                (((1,), (1,)), ((), ())), preferred_element_type=F32,
            ).astype(BF16)
            for v in range(per_step):
                c = u * per_step + v
                proj_out[c] = proj[:, v * chunk : (v + 1) * chunk]

                @pl.when(c != here.k)
                def _():
                    proj_x.send(c)

            return carry

        lax.fori_loop(0, steps, project, 0)
        proj_x.keep()
        proj_x.received()
        stacked = proj_in[...].reshape(line * rank, chunk)
        mixed_out[...] = (
            jnp.dot(mix_ref[...], stacked, preferred_element_type=F32)
            .astype(BF16)
            .reshape(mixed_out.shape)
        )
        mixed_x.send_all()
        mixed_x.keep()
        mixed_x.received()
        mixed = jnp.concatenate([mixed_in[c] for c in range(line)], axis=1)
        acts = full_ref[...].reshape(tokens, cols)
        image = jnp.dot(mixed, acts, preferred_element_type=F32)
        image = image * (1.0 / tokens) + RIDGE * basis_ref[...].astype(F32)
        image_ref[here.y, here.x] = image.reshape(image_ref.shape[2:])
        image_x = Gather(here, image_ref, is_, ir)
        image_x.start()
        image_x.finish()

        whole = image_ref[...].reshape(total_rank, cols)
        tiles = []
        for c in range(0, total_rank, LEAF):
            high = (total_rank - c) // tok
            mine = [eight_rows(image_ref, c + here.p * high + r) for r in range(0, high, 8)]
            tile = dot_t(jnp.concatenate(mine, axis=0), whole[c : c + LEAF])
            tiles.append(tile.reshape(high // 8, 8, LEAF))
        part_out[...] = jnp.concatenate(tiles, axis=0).reshape(part_out.shape)

        def send_part(d, carry):
            to = lax.rem(here.k + d, line)

            @pl.when(to < reducers)
            def _():
                part_x.send(to)

            return carry

        lax.fori_loop(1, line, send_part, 0)

        @pl.when(turn == ITERS - 1)
        def _():
            own = full_ref[here.y, here.x].reshape(tokens // tok, cols).astype(F32)
            mapped[...] = dot_t(own, image_ref[...].reshape(total_rank, cols))

        @pl.when(reducing)
        def _():
            part_x.keep()
            part_x.received()
            totals = [
                jnp.sum(part_in[...] * mask[:, None], axis=0) for mask in member_masks
            ]
            for i in range(line):
                mine = member_masks[0][i][None] * totals[0]
                for g in range(1, groups):
                    mine += member_masks[g][i][None] * totals[g]
                sum_out[i] = mine
            sum_x.send_all()
            sum_x.keep()
            sum_x.received(reducers - 1)

        @pl.when(jnp.logical_not(reducing))
        def _():
            sum_x.received(reducers)

        gram_ref[here.p] = sum_in[...].reshape(gram_ref.shape[1:])
        if tok > 1:
            def send_gram(d, carry):
                to = lax.rem(here.p + d, tok)
                mine = gram_ref.at[here.p]
                group_copy(mine, mine, sems, 5, here.in_plane(to)).start()
                return carry

            lax.fori_loop(1, tok, send_gram, 0)
            gram_x.received()
        first = 0
        for c in range(0, total_rank, LEAF):
            count = (total_rank - c) // tok // 8
            panel = gram_ref[:, first : first + count].reshape(total_rank - c, LEAF)
            m_ref[c:, c : c + LEAF] = panel * (1.0 / group_cols)
            first += count

        proj_x.sent()
        mixed_x.sent()
        image_x.sent()

        @pl.when(reducing)
        def _():
            part_x.sent(reducers - 1)
            sum_x.sent()

        @pl.when(jnp.logical_not(reducing))
        def _():
            part_x.sent(reducers)

        if tok > 1:
            gram_x.sent()
        factor_inverse(m_ref, w_ref)

        @pl.when(turn < ITERS - 1)
        def _():
            at = pl.multiple_of(here.p * rank, rank)
            image = image_ref[...].reshape(total_rank, cols)
            basis_ref[...] = dot(w_ref[pl.ds(at, rank), :], image).astype(BF16)

        return carry

    lax.fori_loop(0, ITERS, iteration, 0)

    codes = dot_t(mapped[...], w_ref[...]).reshape(line, -1, total_rank)
    half = total_rank // 2
    codes_out[...] = jnp.concatenate([codes[:, :, :half], codes[:, :, half:]], axis=1).astype(BF16)
    codes_x.send_all()
    codes_x.keep()
    wide = turned.shape[0]
    per = wide // rows
    at = pl.multiple_of(here.p // per * wide, wide)
    part = image_all[ITERS - 1, :, :, :, :, pl.ds(at, wide)].reshape(total_rank, wide)
    turned[...] = dot(w_ref[...], part).T
    bases_ref[...] = turned[pl.ds(pl.multiple_of(here.p % per * rows, rows), rows), :]
    codes_x.received()
    scale = 1.0 / math.sqrt(group_cols)
    few = latent_ref.shape[0]
    for g in range(groups):
        for c in range(0, half, 128 if half % 128 == 0 else half):
            size = min(128, half)
            mask = member_masks[g][:, :1, :size]
            total = jnp.sum(codes_in[:, :, c : c + size].astype(F32) * mask, axis=0) * scale
            for h in (0, 1):
                at = g * total_rank + h * half + c
                latent_ref[:, at : at + size] = total[h * few : (h + 1) * few].astype(BF16)
    codes_x.sent()


def turned_acts(full_ref, here):
    return full_ref.at[here.y, here.x]


def greet_start(devices):
    barrier = pltpu.get_barrier_semaphore()
    for device in devices:
        pl.semaphore_signal(barrier, inc=1, device_id=device, device_id_type=MESH)


def greet_finish(count):
    pl.semaphore_wait(pltpu.get_barrier_semaphore(), count)


def per_device(acts, init_basis, kept, member):
    tok = lax.axis_size("tok")
    line = lax.axis_size("gr") * lax.axis_size("gc")
    side = math.isqrt(tok)
    groups = kept.shape[0] // GBLK
    rows, total_rank = init_basis.shape[1:]
    shard, cols = acts.shape
    tokens = shard * tok
    rank = total_rank // tok
    group_cols = GBLK * rows * tok
    tiles = sum((total_rank - c) // tok // 8 for c in range(0, total_rank, LEAF))
    reducers = max(d for d in range(1, line + 1) if tiles % d == 0)
    per_tile = tiles // reducers
    pieces = (line, rank, tokens // line)
    init_pieces = (tok, rank, 128)
    codes = (line, shard // line * 2, total_rank // 2)
    bases, latent = pl.pallas_call(
        functools.partial(whole_kernel, groups, group_cols),
        out_shape=(
            jax.ShapeDtypeStruct((rows, total_rank), F32),
            jax.ShapeDtypeStruct((shard // line, groups * total_rank), BF16),
        ),
        in_specs=[pl.BlockSpec(memory_space=pl.ANY), pl.BlockSpec(memory_space=pl.ANY), vmem(), vmem()],
        out_specs=(vmem(), vmem()),
        scratch_shapes=[
            pltpu.VMEM((side, side, 4, shard // 4, cols), BF16),
            pltpu.VMEM((ITERS, side, side, 4, rank // 4, cols), F32),
            pltpu.VMEM((tok, tiles, 8, LEAF), F32),
            pltpu.VMEM((rank, cols), BF16),
            pltpu.VMEM((rows, total_rank), F32),
            pltpu.VMEM(init_pieces, BF16),
            pltpu.VMEM(init_pieces, BF16),
            pltpu.VMEM(pieces, BF16),
            pltpu.VMEM(pieces, BF16),
            pltpu.VMEM(pieces, BF16),
            pltpu.VMEM(pieces, BF16),
            pltpu.VMEM((reducers, per_tile, 8, LEAF), F32),
            pltpu.VMEM((line, per_tile, 8, LEAF), F32),
            pltpu.VMEM((line, per_tile, 8, LEAF), F32),
            pltpu.VMEM((reducers, per_tile, 8, LEAF), F32),
            pltpu.VMEM((total_rank, total_rank), F32),
            pltpu.VMEM((total_rank, total_rank), F32),
            pltpu.VMEM((line * rank, line * rank), BF16),
            pltpu.VMEM(codes, BF16),
            pltpu.VMEM(codes, BF16),
            pltpu.VMEM((shard, total_rank), F32),
            pltpu.VMEM((max(rows, 128), total_rank), F32),
            pltpu.SemaphoreType.DMA((2,)),
            pltpu.SemaphoreType.DMA((2, 7)),
            pltpu.SemaphoreType.DMA((2,)),
            pltpu.SemaphoreType.DMA((2, 20)),
            pltpu.SemaphoreType.DMA((2,)),
            pltpu.SemaphoreType.DMA((2, 20)),
        ],
        compiler_params=params(0),
    )(acts.reshape(4, shard // 4, cols), init_basis[0], kept, member.reshape(1, -1))
    return bases[None], latent


def solution(mesh):
    placed = (P("tok", ("gr", "gc")), P(("gr", "gc"), "tok", None), P(), P())
    return jax.shard_map(
        per_device,
        mesh=mesh,
        in_specs=placed,
        out_specs=(P(("gr", "gc"), "tok", None), P(("tok", "gr", "gc"), None)),
        check_vma=False,
    )
```

```python
import functools
import math

import jax
import jax.numpy as jnp
from jax import lax
from jax.experimental import pallas as pl
from jax.experimental.pallas import tpu as pltpu
from jax.sharding import PartitionSpec as P

GBLK = 8
ITERS = 2
RIDGE = 2.0
LEAF = 128
HIGH = 16
MESH = pl.DeviceIdType.MESH
HIGHEST = lax.Precision.HIGHEST
VMEM_LIMIT = 60 * 2**20
F32 = jnp.float32
BF16 = jnp.bfloat16


def vmem():
    return pl.BlockSpec(memory_space=pltpu.VMEM)


def smem():
    return pl.BlockSpec(memory_space=pltpu.SMEM)


def params(collective_id=None):
    if collective_id is None:
        return pltpu.CompilerParams(vmem_limit_bytes=VMEM_LIMIT)
    return pltpu.CompilerParams(
        vmem_limit_bytes=VMEM_LIMIT, collective_id=collective_id, has_side_effects=True
    )


class Place:
    def __init__(self):
        self.tok = lax.axis_size("tok")
        self.gc = lax.axis_size("gc")
        self.line = lax.axis_size("gr") * self.gc
        self.side = math.isqrt(self.tok)
        self.p = lax.axis_index("tok")
        self.gr_at = lax.axis_index("gr")
        self.gc_at = lax.axis_index("gc")
        self.k = self.gr_at * self.gc + self.gc_at
        self.y = self.p // self.side
        self.x = self.p % self.side

    def in_plane(self, p):
        return (p, self.gr_at, self.gc_at)

    def in_line(self, k):
        return (self.p, k // self.gc, k % self.gc)

    def at_axis(self, axis, at):
        if axis == "x":
            return self.in_plane(self.y * self.side + at)
        return self.in_plane(at * self.side + self.x)


def greet(devices):
    barrier = pltpu.get_barrier_semaphore()
    for device in devices:
        pl.semaphore_signal(barrier, inc=1, device_id=device, device_id_type=MESH)
    if devices:
        pl.semaphore_wait(barrier, len(devices))


def line_devices(here):
    return [here.in_line((here.k + d) % here.line) for d in range(1, here.line)]


def plane_devices(here):
    return [here.in_plane((here.p + d) % here.tok) for d in range(1, here.tok)]


def ring_devices(here):
    if here.tok == 1:
        return []
    side = here.side
    return [
        here.at_axis(axis, (at + d) % side)
        for axis, at in (("x", here.x), ("y", here.y))
        for d in (1, side - 1)
    ]


def rcopy(src, dst, send, recv, device):
    return pltpu.make_async_remote_copy(
        src_ref=src, dst_ref=dst, send_sem=send, recv_sem=recv, device_id=device, device_id_type=MESH
    )


class Gather:
    PARTS = ((0, 2), (0, 2), (0, 1), (1, 1))

    def __init__(self, here, buf, send, recv):
        self.here, self.buf, self.send, self.recv = here, buf, send, recv
        self.side = here.side
        self.axes = (("x", "y"), ("y", "x"))
        self.at = ((here.x, here.y), (here.y, here.x))

    def near(self, part, ring, step):
        return lax.rem(self.at[part][ring] + step, self.side)

    def copy(self, part, ring, kind, owner, rel, slot):
        low, number = self.PARTS[kind]
        first, second = (owner, self.at[part][1]) if ring == 0 else (self.near(part, 0, rel), owner)
        y, x = (second, first) if part == 0 else (first, second)
        ref = self.buf.at[y, x, pl.ds(2 * part + low, number)]
        to = self.near(part, ring, 1 if kind in (0, 2) else self.side - 1)
        device = self.here.at_axis(self.axes[part][ring], to)
        return rcopy(ref, ref, self.send.at[ring], self.recv.at[part, slot], device)

    def one(self, part, kind, step):
        return self.copy(part, 0, kind, self.near(part, 0, step), 0, kind)

    def two(self, part, rel, kind, step):
        return self.copy(part, 1, kind, self.near(part, 1, step), rel, 4 + 4 * rel + kind)

    def start(self):
        if self.here.tok == 1:
            return
        for part in (0, 1):
            self.one(part, 0, 0).start()
            self.one(part, 1, 0).start()
        for part in (0, 1):
            self.share(part, 0)

    def share(self, part, rel):
        self.two(part, rel, 0, 0).start()
        self.two(part, rel, 1, 0).start()

    def pass_on(self, part, rel):
        self.two(part, rel, 0, 3).wait_recv()
        self.two(part, rel, 2, 3).start()
        self.two(part, rel, 1, 1).wait_recv()
        self.two(part, rel, 3, 1).start()

    def finish(self):
        if self.here.tok == 1:
            return
        for part in (0, 1):
            self.one(part, 0, 3).wait_recv()
            self.one(part, 2, 3).start()
            self.share(part, 3)
        for part in (0, 1):
            self.one(part, 1, 1).wait_recv()
            self.one(part, 3, 1).start()
            self.share(part, 1)
        for part in (0, 1):
            self.pass_on(part, 0)
        for part in (0, 1):
            self.one(part, 2, 2).wait_recv()
            self.one(part, 3, 2).wait_recv()
            self.share(part, 2)
        for rel in (3, 1, 2):
            for part in (0, 1):
                self.pass_on(part, rel)
        for rel in (0, 3, 1, 2):
            for part in (0, 1):
                self.two(part, rel, 2, 2).wait_recv()
                self.two(part, rel, 3, 2).wait_recv()

    def sent(self):
        if self.here.tok == 1:
            return
        device = self.here.at_axis("x", self.near(0, 0, 1))
        for ring, ref in ((0, self.buf.at[0, pl.ds(0, 3)]), (1, self.buf.at[pl.ds(0, 3)])):
            rcopy(ref, ref, self.send.at[ring], self.recv.at[0, 0], device).wait_send()


class Cross:
    def __init__(self, here, buf, sems):
        self.here, self.buf, self.sems = here, buf, sems
        self.side = here.side
        self.axes = (("x", "y"), ("y", "x"))
        self.at = ((here.x, here.y), (here.y, here.x))

    def go(self, part, ring, rel):
        first = lax.rem(self.at[part][0] + rel, self.side)
        second = self.at[part][1]
        y, x = (second, first) if part == 0 else (first, second)
        ref = self.buf.at[y, x, pl.ds(2 * part, 2)]
        which = 2 * part + ring
        for d in (2, 1, 3):
            to = lax.rem(self.at[part][ring] + d, self.side)
            device = self.here.at_axis(self.axes[part][ring], to)
            rcopy(ref, ref, self.sems.at[0, which], self.sems.at[1, which], device).start()

    def whole(self, part, ring):
        ref = self.buf.at[0, pl.ds(0, 3), pl.ds(0, 2)] if ring == 0 else self.buf.at[pl.ds(0, 3), :, pl.ds(0, 2)]
        which = 2 * part + ring
        device = self.here.at_axis("x", lax.rem(self.here.x + 1, self.side))
        return rcopy(ref, ref, self.sems.at[0, which], self.sems.at[1, which], device)

    def start(self):
        if self.here.tok > 1:
            for ring in (0, 1):
                for part in (0, 1):
                    self.go(part, ring, 0)

    def middle(self):
        if self.here.tok > 1:
            for part in (0, 1):
                self.whole(part, 0).wait_recv()
                for rel in (1, 3, 2):
                    self.go(part, 1, rel)

    def finish(self):
        if self.here.tok > 1:
            for part in (0, 1):
                self.whole(part, 1).wait_recv()

    def sent(self):
        if self.here.tok > 1:
            for part in (0, 1):
                for ring in (0, 1):
                    self.whole(part, ring).wait_send()


def group_copy(src, dst, sems, which, device):
    return rcopy(src, dst, sems.at[0, which], sems.at[1, which], device)


class Exchange:
    def __init__(self, at, count, device, src, dst, sems, which):
        self.at, self.count, self.device = at, count, device
        self.src, self.dst, self.sems, self.which = src, dst, sems, which

    def send(self, to):
        group_copy(
            self.src.at[to], self.dst.at[self.at], self.sems, self.which, self.device(to)
        ).start()

    def send_all(self):
        def body(d, carry):
            self.send(lax.rem(self.at + d, self.count))
            return carry

        lax.fori_loop(1, self.count, body, 0)

    def keep(self):
        self.dst[self.at] = self.src[self.at]

    def all_of(self, ref, number):
        other = lax.rem(self.at + 1, self.count)
        return group_copy(
            ref.at[pl.ds(0, number)], ref.at[pl.ds(0, number)], self.sems, self.which, self.device(other)
        )

    def received(self, number=None):
        number = self.count - 1 if number is None else number
        if number:
            self.all_of(self.dst, number).wait_recv()

    def sent(self, number=None):
        number = self.count - 1 if number is None else number
        if number:
            self.all_of(self.src, number).wait_send()


def leaf_inverse(block):
    count = LEAF // HIGH
    shape = (HIGH, LEAF)
    lane = lax.broadcasted_iota(jnp.int32, shape, 1)
    sub = lax.broadcasted_iota(jnp.int32, shape, 0)

    def down(v, r):
        return jnp.broadcast_to(v[r : r + 1, :], shape)

    done = []
    rest = block.reshape(count, HIGH, LEAF)
    for s in range(count):
        c0 = HIGH * s
        here = rest[0]
        cols = [jnp.broadcast_to(here[:, c0 + j : c0 + j + 1], shape) for j in range(HIGH)]
        diag = (lane >= c0) & (lane < c0 + HIGH)
        first = jnp.where(diag, jnp.where(lane - c0 == sub, 1.0, 0.0), here)
        full, low = first, first
        pivots = jnp.ones(shape, F32)
        for j in range(HIGH):
            pivot = down(cols[j], j)
            inverse = 1.0 / pivot
            others = jnp.where(sub == j, 0.0, cols[j])
            below = jnp.where(sub > j, cols[j], 0.0)
            for k in range(j + 1, HIGH):
                cols[k] = cols[k] - (others * down(cols[k], j)) * inverse
            full = full - (others * down(full, j)) * inverse
            low = low - (below * down(low, j)) * inverse
            pivots = jnp.where(sub == j, pivot, pivots)
        solved = full / pivots
        done.append(jnp.where(lane < c0 + HIGH, low * lax.rsqrt(pivots), 0.0))
        if s + 1 < count:
            old = rest[1:]
            terms = [
                jnp.broadcast_to(old[:, :, c0 + k : c0 + k + 1], old.shape) * down(solved, k)[None]
                for k in range(HIGH)
            ]
            while len(terms) > 1:
                terms = [terms[i] + terms[i + 1] for i in range(0, len(terms), 2)]
            rest = jnp.where(diag[None], 0.0, old) - terms[0]
    return jnp.stack(done).reshape(LEAF, LEAF)


def dot(a, b):
    return jnp.dot(a, b, precision=HIGHEST, preferred_element_type=F32)


def dot_t(a, b):
    return lax.dot_general(
        a, b, (((1,), (1,)), ((), ())), precision=HIGHEST, preferred_element_type=F32
    )


def factor_inverse(m_ref, w_ref):
    size = m_ref.shape[0]
    w_ref[...] = jnp.zeros(w_ref.shape, F32)

    def turn(step, carry):
        at = pl.ds(pl.multiple_of(step * LEAF, LEAF), LEAF)
        w_ref[at, at] = leaf_inverse(m_ref[at, at])
        for b in range(size // LEAF):
            r0, r1 = b * LEAF, (b + 1) * LEAF

            @pl.when(step == b)
            def _():
                inv = w_ref[r0:r1, r0:r1]
                if r0:
                    left = dot(inv, m_ref[r0:r1, :r0])
                    w_ref[r0:r1, :r0] = left
                if r1 < size:
                    back = dot_t(m_ref[r1:, r0:r1], inv)
                    for c in range(r1, size, LEAF):
                        m_ref[c:, c : c + LEAF] -= dot_t(
                            back[c - r1 :], back[c - r1 : c - r1 + LEAF]
                        )
                    m_ref[r1:, r0:r1] = -dot(back, inv)
                    if r0:
                        m_ref[r1:, :r0] -= dot(back, left)

        return carry

    lax.fori_loop(0, size // LEAF, turn, 0)


def tokens_at(full_ref, u, size):
    side, _, _, quarter, cols = full_ref.shape
    shard = 4 * quarter
    if size >= shard:
        m = size // shard
        if m <= side:
            part = full_ref[u * m // side, pl.ds(u * m % side, m)]
        else:
            part = full_ref[pl.ds(u * (m // side), m // side)]
    else:
        per = quarter // size
        part = full_ref[0, 0, u // per, pl.ds(u % per * size, size)]
    return part.reshape(size, cols)


def eight_rows(image_ref, row):
    side, _, _, quarter, _ = image_ref.shape
    shard, within = row // (4 * quarter), row % (4 * quarter)
    place = (shard // side, shard % side, within // quarter)
    if quarter == 8:
        return image_ref[place]
    return image_ref[(*place, pl.ds(pl.multiple_of(within % quarter, 8), 8))]


def thirds(x, axis=0):
    high = x.astype(BF16)
    rest = x - high.astype(F32)
    middle = rest.astype(BF16)
    return jnp.concatenate([high, middle, (rest - middle.astype(F32)).astype(BF16)], axis=axis)


def sum_thirds(x, axis=0):
    high, middle, low = jnp.split(x, 3, axis=axis)
    return high + (middle + low)


def masks(member_ref, line, groups):
    rows = lax.broadcasted_iota(jnp.int32, (line, line), 0)
    across = lax.broadcasted_iota(jnp.int32, (line, line), 1)
    row = jnp.broadcast_to(member_ref[...].astype(F32), (line, line))
    column = jnp.sum(jnp.where(rows == across, row, 0.0), axis=1, keepdims=True)
    wide = jnp.broadcast_to(column, (line, 128))
    spread = jnp.broadcast_to(wide[:, None, :], (line, 8, 128))
    return (row == column), [jnp.where(spread == g, 1.0, 0.0) for g in range(groups)]


def mixing(linked, rank):
    line = linked.shape[0]
    size = line * rank
    owner = lax.broadcasted_iota(jnp.int32, (size, line), 0) // rank
    block = lax.broadcasted_iota(jnp.int32, (size, line), 1)
    spread = jnp.where(owner == block, 1.0, 0.0).astype(BF16)
    tall = jnp.dot(spread, linked.astype(BF16), preferred_element_type=F32).astype(BF16)
    big = lax.dot_general(tall, spread, (((1,), (1,)), ((), ())), preferred_element_type=F32)
    rows = lax.broadcasted_iota(jnp.int32, (size, size), 0)
    across = lax.broadcasted_iota(jnp.int32, (size, size), 1)
    return jnp.where(rows % rank == across % rank, big, 0.0).astype(BF16)


def whole_kernel(
    groups, group_cols,
    acts_ref, init_ref, kept_ref, member_ref,
    bases_ref, latent_ref,
    full_ref, image_all, gram_ref, basis_ref, init_v, init_out, init_in,
    proj_out, proj_in, mixed_out, mixed_in, part_out, part_in, sum_out, sum_in,
    wide_out, wide_in, summed_out, summed_in, thirds_ref,
    m_ref, w_ref, mix_ref, codes_out, codes_in, mapped, turned,
    local_sems, sems, xs, xr, cross_sems,
):
    here = Place()
    line, tok = here.line, here.tok
    rows = init_v.shape[0]
    rank, cols = basis_ref.shape
    total_rank = rank * tok
    tokens = line * proj_out.shape[2]
    reducers, per_tile = part_out.shape[:2]

    acts_copy = pltpu.make_async_copy(acts_ref, turned_acts(full_ref, here), local_sems.at[0])
    init_copy = pltpu.make_async_copy(init_ref, init_v, local_sems.at[1])
    acts_copy.start()
    init_copy.start()
    greet_start(line_devices(here) + plane_devices(here))
    init_copy.wait()
    turned_init = init_v[...].T
    if tok > 1:
        wide = jnp.concatenate([turned_init, jnp.zeros((total_rank, 128 - rows), F32)], axis=1)
        init_out[...] = wide.astype(BF16).reshape(init_out.shape)
    else:
        basis_ref[...] = turned_init.astype(BF16)
    acts_copy.wait()
    greet_finish(line + tok - 2)

    acts_x = Gather(here, full_ref, xs, xr)
    acts_x.start()
    spread = Exchange(here.p, tok, here.in_plane, init_out, init_in, sems, 0)
    if tok > 1:
        spread.send_all()
        spread.keep()
    same, member_masks = masks(member_ref, line, groups)
    linked = jnp.where(same, kept_ref[...].astype(F32), 0.0)
    mix_ref[...] = mixing(linked, rank)
    acts_x.finish()
    if tok > 1:
        spread.received()
        spread.sent()
        per = 128 // rows
        for c in range(tok // per):
            total = init_in[c * per].astype(F32)
            for d in range(1, per):
                total += pltpu.roll(init_in[c * per + d].astype(F32), d * rows, 1)
            basis_ref[:, c * 128 : c * 128 + 128] = total.astype(BF16)
    acts_x.sent()

    chunk = tokens // line
    per_step = 2 if line % 2 == 0 else 1
    steps = line // per_step

    def line_exchange(src, dst, which):
        return Exchange(here.k, line, here.in_line, src, dst, sems, which)

    reducing = here.k < reducers

    proj_x = line_exchange(proj_out, proj_in, 1)
    mixed_x = line_exchange(mixed_out, mixed_in, 2)
    part_x = line_exchange(part_out, part_in, 3)
    sum_x = line_exchange(sum_out, sum_in, 4)
    codes_x = line_exchange(codes_out, codes_in, 7)
    wide_x = line_exchange(wide_out, wide_in, 8)
    summed_x = line_exchange(summed_out, summed_in, 9)
    first_image, image, mapped_image = (image_all.at[n] for n in range(3))
    first_x = Cross(here, first_image, cross_sems.at[0])
    mapped_x = Cross(here, mapped_image, cross_sems.at[1])

    def project(basis, finish, exchange):
        def body(d, carry):
            u = (here.k // per_step + 1 + d) % steps
            proj = finish(
                lax.dot_general(
                    basis[...], tokens_at(full_ref, u, per_step * chunk),
                    (((1,), (1,)), ((), ())), preferred_element_type=F32,
                )
            )
            for v in range(per_step):
                c = u * per_step + v
                exchange.src[c] = proj[:, v * chunk : (v + 1) * chunk]

                @pl.when(c != here.k)
                def _():
                    exchange.send(c)

            return carry

        lax.fori_loop(0, steps, body, 0)
        exchange.keep()

    def acts():
        return full_ref[...].reshape(tokens, cols)

    project(basis_ref, lambda proj: proj.astype(BF16), proj_x)
    proj_x.received()
    stacked = proj_in[...].reshape(line * rank, chunk)
    mixed_out[...] = (
        jnp.dot(mix_ref[...], stacked, preferred_element_type=F32)
        .astype(BF16)
        .reshape(mixed_out.shape)
    )
    mixed_x.send_all()
    mixed_x.keep()
    mixed_x.received()
    mixed = jnp.concatenate([mixed_in[c] for c in range(line)], axis=1)
    own = jnp.dot(mixed, acts(), preferred_element_type=F32)
    own = own * (1.0 / tokens) + RIDGE * basis_ref[...].astype(F32)
    first_image[here.y, here.x] = own.reshape(image_all.shape[3:])
    first_x.start()
    thirds_ref[...] = thirds(own)
    project(thirds_ref, sum_thirds, wide_x)
    first_x.middle()
    first_x.finish()

    def iteration(turn, carry):
        image_ref = image_all.at[turn]
        gram_at = gram_ref.at[turn]

        whole = image_ref[...].reshape(total_rank, cols)
        tiles = []
        for c in range(0, total_rank, LEAF):
            high = (total_rank - c) // tok
            mine = [eight_rows(image_ref, c + here.p * high + r) for r in range(0, high, 8)]
            tile = dot_t(jnp.concatenate(mine, axis=0), whole[c : c + LEAF])
            tiles.append(tile.reshape(high // 8, 8, LEAF))
        part_out[...] = jnp.concatenate(tiles, axis=0).reshape(part_out.shape)

        def send_part(d, carry):
            to = lax.rem(here.k + d, line)

            @pl.when(to < reducers)
            def _():
                part_x.send(to)

            return carry

        lax.fori_loop(1, line, send_part, 0)

        @pl.when(turn == 0)
        def _():
            wide_x.received()
            split = thirds(wide_in[...].reshape(line * rank, chunk), axis=1)
            product = jnp.dot(mix_ref[...], split, preferred_element_type=F32)
            summed_out[...] = sum_thirds(product, axis=1).reshape(summed_out.shape)
            summed_x.send_all()
            summed_x.keep()

        @pl.when(turn == ITERS - 1)
        def _():
            own = full_ref[here.y, here.x].reshape(tokens // tok, cols).astype(F32)
            mapped[...] = dot_t(own, image_ref[...].reshape(total_rank, cols))

        @pl.when(reducing)
        def _():
            part_x.keep()
            part_x.received()
            totals = [
                jnp.sum(part_in[...] * mask[:, None], axis=0) for mask in member_masks
            ]
            for i in range(line):
                mine = member_masks[0][i][None] * totals[0]
                for g in range(1, groups):
                    mine += member_masks[g][i][None] * totals[g]
                sum_out[i] = mine
            sum_x.send_all()
            sum_x.keep()
            sum_x.received(reducers - 1)

        @pl.when(jnp.logical_not(reducing))
        def _():
            sum_x.received(reducers)

        gram_at[here.p] = sum_in[...].reshape(gram_ref.shape[2:])
        gram_x = Exchange(here.p, tok, here.in_plane, gram_at, gram_at, sems, 5 + turn)
        if tok > 1:
            def send_gram(d, carry):
                to = lax.rem(here.p + d, tok)
                mine = gram_at.at[here.p]
                group_copy(mine, mine, sems, 5 + turn, here.in_plane(to)).start()
                return carry

            lax.fori_loop(1, tok, send_gram, 0)

        @pl.when(turn == 0)
        def _():
            summed_x.received()
            mixed = jnp.concatenate([summed_in[c] for c in range(line)], axis=1)
            product = sum_thirds(jnp.dot(thirds(mixed), acts(), preferred_element_type=F32))
            own = first_image[here.y, here.x].reshape(rank, cols)
            own = product * (1.0 / tokens) + RIDGE * own
            mapped_image[here.y, here.x] = own.reshape(image_all.shape[3:])
            mapped_x.start()

        gram_x.received()
        first = 0
        for c in range(0, total_rank, LEAF):
            count = (total_rank - c) // tok // 8
            panel = gram_at[:, first : first + count].reshape(total_rank - c, LEAF)
            m_ref[c:, c : c + LEAF] = panel * (1.0 / group_cols)
            first += count

        @pl.when(turn == 0)
        def _():
            mapped_x.middle()

        @pl.when(reducing)
        def _():
            part_x.sent(reducers - 1)
            sum_x.sent()

        @pl.when(jnp.logical_not(reducing))
        def _():
            part_x.sent(reducers)

        gram_x.sent()
        factor_inverse(m_ref, w_ref)

        @pl.when(turn == 0)
        def _():
            mapped_x.finish()
            source = mapped_image[...].reshape(total_rank, cols)
            upper = total_rank // 2
            image[...] = jnp.concatenate(
                [dot(w_ref[:upper, :upper], source[:upper]), dot(w_ref[upper:, :], source)], axis=0
            ).reshape(image_all.shape[1:])

        return carry

    lax.fori_loop(0, ITERS, iteration, 0)

    codes = dot_t(mapped[...], w_ref[...]).reshape(line, -1, total_rank)
    half = total_rank // 2
    codes_out[...] = jnp.concatenate([codes[:, :, :half], codes[:, :, half:]], axis=1).astype(BF16)
    codes_x.send_all()
    codes_x.keep()
    wide = turned.shape[0]
    per = wide // rows
    at = pl.multiple_of(here.p // per * wide, wide)
    part = image_all[1, :, :, :, :, pl.ds(at, wide)].reshape(total_rank, wide)
    turned[...] = dot(w_ref[...], part).T
    bases_ref[...] = turned[pl.ds(pl.multiple_of(here.p % per * rows, rows), rows), :]
    codes_x.received()
    scale = 1.0 / math.sqrt(group_cols)
    few = latent_ref.shape[0]
    for g in range(groups):
        for c in range(0, half, 128 if half % 128 == 0 else half):
            size = min(128, half)
            mask = member_masks[g][:, :1, :size]
            total = jnp.sum(codes_in[:, :, c : c + size].astype(F32) * mask, axis=0) * scale
            for h in (0, 1):
                at = g * total_rank + h * half + c
                latent_ref[:, at : at + size] = total[h * few : (h + 1) * few].astype(BF16)
    codes_x.sent()
    for exchange in (proj_x, mixed_x, wide_x, summed_x, first_x, mapped_x):
        exchange.sent()


def turned_acts(full_ref, here):
    return full_ref.at[here.y, here.x]


def greet_start(devices):
    barrier = pltpu.get_barrier_semaphore()
    for device in devices:
        pl.semaphore_signal(barrier, inc=1, device_id=device, device_id_type=MESH)


def greet_finish(count):
    pl.semaphore_wait(pltpu.get_barrier_semaphore(), count)


def per_device(acts, init_basis, kept, member):
    tok = lax.axis_size("tok")
    line = lax.axis_size("gr") * lax.axis_size("gc")
    side = math.isqrt(tok)
    groups = kept.shape[0] // GBLK
    rows, total_rank = init_basis.shape[1:]
    shard, cols = acts.shape
    tokens = shard * tok
    rank = total_rank // tok
    group_cols = GBLK * rows * tok
    tiles = sum((total_rank - c) // tok // 8 for c in range(0, total_rank, LEAF))
    reducers = max(d for d in range(1, line + 1) if tiles % d == 0)
    per_tile = tiles // reducers
    pieces = (line, rank, tokens // line)
    init_pieces = (tok, rank, 128)
    codes = (line, shard // line * 2, total_rank // 2)
    bases, latent = pl.pallas_call(
        functools.partial(whole_kernel, groups, group_cols),
        out_shape=(
            jax.ShapeDtypeStruct((rows, total_rank), F32),
            jax.ShapeDtypeStruct((shard // line, groups * total_rank), BF16),
        ),
        in_specs=[pl.BlockSpec(memory_space=pl.ANY), pl.BlockSpec(memory_space=pl.ANY), vmem(), vmem()],
        out_specs=(vmem(), vmem()),
        scratch_shapes=[
            pltpu.VMEM((side, side, 4, shard // 4, cols), BF16),
            pltpu.VMEM((3, side, side, 4, rank // 4, cols), F32),
            pltpu.VMEM((ITERS, tok, tiles, 8, LEAF), F32),
            pltpu.VMEM((rank, cols), BF16),
            pltpu.VMEM((rows, total_rank), F32),
            pltpu.VMEM(init_pieces, BF16),
            pltpu.VMEM(init_pieces, BF16),
            pltpu.VMEM(pieces, BF16),
            pltpu.VMEM(pieces, BF16),
            pltpu.VMEM(pieces, BF16),
            pltpu.VMEM(pieces, BF16),
            pltpu.VMEM((reducers, per_tile, 8, LEAF), F32),
            pltpu.VMEM((line, per_tile, 8, LEAF), F32),
            pltpu.VMEM((line, per_tile, 8, LEAF), F32),
            pltpu.VMEM((reducers, per_tile, 8, LEAF), F32),
            pltpu.VMEM(pieces, F32),
            pltpu.VMEM(pieces, F32),
            pltpu.VMEM(pieces, F32),
            pltpu.VMEM(pieces, F32),
            pltpu.VMEM((3 * rank, cols), BF16),
            pltpu.VMEM((total_rank, total_rank), F32),
            pltpu.VMEM((total_rank, total_rank), F32),
            pltpu.VMEM((line * rank, line * rank), BF16),
            pltpu.VMEM(codes, BF16),
            pltpu.VMEM(codes, BF16),
            pltpu.VMEM((shard, total_rank), F32),
            pltpu.VMEM((max(rows, 128), total_rank), F32),
            pltpu.SemaphoreType.DMA((2,)),
            pltpu.SemaphoreType.DMA((2, 10)),
            pltpu.SemaphoreType.DMA((2,)),
            pltpu.SemaphoreType.DMA((2, 20)),
            pltpu.SemaphoreType.DMA((2, 2, 4)),
        ],
        compiler_params=params(0),
    )(acts.reshape(4, shard // 4, cols), init_basis[0], kept, member.reshape(1, -1))
    return bases[None], latent


def solution(mesh):
    placed = (P("tok", ("gr", "gc")), P(("gr", "gc"), "tok", None), P(), P())
    return jax.shard_map(
        per_device,
        mesh=mesh,
        in_specs=placed,
        out_specs=(P(("gr", "gc"), "tok", None), P(("tok", "gr", "gc"), None)),
        check_vma=False,
    )
```

```python
import functools
import math

import jax
import jax.numpy as jnp
from jax import lax
from jax.experimental import pallas as pl
from jax.experimental.pallas import tpu as pltpu
from jax.sharding import PartitionSpec as P

GBLK = 8
ITERS = 2
RIDGE = 2.0
LEAF = 128
HIGH = 16
MESH = pl.DeviceIdType.MESH
HIGHEST = lax.Precision.HIGHEST
VMEM_LIMIT = 60 * 2**20
F32 = jnp.float32
BF16 = jnp.bfloat16


def vmem():
    return pl.BlockSpec(memory_space=pltpu.VMEM)


def smem():
    return pl.BlockSpec(memory_space=pltpu.SMEM)


def params(collective_id=None):
    if collective_id is None:
        return pltpu.CompilerParams(vmem_limit_bytes=VMEM_LIMIT)
    return pltpu.CompilerParams(
        vmem_limit_bytes=VMEM_LIMIT, collective_id=collective_id, has_side_effects=True
    )


class Place:
    def __init__(self):
        self.tok = lax.axis_size("tok")
        self.gc = lax.axis_size("gc")
        self.line = lax.axis_size("gr") * self.gc
        self.side = math.isqrt(self.tok)
        self.p = lax.axis_index("tok")
        self.gr_at = lax.axis_index("gr")
        self.gc_at = lax.axis_index("gc")
        self.k = self.gr_at * self.gc + self.gc_at
        self.y = self.p // self.side
        self.x = self.p % self.side

    def in_plane(self, p):
        return (p, self.gr_at, self.gc_at)

    def in_line(self, k):
        return (self.p, k // self.gc, k % self.gc)

    def at_axis(self, axis, at):
        if axis == "x":
            return self.in_plane(self.y * self.side + at)
        return self.in_plane(at * self.side + self.x)


def greet(devices):
    barrier = pltpu.get_barrier_semaphore()
    for device in devices:
        pl.semaphore_signal(barrier, inc=1, device_id=device, device_id_type=MESH)
    if devices:
        pl.semaphore_wait(barrier, len(devices))


def line_others(here):
    steps = sorted(range(1, here.line), key=lambda d: -min(d, here.line - d))
    return [lax.rem(here.k + d, here.line) for d in steps]


def plane_others(here):
    side = here.side
    steps = [(dy, dx) for dy in range(side) for dx in range(side)][1:]
    steps.sort(key=lambda d: -sum(min(a, side - a) for a in d))
    return [lax.rem(here.y + dy, side) * side + lax.rem(here.x + dx, side) for dy, dx in steps]


def ring_devices(here):
    if here.tok == 1:
        return []
    side = here.side
    return [
        here.at_axis(axis, (at + d) % side)
        for axis, at in (("x", here.x), ("y", here.y))
        for d in (1, side - 1)
    ]


def rcopy(src, dst, send, recv, device):
    return pltpu.make_async_remote_copy(
        src_ref=src, dst_ref=dst, send_sem=send, recv_sem=recv, device_id=device, device_id_type=MESH
    )


class Gather:
    PARTS = ((0, 2), (0, 2), (0, 1), (1, 1))

    def __init__(self, here, buf, send, recv):
        self.here, self.buf, self.send, self.recv = here, buf, send, recv
        self.side = here.side
        self.axes = (("x", "y"), ("y", "x"))
        self.at = ((here.x, here.y), (here.y, here.x))

    def near(self, part, ring, step):
        return lax.rem(self.at[part][ring] + step, self.side)

    def copy(self, part, ring, kind, owner, rel, slot):
        low, number = self.PARTS[kind]
        first, second = (owner, self.at[part][1]) if ring == 0 else (self.near(part, 0, rel), owner)
        y, x = (second, first) if part == 0 else (first, second)
        ref = self.buf.at[y, x, pl.ds(2 * part + low, number)]
        to = self.near(part, ring, 1 if kind in (0, 2) else self.side - 1)
        device = self.here.at_axis(self.axes[part][ring], to)
        return rcopy(ref, ref, self.send.at[ring], self.recv.at[part, slot], device)

    def one(self, part, kind, step):
        return self.copy(part, 0, kind, self.near(part, 0, step), 0, kind)

    def two(self, part, rel, kind, step):
        return self.copy(part, 1, kind, self.near(part, 1, step), rel, 4 + 4 * rel + kind)

    def start(self):
        if self.here.tok == 1:
            return
        for part in (0, 1):
            self.one(part, 0, 0).start()
            self.one(part, 1, 0).start()
        for part in (0, 1):
            self.share(part, 0)

    def share(self, part, rel):
        self.two(part, rel, 0, 0).start()
        self.two(part, rel, 1, 0).start()

    def pass_on(self, part, rel):
        self.two(part, rel, 0, 3).wait_recv()
        self.two(part, rel, 2, 3).start()
        self.two(part, rel, 1, 1).wait_recv()
        self.two(part, rel, 3, 1).start()

    def finish(self):
        if self.here.tok == 1:
            return
        for part in (0, 1):
            self.one(part, 0, 3).wait_recv()
            self.one(part, 2, 3).start()
            self.share(part, 3)
        for part in (0, 1):
            self.one(part, 1, 1).wait_recv()
            self.one(part, 3, 1).start()
            self.share(part, 1)
        for part in (0, 1):
            self.pass_on(part, 0)
        for part in (0, 1):
            self.one(part, 2, 2).wait_recv()
            self.one(part, 3, 2).wait_recv()
            self.share(part, 2)
        for rel in (3, 1, 2):
            for part in (0, 1):
                self.pass_on(part, rel)
        for rel in (0, 3, 1, 2):
            for part in (0, 1):
                self.two(part, rel, 2, 2).wait_recv()
                self.two(part, rel, 3, 2).wait_recv()

    def sent(self):
        if self.here.tok == 1:
            return
        device = self.here.at_axis("x", self.near(0, 0, 1))
        for ring, ref in ((0, self.buf.at[0, pl.ds(0, 3)]), (1, self.buf.at[pl.ds(0, 3)])):
            rcopy(ref, ref, self.send.at[ring], self.recv.at[0, 0], device).wait_send()


class Cross:
    def __init__(self, here, buf, sems):
        self.here, self.buf, self.sems = here, buf, sems
        self.side = here.side
        self.axes = (("x", "y"), ("y", "x"))
        self.at = ((here.x, here.y), (here.y, here.x))

    def go(self, part, ring, rel):
        first = lax.rem(self.at[part][0] + rel, self.side)
        second = self.at[part][1]
        y, x = (second, first) if part == 0 else (first, second)
        ref = self.buf.at[y, x, pl.ds(2 * part, 2)]
        which = 2 * part + ring
        for d in (2, 1, 3):
            to = lax.rem(self.at[part][ring] + d, self.side)
            device = self.here.at_axis(self.axes[part][ring], to)
            rcopy(ref, ref, self.sems.at[0, which], self.sems.at[1, which], device).start()

    def whole(self, part, ring):
        ref = self.buf.at[0, pl.ds(0, 3), pl.ds(0, 2)] if ring == 0 else self.buf.at[pl.ds(0, 3), :, pl.ds(0, 2)]
        which = 2 * part + ring
        device = self.here.at_axis("x", lax.rem(self.here.x + 1, self.side))
        return rcopy(ref, ref, self.sems.at[0, which], self.sems.at[1, which], device)

    def start(self):
        if self.here.tok > 1:
            for ring in (0, 1):
                for part in (0, 1):
                    self.go(part, ring, 0)

    def middle(self):
        if self.here.tok > 1:
            for part in (0, 1):
                self.whole(part, 0).wait_recv()
                for rel in (1, 3, 2):
                    self.go(part, 1, rel)

    def finish(self):
        if self.here.tok > 1:
            for part in (0, 1):
                self.whole(part, 1).wait_recv()

    def sent(self):
        if self.here.tok > 1:
            for part in (0, 1):
                for ring in (0, 1):
                    self.whole(part, ring).wait_send()


def group_copy(src, dst, sems, which, device):
    return rcopy(src, dst, sems.at[0, which], sems.at[1, which], device)


class Exchange:
    def __init__(self, at, others, device, src, dst, sems, which):
        self.at, self.others, self.device = at, others, device
        self.count = len(others) + 1
        self.src, self.dst, self.sems, self.which = src, dst, sems, which

    def send(self, to):
        group_copy(
            self.src.at[to], self.dst.at[self.at], self.sems, self.which, self.device(to)
        ).start()

    def send_all(self):
        for other in self.others:
            self.send(other)

    def keep(self):
        self.dst[self.at] = self.src[self.at]

    def all_of(self, ref, number):
        ref = ref.at[pl.ds(0, number)]
        return group_copy(ref, ref, self.sems, self.which, self.device((self.others or [self.at])[0]))

    def received(self, number=None):
        number = self.count - 1 if number is None else number
        if number:
            self.all_of(self.dst, number).wait_recv()

    def sent(self, number=None):
        number = self.count - 1 if number is None else number
        if number:
            self.all_of(self.src, number).wait_send()


def leaf_inverse(block):
    count = LEAF // HIGH
    shape = (HIGH, LEAF)
    lane = lax.broadcasted_iota(jnp.int32, shape, 1)
    sub = lax.broadcasted_iota(jnp.int32, shape, 0)

    def down(v, r):
        return jnp.broadcast_to(v[r : r + 1, :], shape)

    done = []
    rest = block.reshape(count, HIGH, LEAF)
    for s in range(count):
        c0 = HIGH * s
        here = rest[0]
        cols = [jnp.broadcast_to(here[:, c0 + j : c0 + j + 1], shape) for j in range(HIGH)]
        diag = (lane >= c0) & (lane < c0 + HIGH)
        first = jnp.where(diag, jnp.where(lane - c0 == sub, 1.0, 0.0), here)
        full, low = first, first
        pivots = jnp.ones(shape, F32)
        pivot = down(cols[0], 0)
        for j in range(HIGH):
            inverse = 1.0 / pivot
            if j + 1 < HIGH:
                cross = down(cols[j + 1], j) * down(cols[j], j + 1)
                later = down(cols[j + 1], j + 1) - cross * inverse
            others = jnp.where(sub == j, 0.0, cols[j])
            below = jnp.where(sub > j, cols[j], 0.0)
            for k in range(j + 1, HIGH):
                cols[k] = cols[k] - (others * down(cols[k], j)) * inverse
            full = full - (others * down(full, j)) * inverse
            low = low - (below * down(low, j)) * inverse
            pivots = jnp.where(sub == j, pivot, pivots)
            if j + 1 < HIGH:
                pivot = later
        solved = full / pivots
        done.append(jnp.where(lane < c0 + HIGH, low * lax.rsqrt(pivots), 0.0))
        if s + 1 < count:
            old = rest[1:]
            terms = [
                jnp.broadcast_to(old[:, :, c0 + k : c0 + k + 1], old.shape) * down(solved, k)[None]
                for k in range(HIGH)
            ]
            while len(terms) > 1:
                terms = [terms[i] + terms[i + 1] for i in range(0, len(terms), 2)]
            rest = jnp.where(diag[None], 0.0, old) - terms[0]
    return jnp.stack(done).reshape(LEAF, LEAF)


def dot(a, b):
    return jnp.dot(a, b, precision=HIGHEST, preferred_element_type=F32)


def dot_t(a, b):
    return lax.dot_general(
        a, b, (((1,), (1,)), ((), ())), precision=HIGHEST, preferred_element_type=F32
    )


def factor_inverse(m_ref, w_ref, others):
    size = m_ref.shape[0]
    w_ref[...] = jnp.zeros(w_ref.shape, F32)

    def turn(step, carry):
        at = pl.ds(pl.multiple_of(step * LEAF, LEAF), LEAF)
        w_ref[at, at] = leaf_inverse(m_ref[at, at])
        for b in range(size // LEAF):
            r0, r1 = b * LEAF, (b + 1) * LEAF

            @pl.when(step == b)
            def _():
                if b == 0:
                    others()
                inv = w_ref[r0:r1, r0:r1]
                if r0:
                    left = dot(inv, m_ref[r0:r1, :r0])
                    w_ref[r0:r1, :r0] = left
                if r1 < size:
                    back = dot_t(m_ref[r1:, r0:r1], inv)
                    for c in range(r1, size, LEAF):
                        m_ref[c:, c : c + LEAF] -= dot_t(
                            back[c - r1 :], back[c - r1 : c - r1 + LEAF]
                        )
                    m_ref[r1:, r0:r1] = -dot(back, inv)
                    if r0:
                        m_ref[r1:, :r0] -= dot(back, left)

        return carry

    lax.fori_loop(0, size // LEAF, turn, 0)


def tokens_at(full_ref, u, size):
    side, _, _, quarter, cols = full_ref.shape
    shard = 4 * quarter
    if size >= shard:
        m = size // shard
        if m <= side:
            part = full_ref[u * m // side, pl.ds(u * m % side, m)]
        else:
            part = full_ref[pl.ds(u * (m // side), m // side)]
    else:
        per = quarter // size
        part = full_ref[0, 0, u // per, pl.ds(u % per * size, size)]
    return part.reshape(size, cols)


def eight_rows(image_ref, row):
    side, _, _, quarter, _ = image_ref.shape
    shard, within = row // (4 * quarter), row % (4 * quarter)
    place = (shard // side, shard % side, within // quarter)
    if quarter == 8:
        return image_ref[place]
    return image_ref[(*place, pl.ds(pl.multiple_of(within % quarter, 8), 8))]


def thirds(x, axis=0):
    high = x.astype(BF16)
    rest = x - high.astype(F32)
    middle = rest.astype(BF16)
    return jnp.concatenate([high, middle, (rest - middle.astype(F32)).astype(BF16)], axis=axis)


def sum_thirds(x, axis=0):
    high, middle, low = jnp.split(x, 3, axis=axis)
    return high + (middle + low)


def masks(member_ref, line, groups):
    rows = lax.broadcasted_iota(jnp.int32, (line, line), 0)
    across = lax.broadcasted_iota(jnp.int32, (line, line), 1)
    row = jnp.broadcast_to(member_ref[...].astype(F32), (line, line))
    column = jnp.sum(jnp.where(rows == across, row, 0.0), axis=1, keepdims=True)
    wide = jnp.broadcast_to(column, (line, 128))
    spread = jnp.broadcast_to(wide[:, None, :], (line, 8, 128))
    return (row == column), [jnp.where(spread == g, 1.0, 0.0) for g in range(groups)]


def mixing(linked, rank):
    line = linked.shape[0]
    size = line * rank
    owner = lax.broadcasted_iota(jnp.int32, (size, line), 0) // rank
    block = lax.broadcasted_iota(jnp.int32, (size, line), 1)
    spread = jnp.where(owner == block, 1.0, 0.0).astype(BF16)
    tall = jnp.dot(spread, linked.astype(BF16), preferred_element_type=F32).astype(BF16)
    big = lax.dot_general(tall, spread, (((1,), (1,)), ((), ())), preferred_element_type=F32)
    rows = lax.broadcasted_iota(jnp.int32, (size, size), 0)
    across = lax.broadcasted_iota(jnp.int32, (size, size), 1)
    return jnp.where(rows % rank == across % rank, big, 0.0).astype(BF16)


def whole_kernel(
    groups, group_cols,
    acts_ref, init_ref, kept_ref, member_ref,
    bases_ref, latent_ref,
    full_ref, image_all, gram_ref, basis_ref, init_v, init_out, init_in,
    proj_out, proj_in, mixed_out, mixed_in, part_out, part_in, sum_out, sum_in,
    wide_out, wide_in, summed_out, summed_in, thirds_ref,
    own_ref, piece_out, piece_in, rows_out, rows_in,
    m_ref, w_ref, mix_ref, codes_out, codes_in, mapped, turned,
    local_sems, sems, xs, xr, cross_sems,
):
    here = Place()
    line, tok = here.line, here.tok
    rows = init_v.shape[0]
    rank, cols = basis_ref.shape
    total_rank = rank * tok
    tokens = line * proj_out.shape[2]
    reducers, per_tile = part_out.shape[:2]

    acts_copy = pltpu.make_async_copy(acts_ref, turned_acts(full_ref, here), local_sems.at[0])
    init_copy = pltpu.make_async_copy(init_ref, init_v, local_sems.at[1])
    acts_copy.start()
    init_copy.start()
    line_to, plane_to = line_others(here), plane_others(here)
    greet_start([here.in_line(k) for k in line_to] + [here.in_plane(p) for p in plane_to])
    init_copy.wait()
    turned_init = init_v[...].T
    if tok > 1:
        wide = jnp.concatenate([turned_init, jnp.zeros((total_rank, 128 - rows), F32)], axis=1)
        init_out[...] = wide.astype(BF16).reshape(init_out.shape)
    else:
        basis_ref[...] = turned_init.astype(BF16)
    acts_copy.wait()
    greet_finish(line + tok - 2)

    acts_x = Gather(here, full_ref, xs, xr)
    acts_x.start()
    spread = Exchange(here.p, plane_to, here.in_plane, init_out, init_in, sems, 0)
    if tok > 1:
        spread.send_all()
        spread.keep()
    same, member_masks = masks(member_ref, line, groups)
    linked = jnp.where(same, kept_ref[...].astype(F32), 0.0)
    mix_ref[...] = mixing(linked, rank)
    acts_x.finish()
    if tok > 1:
        spread.received()
        spread.sent()
        per = 128 // rows
        for c in range(tok // per):
            total = init_in[c * per].astype(F32)
            for d in range(1, per):
                total += pltpu.roll(init_in[c * per + d].astype(F32), d * rows, 1)
            basis_ref[:, c * 128 : c * 128 + 128] = total.astype(BF16)
    acts_x.sent()

    chunk = tokens // line
    per_step = 2 if line % 2 == 0 else 1
    steps = line // per_step

    def line_exchange(src, dst, which):
        return Exchange(here.k, line_to, here.in_line, src, dst, sems, which)

    reducing = here.k < reducers

    proj_x = line_exchange(proj_out, proj_in, 1)
    mixed_x = line_exchange(mixed_out, mixed_in, 2)
    part_x = line_exchange(part_out, part_in, 3)
    sum_x = line_exchange(sum_out, sum_in, 4)
    codes_x = line_exchange(codes_out, codes_in, 9)
    wide_x = line_exchange(wide_out, wide_in, 10)
    summed_x = line_exchange(summed_out, summed_in, 11)
    image_ref, mapped_image = image_all.at[0], image_all.at[1]
    mapped_x = Cross(here, mapped_image, cross_sems)

    def project(basis, finish, exchange):
        def body(d, carry):
            away = steps // 2 + (2 * (d % 2) - 1) * ((d + 1) // 2)
            u = (here.k // per_step + away) % steps
            proj = finish(
                lax.dot_general(
                    basis[...], tokens_at(full_ref, u, per_step * chunk),
                    (((1,), (1,)), ((), ())), preferred_element_type=F32,
                )
            )
            for v in range(per_step):
                c = u * per_step + v
                exchange.src[c] = proj[:, v * chunk : (v + 1) * chunk]

                @pl.when(c != here.k)
                def _():
                    exchange.send(c)

            return carry

        lax.fori_loop(0, steps, body, 0)
        exchange.keep()

    def acts():
        return full_ref[...].reshape(tokens, cols)

    project(basis_ref, lambda proj: proj.astype(BF16), proj_x)
    proj_x.received()
    stacked = proj_in[...].reshape(line * rank, chunk)
    mixed_out[...] = (
        jnp.dot(mix_ref[...], stacked, preferred_element_type=F32)
        .astype(BF16)
        .reshape(mixed_out.shape)
    )
    mixed_x.send_all()
    mixed_x.keep()
    mixed_x.received()
    mixed = jnp.concatenate([mixed_in[c] for c in range(line)], axis=1)
    own = jnp.dot(mixed, acts(), preferred_element_type=F32)
    own = own * (1.0 / tokens) + RIDGE * basis_ref[...].astype(F32)
    own_ref[...] = own
    chunks, split = piece_out.shape[0], tok // piece_out.shape[0]
    width = cols // chunks
    for c in range(chunks):
        piece_out[c] = own[:, c * width : (c + 1) * width]
    for to in plane_to:
        group_copy(
            piece_out.at[to // split], piece_in.at[here.p], sems, 12, here.in_plane(to)
        ).start()
    piece_in[here.p] = piece_out[here.p // split]
    thirds_ref[...] = thirds(own)
    project(thirds_ref, sum_thirds, wide_x)

    if tok > 1:
        arrived = piece_in.at[pl.ds(0, tok - 1)]
        piece_copy = group_copy(arrived, arrived, sems, 12, here.in_plane(plane_to[0]))
        piece_copy.wait_recv()
    kind, slot = here.p % split, here.p // split
    tile_at = 0
    for c in range(0, total_rank, LEAF):
        high = (total_rank - c) // tok
        mine = []
        for m in range(chunks):
            for r in range(0, high, 8):
                row = c + (split * m + kind) * high + r
                mine.append(piece_in[row // rank, pl.ds(pl.multiple_of(row % rank, 8), 8)])
        panel = piece_in[c // rank : (c + LEAF) // rank].reshape(LEAF, width)
        tile = dot_t(jnp.concatenate(mine, axis=0), panel)
        rows_out[:, tile_at : tile_at + high // 8] = tile.reshape(chunks, high // 8, 8, LEAF)
        tile_at += high // 8
    for d in sorted(range(1, chunks), key=lambda d: -min(d, chunks - d)):
        to = lax.rem(slot + d, chunks)
        group_copy(
            rows_out.at[to], rows_in.at[slot], sems, 13, here.in_plane(split * to + kind)
        ).start()
    rows_in[slot] = rows_out[slot]
    if tok > 1:
        arrived = rows_in.at[pl.ds(0, chunks - 1)]
        rows_copy = group_copy(arrived, arrived, sems, 13, here.in_plane(plane_to[0]))
        rows_copy.wait_recv()
    part_out[...] = jnp.sum(rows_in[...], axis=0).reshape(part_out.shape)

    def iteration(turn, carry):
        gram_at = gram_ref.at[turn]

        @pl.when(turn > 0)
        def _():
            whole = image_ref[...].reshape(total_rank, cols)
            tiles = []
            for c in range(0, total_rank, LEAF):
                high = (total_rank - c) // tok
                mine = [eight_rows(image_ref, c + here.p * high + r) for r in range(0, high, 8)]
                tile = dot_t(jnp.concatenate(mine, axis=0), whole[c : c + LEAF])
                tiles.append(tile.reshape(high // 8, 8, LEAF))
            part_out[...] = jnp.concatenate(tiles, axis=0).reshape(part_out.shape)

        for to in line_to:

            @pl.when(to < reducers)
            def _():
                part_x.send(to)

        @pl.when(turn == 0)
        def _():
            wide_x.received()
            split = thirds(wide_in[...].reshape(line * rank, chunk), axis=1)
            product = jnp.dot(mix_ref[...], split, preferred_element_type=F32)
            summed_out[...] = sum_thirds(product, axis=1).reshape(summed_out.shape)
            summed_x.send_all()
            summed_x.keep()

        @pl.when(turn == ITERS - 1)
        def _():
            own = full_ref[here.y, here.x].reshape(tokens // tok, cols).astype(F32)
            mapped[...] = dot_t(own, image_ref[...].reshape(total_rank, cols))

        @pl.when(reducing)
        def _():
            part_x.keep()
            part_x.received()
            totals = [
                jnp.sum(part_in[...] * mask[:, None], axis=0) for mask in member_masks
            ]
            for i in range(line):
                mine = member_masks[0][i][None] * totals[0]
                for g in range(1, groups):
                    mine += member_masks[g][i][None] * totals[g]
                sum_out[i] = mine
            sum_x.send_all()
            sum_x.keep()
            sum_x.received(reducers - 1)

        @pl.when(jnp.logical_not(reducing))
        def _():
            sum_x.received(reducers)

        gram_at[here.p] = sum_in[...].reshape(gram_ref.shape[2:])
        front = total_rank // tok // 8
        spans = [(0, front), (front, gram_ref.shape[2] - front)]

        def gram_copy(n, ref, to):
            return group_copy(ref, ref, sems, 5 + 2 * turn + n, here.in_plane(to))

        def gram_whole(n):
            return gram_copy(n, gram_at.at[pl.ds(0, tok - 1), pl.ds(*spans[n])], plane_to[0])

        if tok > 1:
            for n in (0, 1):
                for to in plane_to:
                    gram_copy(n, gram_at.at[here.p, pl.ds(*spans[n])], to).start()

        @pl.when(turn == 0)
        def _():
            summed_x.received()
            mixed = jnp.concatenate([summed_in[c] for c in range(line)], axis=1)
            product = sum_thirds(jnp.dot(thirds(mixed), acts(), preferred_element_type=F32))
            own = product * (1.0 / tokens) + RIDGE * own_ref[...]
            mapped_image[here.y, here.x] = own.reshape(image_all.shape[3:])
            mapped_x.start()

        def panels(n):
            if tok > 1:
                gram_whole(n).wait_recv()
            first = 0
            for c in range(0, total_rank, LEAF):
                count = (total_rank - c) // tok // 8
                if (c > 0) == (n > 0):
                    panel = gram_at[:, first : first + count].reshape(total_rank - c, LEAF)
                    m_ref[c:, c : c + LEAF] = panel * (1.0 / group_cols)
                first += count

        panels(0)

        @pl.when(turn == 0)
        def _():
            mapped_x.middle()

        @pl.when(reducing)
        def _():
            part_x.sent(reducers - 1)
            sum_x.sent()

        @pl.when(jnp.logical_not(reducing))
        def _():
            part_x.sent(reducers)

        factor_inverse(m_ref, w_ref, lambda: panels(1))
        if tok > 1:
            for n in (0, 1):
                gram_whole(n).wait_send()

        @pl.when(turn == 0)
        def _():
            mapped_x.finish()
            source = mapped_image[...].reshape(total_rank, cols)
            upper = total_rank // 2
            image_ref[...] = jnp.concatenate(
                [dot(w_ref[:upper, :upper], source[:upper]), dot(w_ref[upper:, :], source)], axis=0
            ).reshape(image_all.shape[1:])

        return carry

    lax.fori_loop(0, ITERS, iteration, 0)

    codes = dot_t(mapped[...], w_ref[...]).reshape(line, -1, total_rank)
    half = total_rank // 2
    codes_out[...] = jnp.concatenate([codes[:, :, :half], codes[:, :, half:]], axis=1).astype(BF16)
    codes_x.send_all()
    codes_x.keep()
    wide = turned.shape[0]
    per = wide // rows
    at = pl.multiple_of(here.p // per * wide, wide)
    part = image_all[0, :, :, :, :, pl.ds(at, wide)].reshape(total_rank, wide)
    turned[...] = dot(w_ref[...], part).T
    bases_ref[...] = turned[pl.ds(pl.multiple_of(here.p % per * rows, rows), rows), :]
    codes_x.received()
    scale = 1.0 / math.sqrt(group_cols)
    few = latent_ref.shape[0]
    for g in range(groups):
        for c in range(0, half, 128 if half % 128 == 0 else half):
            size = min(128, half)
            mask = member_masks[g][:, :1, :size]
            total = jnp.sum(codes_in[:, :, c : c + size].astype(F32) * mask, axis=0) * scale
            for h in (0, 1):
                at = g * total_rank + h * half + c
                latent_ref[:, at : at + size] = total[h * few : (h + 1) * few].astype(BF16)
    codes_x.sent()
    for exchange in (proj_x, mixed_x, wide_x, summed_x, mapped_x):
        exchange.sent()
    if tok > 1:
        piece_copy.wait_send()
        rows_copy.wait_send()


def turned_acts(full_ref, here):
    return full_ref.at[here.y, here.x]


def greet_start(devices):
    barrier = pltpu.get_barrier_semaphore()
    for device in devices:
        pl.semaphore_signal(barrier, inc=1, device_id=device, device_id_type=MESH)


def greet_finish(count):
    pl.semaphore_wait(pltpu.get_barrier_semaphore(), count)


def per_device(acts, init_basis, kept, member):
    tok = lax.axis_size("tok")
    line = lax.axis_size("gr") * lax.axis_size("gc")
    side = math.isqrt(tok)
    groups = kept.shape[0] // GBLK
    rows, total_rank = init_basis.shape[1:]
    shard, cols = acts.shape
    tokens = shard * tok
    rank = total_rank // tok
    group_cols = GBLK * rows * tok
    tiles = sum((total_rank - c) // tok // 8 for c in range(0, total_rank, LEAF))
    reducers = max(d for d in range(1, line + 1) if tiles % d == 0)
    per_tile = tiles // reducers
    chunks = max(1, tok // 2)
    pieces = (line, rank, tokens // line)
    init_pieces = (tok, rank, 128)
    codes = (line, shard // line * 2, total_rank // 2)
    bases, latent = pl.pallas_call(
        functools.partial(whole_kernel, groups, group_cols),
        out_shape=(
            jax.ShapeDtypeStruct((rows, total_rank), F32),
            jax.ShapeDtypeStruct((shard // line, groups * total_rank), BF16),
        ),
        in_specs=[pl.BlockSpec(memory_space=pl.ANY), pl.BlockSpec(memory_space=pl.ANY), vmem(), vmem()],
        out_specs=(vmem(), vmem()),
        scratch_shapes=[
            pltpu.VMEM((side, side, 4, shard // 4, cols), BF16),
            pltpu.VMEM((2, side, side, 4, rank // 4, cols), F32),
            pltpu.VMEM((ITERS, tok, tiles, 8, LEAF), F32),
            pltpu.VMEM((rank, cols), BF16),
            pltpu.VMEM((rows, total_rank), F32),
            pltpu.VMEM(init_pieces, BF16),
            pltpu.VMEM(init_pieces, BF16),
            pltpu.VMEM(pieces, BF16),
            pltpu.VMEM(pieces, BF16),
            pltpu.VMEM(pieces, BF16),
            pltpu.VMEM(pieces, BF16),
            pltpu.VMEM((reducers, per_tile, 8, LEAF), F32),
            pltpu.VMEM((line, per_tile, 8, LEAF), F32),
            pltpu.VMEM((line, per_tile, 8, LEAF), F32),
            pltpu.VMEM((reducers, per_tile, 8, LEAF), F32),
            pltpu.VMEM(pieces, F32),
            pltpu.VMEM(pieces, F32),
            pltpu.VMEM(pieces, F32),
            pltpu.VMEM(pieces, F32),
            pltpu.VMEM((3 * rank, cols), BF16),
            pltpu.VMEM((rank, cols), F32),
            pltpu.VMEM((chunks, rank, cols // chunks), F32),
            pltpu.VMEM((tok, rank, cols // chunks), F32),
            pltpu.VMEM((chunks, tiles, 8, LEAF), F32),
            pltpu.VMEM((chunks, tiles, 8, LEAF), F32),
            pltpu.VMEM((total_rank, total_rank), F32),
            pltpu.VMEM((total_rank, total_rank), F32),
            pltpu.VMEM((line * rank, line * rank), BF16),
            pltpu.VMEM(codes, BF16),
            pltpu.VMEM(codes, BF16),
            pltpu.VMEM((shard, total_rank), F32),
            pltpu.VMEM((max(rows, 128), total_rank), F32),
            pltpu.SemaphoreType.DMA((2,)),
            pltpu.SemaphoreType.DMA((2, 14)),
            pltpu.SemaphoreType.DMA((2,)),
            pltpu.SemaphoreType.DMA((2, 20)),
            pltpu.SemaphoreType.DMA((2, 4)),
        ],
        compiler_params=params(0),
    )(acts.reshape(4, shard // 4, cols), init_basis[0], kept, member.reshape(1, -1))
    return bases[None], latent


def solution(mesh):
    placed = (P("tok", ("gr", "gc")), P(("gr", "gc"), "tok", None), P(), P())
    return jax.shard_map(
        per_device,
        mesh=mesh,
        in_specs=placed,
        out_specs=(P(("gr", "gc"), "tok", None), P(("tok", "gr", "gc"), None)),
        check_vma=False,
    )
```

```python
import functools
import math

import jax
import jax.numpy as jnp
from jax import lax
from jax.experimental import pallas as pl
from jax.experimental.pallas import tpu as pltpu
from jax.sharding import PartitionSpec as P

GBLK = 8
ITERS = 2
RIDGE = 2.0
LEAF = 128
HIGH = 16
MESH = pl.DeviceIdType.MESH
HIGHEST = lax.Precision.HIGHEST
VMEM_LIMIT = 60 * 2**20
F32 = jnp.float32
BF16 = jnp.bfloat16


def vmem():
    return pl.BlockSpec(memory_space=pltpu.VMEM)


def smem():
    return pl.BlockSpec(memory_space=pltpu.SMEM)


def params(collective_id=None):
    if collective_id is None:
        return pltpu.CompilerParams(vmem_limit_bytes=VMEM_LIMIT)
    return pltpu.CompilerParams(
        vmem_limit_bytes=VMEM_LIMIT, collective_id=collective_id, has_side_effects=True
    )


class Place:
    def __init__(self):
        self.tok = lax.axis_size("tok")
        self.gc = lax.axis_size("gc")
        self.line = lax.axis_size("gr") * self.gc
        self.side = math.isqrt(self.tok)
        self.p = lax.axis_index("tok")
        self.gr_at = lax.axis_index("gr")
        self.gc_at = lax.axis_index("gc")
        self.k = self.gr_at * self.gc + self.gc_at
        self.y = self.p // self.side
        self.x = self.p % self.side

    def in_plane(self, p):
        return (p, self.gr_at, self.gc_at)

    def in_line(self, k):
        return (self.p, k // self.gc, k % self.gc)

    def at_axis(self, axis, at):
        if axis == "x":
            return self.in_plane(self.y * self.side + at)
        return self.in_plane(at * self.side + self.x)


def greet(devices):
    barrier = pltpu.get_barrier_semaphore()
    for device in devices:
        pl.semaphore_signal(barrier, inc=1, device_id=device, device_id_type=MESH)
    if devices:
        pl.semaphore_wait(barrier, len(devices))


def line_others(here):
    steps = sorted(range(1, here.line), key=lambda d: -min(d, here.line - d))
    return [lax.rem(here.k + d, here.line) for d in steps]


def plane_others(here):
    side = here.side
    steps = [(dy, dx) for dy in range(side) for dx in range(side)][1:]
    steps.sort(key=lambda d: -sum(min(a, side - a) for a in d))
    return [lax.rem(here.y + dy, side) * side + lax.rem(here.x + dx, side) for dy, dx in steps]


def ring_devices(here):
    if here.tok == 1:
        return []
    side = here.side
    return [
        here.at_axis(axis, (at + d) % side)
        for axis, at in (("x", here.x), ("y", here.y))
        for d in (1, side - 1)
    ]


def rcopy(src, dst, send, recv, device):
    return pltpu.make_async_remote_copy(
        src_ref=src, dst_ref=dst, send_sem=send, recv_sem=recv, device_id=device, device_id_type=MESH
    )


class Gather:
    PARTS = ((0, 2), (0, 2), (0, 1), (1, 1))

    def __init__(self, here, buf, send, recv):
        self.here, self.buf, self.send, self.recv = here, buf, send, recv
        self.side = here.side
        self.axes = (("x", "y"), ("y", "x"))
        self.at = ((here.x, here.y), (here.y, here.x))

    def near(self, part, ring, step):
        return lax.rem(self.at[part][ring] + step, self.side)

    def copy(self, part, ring, kind, owner, rel, slot):
        low, number = self.PARTS[kind]
        first, second = (owner, self.at[part][1]) if ring == 0 else (self.near(part, 0, rel), owner)
        y, x = (second, first) if part == 0 else (first, second)
        ref = self.buf.at[y, x, pl.ds(2 * part + low, number)]
        to = self.near(part, ring, 1 if kind in (0, 2) else self.side - 1)
        device = self.here.at_axis(self.axes[part][ring], to)
        return rcopy(ref, ref, self.send.at[ring], self.recv.at[part, slot], device)

    def one(self, part, kind, step):
        return self.copy(part, 0, kind, self.near(part, 0, step), 0, kind)

    def two(self, part, rel, kind, step):
        return self.copy(part, 1, kind, self.near(part, 1, step), rel, 4 + 4 * rel + kind)

    def start(self):
        if self.here.tok == 1:
            return
        for part in (0, 1):
            self.one(part, 0, 0).start()
            self.one(part, 1, 0).start()
        for part in (0, 1):
            self.share(part, 0)

    def share(self, part, rel):
        self.two(part, rel, 0, 0).start()
        self.two(part, rel, 1, 0).start()

    def pass_on(self, part, rel):
        self.two(part, rel, 0, 3).wait_recv()
        self.two(part, rel, 2, 3).start()
        self.two(part, rel, 1, 1).wait_recv()
        self.two(part, rel, 3, 1).start()

    def finish(self):
        if self.here.tok == 1:
            return
        for part in (0, 1):
            self.one(part, 0, 3).wait_recv()
            self.one(part, 2, 3).start()
            self.share(part, 3)
        for part in (0, 1):
            self.one(part, 1, 1).wait_recv()
            self.one(part, 3, 1).start()
            self.share(part, 1)
        for part in (0, 1):
            self.pass_on(part, 0)
        for part in (0, 1):
            self.one(part, 2, 2).wait_recv()
            self.one(part, 3, 2).wait_recv()
            self.share(part, 2)
        for rel in (3, 1, 2):
            for part in (0, 1):
                self.pass_on(part, rel)
        for rel in (0, 3, 1, 2):
            for part in (0, 1):
                self.two(part, rel, 2, 2).wait_recv()
                self.two(part, rel, 3, 2).wait_recv()

    def sent(self):
        if self.here.tok == 1:
            return
        device = self.here.at_axis("x", self.near(0, 0, 1))
        for ring, ref in ((0, self.buf.at[0, pl.ds(0, 3)]), (1, self.buf.at[pl.ds(0, 3)])):
            rcopy(ref, ref, self.send.at[ring], self.recv.at[0, 0], device).wait_send()


class Cross:
    def __init__(self, here, buf, sems):
        self.here, self.buf, self.sems = here, buf, sems
        self.side = here.side
        self.axes = (("x", "y"), ("y", "x"))
        self.at = ((here.x, here.y), (here.y, here.x))

    def go(self, part, ring, rel):
        first = lax.rem(self.at[part][0] + rel, self.side)
        second = self.at[part][1]
        y, x = (second, first) if part == 0 else (first, second)
        ref = self.buf.at[y, x, pl.ds(2 * part, 2)]
        which = 2 * part + ring
        for d in (2, 1, 3):
            to = lax.rem(self.at[part][ring] + d, self.side)
            device = self.here.at_axis(self.axes[part][ring], to)
            rcopy(ref, ref, self.sems.at[0, which], self.sems.at[1, which], device).start()

    def whole(self, part, ring):
        ref = self.buf.at[0, pl.ds(0, 3), pl.ds(0, 2)] if ring == 0 else self.buf.at[pl.ds(0, 3), :, pl.ds(0, 2)]
        which = 2 * part + ring
        device = self.here.at_axis("x", lax.rem(self.here.x + 1, self.side))
        return rcopy(ref, ref, self.sems.at[0, which], self.sems.at[1, which], device)

    def start(self):
        if self.here.tok > 1:
            for ring in (0, 1):
                for part in (0, 1):
                    self.go(part, ring, 0)

    def middle(self):
        if self.here.tok > 1:
            for part in (0, 1):
                self.whole(part, 0).wait_recv()
                for rel in (1, 3, 2):
                    self.go(part, 1, rel)

    def finish(self):
        if self.here.tok > 1:
            for part in (0, 1):
                self.whole(part, 1).wait_recv()

    def sent(self):
        if self.here.tok > 1:
            for part in (0, 1):
                for ring in (0, 1):
                    self.whole(part, ring).wait_send()


def group_copy(src, dst, sems, which, device):
    return rcopy(src, dst, sems.at[0, which], sems.at[1, which], device)


class Exchange:
    def __init__(self, at, others, device, src, dst, sems, which):
        self.at, self.others, self.device = at, others, device
        self.count = len(others) + 1
        self.src, self.dst, self.sems, self.which = src, dst, sems, which

    def send(self, to):
        group_copy(
            self.src.at[to], self.dst.at[self.at], self.sems, self.which, self.device(to)
        ).start()

    def send_all(self):
        for other in self.others:
            self.send(other)

    def keep(self):
        self.dst[self.at] = self.src[self.at]

    def all_of(self, ref, number):
        ref = ref.at[pl.ds(0, number)]
        return group_copy(ref, ref, self.sems, self.which, self.device((self.others or [self.at])[0]))

    def received(self, number=None):
        number = self.count - 1 if number is None else number
        if number:
            self.all_of(self.dst, number).wait_recv()

    def sent(self, number=None):
        number = self.count - 1 if number is None else number
        if number:
            self.all_of(self.src, number).wait_send()


def leaf_inverse(block):
    count = LEAF // HIGH
    shape = (HIGH, LEAF)
    lane = lax.broadcasted_iota(jnp.int32, shape, 1)
    sub = lax.broadcasted_iota(jnp.int32, shape, 0)

    def down(v, r):
        return jnp.broadcast_to(v[r : r + 1, :], shape)

    done = []
    rest = block.reshape(count, HIGH, LEAF)
    for s in range(count):
        c0 = HIGH * s
        here = rest[0]
        cols = [jnp.broadcast_to(here[:, c0 + j : c0 + j + 1], shape) for j in range(HIGH)]
        diag = (lane >= c0) & (lane < c0 + HIGH)
        first = jnp.where(diag, jnp.where(lane - c0 == sub, 1.0, 0.0), here)
        full, low = first, first
        pivots = jnp.ones(shape, F32)
        pivot = down(cols[0], 0)
        for j in range(HIGH):
            inverse = 1.0 / pivot
            if j + 1 < HIGH:
                cross = down(cols[j + 1], j) * down(cols[j], j + 1)
                later = down(cols[j + 1], j + 1) - cross * inverse
            others = jnp.where(sub == j, 0.0, cols[j])
            below = jnp.where(sub > j, cols[j], 0.0)
            for k in range(j + 1, HIGH):
                cols[k] = cols[k] - (others * down(cols[k], j)) * inverse
            full = full - (others * down(full, j)) * inverse
            low = low - (below * down(low, j)) * inverse
            pivots = jnp.where(sub == j, pivot, pivots)
            if j + 1 < HIGH:
                pivot = later
        solved = full / pivots
        done.append(jnp.where(lane < c0 + HIGH, low * lax.rsqrt(pivots), 0.0))
        if s + 1 < count:
            old = rest[1:]
            terms = [
                jnp.broadcast_to(old[:, :, c0 + k : c0 + k + 1], old.shape) * down(solved, k)[None]
                for k in range(HIGH)
            ]
            while len(terms) > 1:
                terms = [terms[i] + terms[i + 1] for i in range(0, len(terms), 2)]
            rest = jnp.where(diag[None], 0.0, old) - terms[0]
    return jnp.stack(done).reshape(LEAF, LEAF)


def dot(a, b):
    return jnp.dot(a, b, precision=HIGHEST, preferred_element_type=F32)


def halves(x):
    high = x.astype(BF16)
    return high, (x - high.astype(F32)).astype(BF16)


def dot3(a, b):
    (ah, al), (bh, bl) = halves(a), halves(b)

    def product(p, q):
        return jnp.dot(p, q, preferred_element_type=F32)

    return product(ah, bh) + (product(ah, bl) + product(al, bh))


def dot_t(a, b):
    return lax.dot_general(
        a, b, (((1,), (1,)), ((), ())), precision=HIGHEST, preferred_element_type=F32
    )


def factor_inverse(m_ref, w_ref, others):
    size = m_ref.shape[0]
    w_ref[...] = jnp.zeros(w_ref.shape, F32)

    def turn(step, carry):
        at = pl.ds(pl.multiple_of(step * LEAF, LEAF), LEAF)
        w_ref[at, at] = leaf_inverse(m_ref[at, at])
        for b in range(size // LEAF):
            r0, r1 = b * LEAF, (b + 1) * LEAF

            @pl.when(step == b)
            def _():
                if b < 2:
                    others(b)
                inv = w_ref[r0:r1, r0:r1]
                if r0:
                    left = dot(inv, m_ref[r0:r1, :r0])
                    w_ref[r0:r1, :r0] = left
                if r1 < size:
                    back = dot_t(m_ref[r1:, r0:r1], inv)
                    for c in range(r1, size, LEAF):
                        m_ref[c:, c : c + LEAF] -= dot_t(
                            back[c - r1 :], back[c - r1 : c - r1 + LEAF]
                        )
                    m_ref[r1:, r0:r1] = -dot(back, inv)
                    if r0:
                        m_ref[r1:, :r0] -= dot(back, left)

        return carry

    lax.fori_loop(0, size // LEAF, turn, 0)


def tokens_at(full_ref, u, size):
    side, _, _, quarter, cols = full_ref.shape
    shard = 4 * quarter
    if size >= shard:
        m = size // shard
        if m <= side:
            part = full_ref[u * m // side, pl.ds(u * m % side, m)]
        else:
            part = full_ref[pl.ds(u * (m // side), m // side)]
    else:
        per = quarter // size
        part = full_ref[0, 0, u // per, pl.ds(u % per * size, size)]
    return part.reshape(size, cols)


def eight_rows(image_ref, row):
    side, _, _, quarter, _ = image_ref.shape
    shard, within = row // (4 * quarter), row % (4 * quarter)
    place = (shard // side, shard % side, within // quarter)
    if quarter == 8:
        return image_ref[place]
    return image_ref[(*place, pl.ds(pl.multiple_of(within % quarter, 8), 8))]


def thirds(x, axis=0):
    high = x.astype(BF16)
    rest = x - high.astype(F32)
    middle = rest.astype(BF16)
    return jnp.concatenate([high, middle, (rest - middle.astype(F32)).astype(BF16)], axis=axis)


def sum_thirds(x, axis=0):
    high, middle, low = jnp.split(x, 3, axis=axis)
    return high + (middle + low)


def masks(member_ref, line, groups):
    rows = lax.broadcasted_iota(jnp.int32, (line, line), 0)
    across = lax.broadcasted_iota(jnp.int32, (line, line), 1)
    row = jnp.broadcast_to(member_ref[...].astype(F32), (line, line))
    column = jnp.sum(jnp.where(rows == across, row, 0.0), axis=1, keepdims=True)
    wide = jnp.broadcast_to(column, (line, 128))
    spread = jnp.broadcast_to(wide[:, None, :], (line, 8, 128))
    return (row == column), [jnp.where(spread == g, 1.0, 0.0) for g in range(groups)]


def mixing(linked, rank):
    line = linked.shape[0]
    size = line * rank
    owner = lax.broadcasted_iota(jnp.int32, (size, line), 0) // rank
    block = lax.broadcasted_iota(jnp.int32, (size, line), 1)
    spread = jnp.where(owner == block, 1.0, 0.0).astype(BF16)
    tall = jnp.dot(spread, linked.astype(BF16), preferred_element_type=F32).astype(BF16)
    big = lax.dot_general(tall, spread, (((1,), (1,)), ((), ())), preferred_element_type=F32)
    rows = lax.broadcasted_iota(jnp.int32, (size, size), 0)
    across = lax.broadcasted_iota(jnp.int32, (size, size), 1)
    return jnp.where(rows % rank == across % rank, big, 0.0).astype(BF16)


def whole_kernel(
    groups, group_cols,
    acts_ref, init_ref, kept_hbm, member_hbm,
    bases_ref, latent_ref,
    kept_ref, member_ref, full_ref, image_all, gram_ref, basis_ref, init_v, init_out, init_in,
    proj_out, proj_in, mixed_out, mixed_in, part_out, part_in, sum_out, sum_in,
    wide_out, wide_in, summed_out, summed_in, thirds_ref,
    own_ref, piece_out, piece_in, rows_out, rows_in,
    m_ref, w_ref, mix_ref, codes_out, codes_in, mapped, turned,
    local_sems, sems, xs, xr, cross_sems,
):
    here = Place()
    line, tok = here.line, here.tok
    rows = init_v.shape[0]
    rank, cols = basis_ref.shape
    total_rank = rank * tok
    tokens = line * proj_out.shape[2]
    reducers, per_tile = part_out.shape[:2]

    acts_copy = pltpu.make_async_copy(acts_ref, turned_acts(full_ref, here), local_sems.at[0])
    init_copy = pltpu.make_async_copy(init_ref, init_v, local_sems.at[1])
    kept_copy = pltpu.make_async_copy(kept_hbm, kept_ref, local_sems.at[2])
    member_copy = pltpu.make_async_copy(member_hbm, member_ref, local_sems.at[3])
    for copy in (acts_copy, init_copy, kept_copy, member_copy):
        copy.start()
    line_to, plane_to = line_others(here), plane_others(here)
    greet_start([here.in_line(k) for k in line_to] + [here.in_plane(p) for p in plane_to])
    init_copy.wait()
    turned_init = init_v[...].T
    if tok > 1:
        wide = jnp.concatenate([turned_init, jnp.zeros((total_rank, 128 - rows), F32)], axis=1)
        init_out[...] = wide.astype(BF16).reshape(init_out.shape)
    else:
        basis_ref[...] = turned_init.astype(BF16)
    acts_copy.wait()
    greet_finish(line + tok - 2)

    acts_x = Gather(here, full_ref, xs, xr)
    acts_x.start()
    spread = Exchange(here.p, plane_to, here.in_plane, init_out, init_in, sems, 0)
    if tok > 1:
        spread.send_all()
        spread.keep()
    kept_copy.wait()
    member_copy.wait()
    same, member_masks = masks(member_ref, line, groups)
    linked = jnp.where(same, kept_ref[...].astype(F32), 0.0)
    mix_ref[...] = mixing(linked, rank)
    acts_x.finish()
    if tok > 1:
        spread.received()
        spread.sent()
        per = 128 // rows
        for c in range(tok // per):
            total = init_in[c * per].astype(F32)
            for d in range(1, per):
                total += pltpu.roll(init_in[c * per + d].astype(F32), d * rows, 1)
            basis_ref[:, c * 128 : c * 128 + 128] = total.astype(BF16)
    acts_x.sent()

    chunk = tokens // line
    per_step = 2 if line % 2 == 0 else 1
    steps = line // per_step

    def line_exchange(src, dst, which):
        return Exchange(here.k, line_to, here.in_line, src, dst, sems, which)

    reducing = here.k < reducers

    proj_x = line_exchange(proj_out, proj_in, 1)
    mixed_x = line_exchange(mixed_out, mixed_in, 2)
    part_x = line_exchange(part_out, part_in, 3)
    sum_x = line_exchange(sum_out, sum_in, 4)
    codes_x = line_exchange(codes_out, codes_in, 9)
    wide_x = line_exchange(wide_out, wide_in, 10)
    summed_x = line_exchange(summed_out, summed_in, 11)
    image_ref, mapped_image = image_all.at[0], image_all.at[1]
    mapped_x = Cross(here, mapped_image, cross_sems)

    def project(basis, finish, exchange):
        def body(d, carry):
            away = steps // 2 + (2 * (d % 2) - 1) * ((d + 1) // 2)
            u = (here.k // per_step + away) % steps
            proj = finish(
                lax.dot_general(
                    basis[...], tokens_at(full_ref, u, per_step * chunk),
                    (((1,), (1,)), ((), ())), preferred_element_type=F32,
                )
            )
            for v in range(per_step):
                c = u * per_step + v
                exchange.src[c] = proj[:, v * chunk : (v + 1) * chunk]

                @pl.when(c != here.k)
                def _():
                    exchange.send(c)

            return carry

        lax.fori_loop(0, steps, body, 0)
        exchange.keep()

    def acts():
        return full_ref[...].reshape(tokens, cols)

    project(basis_ref, lambda proj: proj.astype(BF16), proj_x)
    proj_x.received()
    stacked = proj_in[...].reshape(line * rank, chunk)
    mixed_out[...] = (
        jnp.dot(mix_ref[...], stacked, preferred_element_type=F32)
        .astype(BF16)
        .reshape(mixed_out.shape)
    )
    mixed_x.send_all()
    mixed_x.keep()
    mixed_x.received()
    mixed = jnp.concatenate([mixed_in[c] for c in range(line)], axis=1)
    own = jnp.dot(mixed, acts(), preferred_element_type=F32)
    own = own * (1.0 / tokens) + RIDGE * basis_ref[...].astype(F32)
    own_ref[...] = own
    chunks, split = piece_out.shape[0], tok // piece_out.shape[0]
    width = cols // chunks
    for c in range(chunks):
        piece_out[c] = own[:, c * width : (c + 1) * width]
    for to in plane_to:
        group_copy(
            piece_out.at[to // split], piece_in.at[here.p], sems, 12, here.in_plane(to)
        ).start()
    piece_in[here.p] = piece_out[here.p // split]
    thirds_ref[...] = thirds(own)
    project(thirds_ref, sum_thirds, wide_x)

    if tok > 1:
        arrived = piece_in.at[pl.ds(0, tok - 1)]
        piece_copy = group_copy(arrived, arrived, sems, 12, here.in_plane(plane_to[0]))
        piece_copy.wait_recv()
    kind, slot = here.p % split, here.p // split
    tile_at = 0
    for c in range(0, total_rank, LEAF):
        high = (total_rank - c) // tok
        mine = []
        for m in range(chunks):
            for r in range(0, high, 8):
                row = c + (split * m + kind) * high + r
                mine.append(piece_in[row // rank, pl.ds(pl.multiple_of(row % rank, 8), 8)])
        panel = piece_in[c // rank : (c + LEAF) // rank].reshape(LEAF, width)
        tile = dot_t(jnp.concatenate(mine, axis=0), panel)
        rows_out[:, tile_at : tile_at + high // 8] = tile.reshape(chunks, high // 8, 8, LEAF)
        tile_at += high // 8
    for d in sorted(range(1, chunks), key=lambda d: -min(d, chunks - d)):
        to = lax.rem(slot + d, chunks)
        group_copy(
            rows_out.at[to], rows_in.at[slot], sems, 13, here.in_plane(split * to + kind)
        ).start()
    rows_in[slot] = rows_out[slot]
    if tok > 1:
        arrived = rows_in.at[pl.ds(0, chunks - 1)]
        rows_copy = group_copy(arrived, arrived, sems, 13, here.in_plane(plane_to[0]))
        rows_copy.wait_recv()
    part_out[...] = jnp.sum(rows_in[...], axis=0).reshape(part_out.shape)

    def iteration(turn, carry):
        gram_at = gram_ref.at[turn]

        @pl.when(turn > 0)
        def _():
            whole = image_ref[...].reshape(total_rank, cols)
            tiles = []
            for c in range(0, total_rank, LEAF):
                high = (total_rank - c) // tok
                mine = [eight_rows(image_ref, c + here.p * high + r) for r in range(0, high, 8)]
                tile = dot_t(jnp.concatenate(mine, axis=0), whole[c : c + LEAF])
                tiles.append(tile.reshape(high // 8, 8, LEAF))
            part_out[...] = jnp.concatenate(tiles, axis=0).reshape(part_out.shape)

        for to in line_to:

            @pl.when(to < reducers)
            def _():
                part_x.send(to)

        @pl.when(turn == 0)
        def _():
            wide_x.received()
            split = thirds(wide_in[...].reshape(line * rank, chunk), axis=1)
            product = jnp.dot(mix_ref[...], split, preferred_element_type=F32)
            summed_out[...] = sum_thirds(product, axis=1).reshape(summed_out.shape)
            summed_x.send_all()
            summed_x.keep()

        @pl.when(turn == ITERS - 1)
        def _():
            own = full_ref[here.y, here.x].reshape(tokens // tok, cols).astype(F32)
            mapped[...] = dot_t(own, image_ref[...].reshape(total_rank, cols))

        @pl.when(reducing)
        def _():
            part_x.keep()
            part_x.received()
            totals = [
                jnp.sum(part_in[...] * mask[:, None], axis=0) for mask in member_masks
            ]
            for i in range(line):
                mine = member_masks[0][i][None] * totals[0]
                for g in range(1, groups):
                    mine += member_masks[g][i][None] * totals[g]
                sum_out[i] = mine
            sum_x.send_all()
            sum_x.keep()
            sum_x.received(reducers - 1)

        @pl.when(jnp.logical_not(reducing))
        def _():
            sum_x.received(reducers)

        gram_at[here.p] = sum_in[...].reshape(gram_ref.shape[2:])
        front = total_rank // tok // 8
        spans = [(0, front), (front, gram_ref.shape[2] - front)]

        def gram_copy(n, ref, to):
            return group_copy(ref, ref, sems, 5 + 2 * turn + n, here.in_plane(to))

        def gram_whole(n):
            return gram_copy(n, gram_at.at[pl.ds(0, tok - 1), pl.ds(*spans[n])], plane_to[0])

        if tok > 1:
            for n in (0, 1):
                for to in plane_to:
                    gram_copy(n, gram_at.at[here.p, pl.ds(*spans[n])], to).start()

        @pl.when(turn == 0)
        def _():
            summed_x.received()
            mixed = jnp.concatenate([summed_in[c] for c in range(line)], axis=1)
            product = sum_thirds(jnp.dot(thirds(mixed), acts(), preferred_element_type=F32))
            own = product * (1.0 / tokens) + RIDGE * own_ref[...]
            mapped_image[here.y, here.x] = own.reshape(image_all.shape[3:])
            mapped_x.start()

        def panels(n):
            if tok > 1:
                gram_whole(n).wait_recv()
            first = 0
            for c in range(0, total_rank, LEAF):
                count = (total_rank - c) // tok // 8
                if (c > 0) == (n > 0):
                    panel = gram_at[:, first : first + count].reshape(total_rank - c, LEAF)
                    m_ref[c:, c : c + LEAF] = panel * (1.0 / group_cols)
                first += count

        panels(0)

        def more(b):
            if b == 0:
                panels(1)
                return

            @pl.when(turn == 0)
            def _():
                mapped_x.middle()

        @pl.when(reducing)
        def _():
            part_x.sent(reducers - 1)
            sum_x.sent()

        @pl.when(jnp.logical_not(reducing))
        def _():
            part_x.sent(reducers)

        factor_inverse(m_ref, w_ref, more)
        if tok > 1:
            for n in (0, 1):
                gram_whole(n).wait_send()

        @pl.when(turn == 0)
        def _():
            mapped_x.finish()
            source = mapped_image[...].reshape(total_rank, cols)
            upper = total_rank // 2
            image_ref[...] = jnp.concatenate(
                [dot3(w_ref[:upper, :upper], source[:upper]), dot3(w_ref[upper:, :], source)], axis=0
            ).reshape(image_all.shape[1:])

        return carry

    lax.fori_loop(0, ITERS, iteration, 0)

    codes = dot_t(mapped[...], w_ref[...]).reshape(line, -1, total_rank)
    half = total_rank // 2
    codes_out[...] = jnp.concatenate([codes[:, :, :half], codes[:, :, half:]], axis=1).astype(BF16)
    codes_x.send_all()
    codes_x.keep()
    wide = turned.shape[0]
    per = wide // rows
    at = pl.multiple_of(here.p // per * wide, wide)
    part = image_all[0, :, :, :, :, pl.ds(at, wide)].reshape(total_rank, wide)
    turned[...] = dot(w_ref[...], part).T
    bases_ref[...] = turned[pl.ds(pl.multiple_of(here.p % per * rows, rows), rows), :]
    codes_x.received()
    scale = 1.0 / math.sqrt(group_cols)
    few = latent_ref.shape[0]
    for g in range(groups):
        for c in range(0, half, 128 if half % 128 == 0 else half):
            size = min(128, half)
            mask = member_masks[g][:, :1, :size]
            total = jnp.sum(codes_in[:, :, c : c + size].astype(F32) * mask, axis=0) * scale
            for h in (0, 1):
                at = g * total_rank + h * half + c
                latent_ref[:, at : at + size] = total[h * few : (h + 1) * few].astype(BF16)
    codes_x.sent()
    for exchange in (proj_x, mixed_x, wide_x, summed_x, mapped_x):
        exchange.sent()
    if tok > 1:
        piece_copy.wait_send()
        rows_copy.wait_send()


def turned_acts(full_ref, here):
    return full_ref.at[here.y, here.x]


def greet_start(devices):
    barrier = pltpu.get_barrier_semaphore()
    for device in devices:
        pl.semaphore_signal(barrier, inc=1, device_id=device, device_id_type=MESH)


def greet_finish(count):
    pl.semaphore_wait(pltpu.get_barrier_semaphore(), count)


def per_device(acts, init_basis, kept, member):
    tok = lax.axis_size("tok")
    line = lax.axis_size("gr") * lax.axis_size("gc")
    side = math.isqrt(tok)
    groups = kept.shape[0] // GBLK
    rows, total_rank = init_basis.shape[1:]
    shard, cols = acts.shape
    tokens = shard * tok
    rank = total_rank // tok
    group_cols = GBLK * rows * tok
    tiles = sum((total_rank - c) // tok // 8 for c in range(0, total_rank, LEAF))
    reducers = max(d for d in range(1, line + 1) if tiles % d == 0)
    per_tile = tiles // reducers
    chunks = max(1, tok // 2)
    pieces = (line, rank, tokens // line)
    init_pieces = (tok, rank, 128)
    codes = (line, shard // line * 2, total_rank // 2)
    bases, latent = pl.pallas_call(
        functools.partial(whole_kernel, groups, group_cols),
        out_shape=(
            jax.ShapeDtypeStruct((rows, total_rank), F32),
            jax.ShapeDtypeStruct((shard // line, groups * total_rank), BF16),
        ),
        in_specs=[pl.BlockSpec(memory_space=pl.ANY)] * 4,
        out_specs=(vmem(), vmem()),
        scratch_shapes=[
            pltpu.VMEM(kept.shape, kept.dtype),
            pltpu.VMEM((1, kept.shape[0]), member.dtype),
            pltpu.VMEM((side, side, 4, shard // 4, cols), BF16),
            pltpu.VMEM((2, side, side, 4, rank // 4, cols), F32),
            pltpu.VMEM((ITERS, tok, tiles, 8, LEAF), F32),
            pltpu.VMEM((rank, cols), BF16),
            pltpu.VMEM((rows, total_rank), F32),
            pltpu.VMEM(init_pieces, BF16),
            pltpu.VMEM(init_pieces, BF16),
            pltpu.VMEM(pieces, BF16),
            pltpu.VMEM(pieces, BF16),
            pltpu.VMEM(pieces, BF16),
            pltpu.VMEM(pieces, BF16),
            pltpu.VMEM((reducers, per_tile, 8, LEAF), F32),
            pltpu.VMEM((line, per_tile, 8, LEAF), F32),
            pltpu.VMEM((line, per_tile, 8, LEAF), F32),
            pltpu.VMEM((reducers, per_tile, 8, LEAF), F32),
            pltpu.VMEM(pieces, F32),
            pltpu.VMEM(pieces, F32),
            pltpu.VMEM(pieces, F32),
            pltpu.VMEM(pieces, F32),
            pltpu.VMEM((3 * rank, cols), BF16),
            pltpu.VMEM((rank, cols), F32),
            pltpu.VMEM((chunks, rank, cols // chunks), F32),
            pltpu.VMEM((tok, rank, cols // chunks), F32),
            pltpu.VMEM((chunks, tiles, 8, LEAF), F32),
            pltpu.VMEM((chunks, tiles, 8, LEAF), F32),
            pltpu.VMEM((total_rank, total_rank), F32),
            pltpu.VMEM((total_rank, total_rank), F32),
            pltpu.VMEM((line * rank, line * rank), BF16),
            pltpu.VMEM(codes, BF16),
            pltpu.VMEM(codes, BF16),
            pltpu.VMEM((shard, total_rank), F32),
            pltpu.VMEM((max(rows, 128), total_rank), F32),
            pltpu.SemaphoreType.DMA((4,)),
            pltpu.SemaphoreType.DMA((2, 14)),
            pltpu.SemaphoreType.DMA((2,)),
            pltpu.SemaphoreType.DMA((2, 20)),
            pltpu.SemaphoreType.DMA((2, 4)),
        ],
        compiler_params=params(0),
    )(acts.reshape(4, shard // 4, cols), init_basis[0], kept, member.reshape(1, -1))
    return bases[None], latent


def solution(mesh):
    placed = (P("tok", ("gr", "gc")), P(("gr", "gc"), "tok", None), P(), P())
    return jax.shard_map(
        per_device,
        mesh=mesh,
        in_specs=placed,
        out_specs=(P(("gr", "gc"), "tok", None), P(("tok", "gr", "gc"), None)),
        check_vma=False,
    )
```

```python
import functools
import math

import jax
import jax.numpy as jnp
from jax import lax
from jax.experimental import pallas as pl
from jax.experimental.pallas import tpu as pltpu
from jax.sharding import PartitionSpec as P

GBLK = 8
ITERS = 2
RIDGE = 2.0
LEAF = 128
HIGH = 16
MESH = pl.DeviceIdType.MESH
HIGHEST = lax.Precision.HIGHEST
VMEM_LIMIT = 60 * 2**20
F32 = jnp.float32
BF16 = jnp.bfloat16


def vmem():
    return pl.BlockSpec(memory_space=pltpu.VMEM)


def smem():
    return pl.BlockSpec(memory_space=pltpu.SMEM)


def params(collective_id=None):
    if collective_id is None:
        return pltpu.CompilerParams(vmem_limit_bytes=VMEM_LIMIT)
    return pltpu.CompilerParams(
        vmem_limit_bytes=VMEM_LIMIT, collective_id=collective_id, has_side_effects=True
    )


class Place:
    def __init__(self):
        self.tok = lax.axis_size("tok")
        self.gc = lax.axis_size("gc")
        self.line = lax.axis_size("gr") * self.gc
        self.side = math.isqrt(self.tok)
        self.p = lax.axis_index("tok")
        self.gr_at = lax.axis_index("gr")
        self.gc_at = lax.axis_index("gc")
        self.k = self.gr_at * self.gc + self.gc_at
        self.y = self.p // self.side
        self.x = self.p % self.side

    def in_plane(self, p):
        return (p, self.gr_at, self.gc_at)

    def in_line(self, k):
        return (self.p, k // self.gc, k % self.gc)

    def at_axis(self, axis, at):
        if axis == "x":
            return self.in_plane(self.y * self.side + at)
        return self.in_plane(at * self.side + self.x)


def greet(devices):
    barrier = pltpu.get_barrier_semaphore()
    for device in devices:
        pl.semaphore_signal(barrier, inc=1, device_id=device, device_id_type=MESH)
    if devices:
        pl.semaphore_wait(barrier, len(devices))


def line_others(here):
    steps = sorted(range(1, here.line), key=lambda d: -min(d, here.line - d))
    return [lax.rem(here.k + d, here.line) for d in steps]


def plane_others(here):
    side = here.side
    steps = [(dy, dx) for dy in range(side) for dx in range(side)][1:]
    steps.sort(key=lambda d: -sum(min(a, side - a) for a in d))
    return [lax.rem(here.y + dy, side) * side + lax.rem(here.x + dx, side) for dy, dx in steps]


def ring_devices(here):
    if here.tok == 1:
        return []
    side = here.side
    return [
        here.at_axis(axis, (at + d) % side)
        for axis, at in (("x", here.x), ("y", here.y))
        for d in (1, side - 1)
    ]


def rcopy(src, dst, send, recv, device):
    return pltpu.make_async_remote_copy(
        src_ref=src, dst_ref=dst, send_sem=send, recv_sem=recv, device_id=device, device_id_type=MESH
    )


class Gather:
    PARTS = ((0, 2), (0, 2), (0, 1), (1, 1))

    def __init__(self, here, buf, send, recv):
        self.here, self.buf, self.send, self.recv = here, buf, send, recv
        self.side = here.side
        self.axes = (("x", "y"), ("y", "x"))
        self.at = ((here.x, here.y), (here.y, here.x))

    def near(self, part, ring, step):
        return lax.rem(self.at[part][ring] + step, self.side)

    def copy(self, part, ring, kind, owner, rel, slot):
        low, number = self.PARTS[kind]
        first, second = (owner, self.at[part][1]) if ring == 0 else (self.near(part, 0, rel), owner)
        y, x = (second, first) if part == 0 else (first, second)
        ref = self.buf.at[y, x, pl.ds(2 * part + low, number)]
        to = self.near(part, ring, 1 if kind in (0, 2) else self.side - 1)
        device = self.here.at_axis(self.axes[part][ring], to)
        return rcopy(ref, ref, self.send.at[ring], self.recv.at[part, slot], device)

    def one(self, part, kind, step):
        return self.copy(part, 0, kind, self.near(part, 0, step), 0, kind)

    def two(self, part, rel, kind, step):
        return self.copy(part, 1, kind, self.near(part, 1, step), rel, 4 + 4 * rel + kind)

    def start(self):
        if self.here.tok == 1:
            return
        for part in (0, 1):
            self.one(part, 0, 0).start()
            self.one(part, 1, 0).start()
        for part in (0, 1):
            self.share(part, 0)

    def share(self, part, rel):
        self.two(part, rel, 0, 0).start()
        self.two(part, rel, 1, 0).start()

    def pass_on(self, part, rel):
        self.two(part, rel, 0, 3).wait_recv()
        self.two(part, rel, 2, 3).start()
        self.two(part, rel, 1, 1).wait_recv()
        self.two(part, rel, 3, 1).start()

    def finish(self):
        if self.here.tok == 1:
            return
        for part in (0, 1):
            self.one(part, 0, 3).wait_recv()
            self.one(part, 2, 3).start()
            self.share(part, 3)
        for part in (0, 1):
            self.one(part, 1, 1).wait_recv()
            self.one(part, 3, 1).start()
            self.share(part, 1)
        for part in (0, 1):
            self.pass_on(part, 0)
        for part in (0, 1):
            self.one(part, 2, 2).wait_recv()
            self.one(part, 3, 2).wait_recv()
            self.share(part, 2)
        for rel in (3, 1, 2):
            for part in (0, 1):
                self.pass_on(part, rel)
        for rel in (0, 3, 1, 2):
            for part in (0, 1):
                self.two(part, rel, 2, 2).wait_recv()
                self.two(part, rel, 3, 2).wait_recv()

    def sent(self):
        if self.here.tok == 1:
            return
        device = self.here.at_axis("x", self.near(0, 0, 1))
        for ring, ref in ((0, self.buf.at[0, pl.ds(0, 3)]), (1, self.buf.at[pl.ds(0, 3)])):
            rcopy(ref, ref, self.send.at[ring], self.recv.at[0, 0], device).wait_send()


class Cross:
    def __init__(self, here, buf, sems):
        self.here, self.buf, self.sems = here, buf, sems
        self.side = here.side
        self.axes = (("x", "y"), ("y", "x"))
        self.at = ((here.x, here.y), (here.y, here.x))

    def go(self, part, ring, rel):
        first = lax.rem(self.at[part][0] + rel, self.side)
        second = self.at[part][1]
        y, x = (second, first) if part == 0 else (first, second)
        ref = self.buf.at[y, x, pl.ds(2 * part, 2)]
        which = 2 * part + ring
        for d in (2, 1, 3):
            to = lax.rem(self.at[part][ring] + d, self.side)
            device = self.here.at_axis(self.axes[part][ring], to)
            rcopy(ref, ref, self.sems.at[0, which], self.sems.at[1, which], device).start()

    def whole(self, part, ring):
        ref = self.buf.at[0, pl.ds(0, 3), pl.ds(0, 2)] if ring == 0 else self.buf.at[pl.ds(0, 3), :, pl.ds(0, 2)]
        which = 2 * part + ring
        device = self.here.at_axis("x", lax.rem(self.here.x + 1, self.side))
        return rcopy(ref, ref, self.sems.at[0, which], self.sems.at[1, which], device)

    def start(self):
        if self.here.tok > 1:
            for ring in (0, 1):
                for part in (0, 1):
                    self.go(part, ring, 0)

    def middle(self):
        if self.here.tok > 1:
            for part in (0, 1):
                self.whole(part, 0).wait_recv()
                for rel in (1, 3, 2):
                    self.go(part, 1, rel)

    def finish(self):
        if self.here.tok > 1:
            for part in (0, 1):
                self.whole(part, 1).wait_recv()

    def sent(self):
        if self.here.tok > 1:
            for part in (0, 1):
                for ring in (0, 1):
                    self.whole(part, ring).wait_send()


def group_copy(src, dst, sems, which, device):
    return rcopy(src, dst, sems.at[0, which], sems.at[1, which], device)


class Exchange:
    def __init__(self, at, others, device, src, dst, sems, which):
        self.at, self.others, self.device = at, others, device
        self.count = len(others) + 1
        self.src, self.dst, self.sems, self.which = src, dst, sems, which

    def send(self, to):
        group_copy(
            self.src.at[to], self.dst.at[self.at], self.sems, self.which, self.device(to)
        ).start()

    def send_all(self):
        for other in self.others:
            self.send(other)

    def keep(self):
        self.dst[self.at] = self.src[self.at]

    def all_of(self, ref, number):
        ref = ref.at[pl.ds(0, number)]
        return group_copy(ref, ref, self.sems, self.which, self.device((self.others or [self.at])[0]))

    def received(self, number=None):
        number = self.count - 1 if number is None else number
        if number:
            self.all_of(self.dst, number).wait_recv()

    def sent(self, number=None):
        number = self.count - 1 if number is None else number
        if number:
            self.all_of(self.src, number).wait_send()


def leaf_inverse(block):
    count = LEAF // HIGH
    shape = (HIGH, LEAF)
    lane = lax.broadcasted_iota(jnp.int32, shape, 1)
    sub = lax.broadcasted_iota(jnp.int32, shape, 0)

    def down(v, r):
        return jnp.broadcast_to(v[r : r + 1, :], shape)

    done = []
    rest = block.reshape(count, HIGH, LEAF)
    for s in range(count):
        c0 = HIGH * s
        here = rest[0]
        cols = [jnp.broadcast_to(here[:, c0 + j : c0 + j + 1], shape) for j in range(HIGH)]
        diag = (lane >= c0) & (lane < c0 + HIGH)
        first = jnp.where(diag, jnp.where(lane - c0 == sub, 1.0, 0.0), here)
        full, low = first, first
        pivots = jnp.ones(shape, F32)
        pivot = down(cols[0], 0)
        for j in range(HIGH):
            inverse = 1.0 / pivot
            if j + 1 < HIGH:
                cross = down(cols[j + 1], j) * down(cols[j], j + 1)
                later = down(cols[j + 1], j + 1) - cross * inverse
            others = jnp.where(sub == j, 0.0, cols[j])
            below = jnp.where(sub > j, cols[j], 0.0)
            for k in range(j + 1, HIGH):
                cols[k] = cols[k] - (others * down(cols[k], j)) * inverse
            full = full - (others * down(full, j)) * inverse
            low = low - (below * down(low, j)) * inverse
            pivots = jnp.where(sub == j, pivot, pivots)
            if j + 1 < HIGH:
                pivot = later
        solved = full / pivots
        done.append(jnp.where(lane < c0 + HIGH, low * lax.rsqrt(pivots), 0.0))
        if s + 1 < count:
            old = rest[1:]
            terms = [
                jnp.broadcast_to(old[:, :, c0 + k : c0 + k + 1], old.shape) * down(solved, k)[None]
                for k in range(HIGH)
            ]
            while len(terms) > 1:
                terms = [terms[i] + terms[i + 1] for i in range(0, len(terms), 2)]
            rest = jnp.where(diag[None], 0.0, old) - terms[0]
    return jnp.stack(done).reshape(LEAF, LEAF)


def dot(a, b):
    return jnp.dot(a, b, precision=HIGHEST, preferred_element_type=F32)


def halves(x):
    high = x.astype(BF16)
    return high, (x - high.astype(F32)).astype(BF16)


def dot3(a, b):
    (ah, al), (bh, bl) = halves(a), halves(b)

    def product(p, q):
        return jnp.dot(p, q, preferred_element_type=F32)

    return product(ah, bh) + (product(ah, bl) + product(al, bh))


def dot_t(a, b):
    return lax.dot_general(
        a, b, (((1,), (1,)), ((), ())), precision=HIGHEST, preferred_element_type=F32
    )


def factor_inverse(m_ref, w_ref, others):
    size = m_ref.shape[0]
    w_ref[...] = jnp.zeros(w_ref.shape, F32)

    def turn(step, carry):
        at = pl.ds(pl.multiple_of(step * LEAF, LEAF), LEAF)
        w_ref[at, at] = leaf_inverse(m_ref[at, at])
        for b in range(size // LEAF):
            r0, r1 = b * LEAF, (b + 1) * LEAF

            @pl.when(step == b)
            def _():
                if b < 2:
                    others(b)
                inv = w_ref[r0:r1, r0:r1]
                if r0:
                    left = dot3(inv, m_ref[r0:r1, :r0])
                    w_ref[r0:r1, :r0] = left
                if r1 < size:
                    back = dot_t(m_ref[r1:, r0:r1], inv)
                    for c in range(r1, size, LEAF):
                        m_ref[c:, c : c + LEAF] -= dot_t(
                            back[c - r1 :], back[c - r1 : c - r1 + LEAF]
                        )
                    m_ref[r1:, r0:r1] = -dot3(back, inv)
                    if r0:
                        m_ref[r1:, :r0] -= dot3(back, left)

        return carry

    lax.fori_loop(0, size // LEAF, turn, 0)


def tokens_at(full_ref, u, size):
    side, _, _, quarter, cols = full_ref.shape
    shard = 4 * quarter
    if size >= shard:
        m = size // shard
        if m <= side:
            part = full_ref[u * m // side, pl.ds(u * m % side, m)]
        else:
            part = full_ref[pl.ds(u * (m // side), m // side)]
    else:
        per = quarter // size
        part = full_ref[0, 0, u // per, pl.ds(u % per * size, size)]
    return part.reshape(size, cols)


def eight_rows(image_ref, row):
    side, _, _, quarter, _ = image_ref.shape
    shard, within = row // (4 * quarter), row % (4 * quarter)
    place = (shard // side, shard % side, within // quarter)
    if quarter == 8:
        return image_ref[place]
    return image_ref[(*place, pl.ds(pl.multiple_of(within % quarter, 8), 8))]


def thirds(x, axis=0):
    high = x.astype(BF16)
    rest = x - high.astype(F32)
    middle = rest.astype(BF16)
    return jnp.concatenate([high, middle, (rest - middle.astype(F32)).astype(BF16)], axis=axis)


def sum_thirds(x, axis=0):
    high, middle, low = jnp.split(x, 3, axis=axis)
    return high + (middle + low)


def masks(member_ref, line, groups):
    rows = lax.broadcasted_iota(jnp.int32, (line, line), 0)
    across = lax.broadcasted_iota(jnp.int32, (line, line), 1)
    row = jnp.broadcast_to(member_ref[...].astype(F32), (line, line))
    column = jnp.sum(jnp.where(rows == across, row, 0.0), axis=1, keepdims=True)
    wide = jnp.broadcast_to(column, (line, 128))
    spread = jnp.broadcast_to(wide[:, None, :], (line, 8, 128))
    return (row == column), [jnp.where(spread == g, 1.0, 0.0) for g in range(groups)]


def mixing(linked, rank):
    line = linked.shape[0]
    size = line * rank
    owner = lax.broadcasted_iota(jnp.int32, (size, line), 0) // rank
    block = lax.broadcasted_iota(jnp.int32, (size, line), 1)
    spread = jnp.where(owner == block, 1.0, 0.0).astype(BF16)
    tall = jnp.dot(spread, linked.astype(BF16), preferred_element_type=F32).astype(BF16)
    big = lax.dot_general(tall, spread, (((1,), (1,)), ((), ())), preferred_element_type=F32)
    rows = lax.broadcasted_iota(jnp.int32, (size, size), 0)
    across = lax.broadcasted_iota(jnp.int32, (size, size), 1)
    return jnp.where(rows % rank == across % rank, big, 0.0).astype(BF16)


def whole_kernel(
    groups, group_cols,
    acts_ref, init_ref, kept_hbm, member_hbm,
    bases_ref, latent_ref,
    kept_ref, member_ref, full_ref, image_all, gram_ref, basis_ref, init_v, init_out, init_in,
    proj_out, proj_in, mixed_out, mixed_in, part_out, part_in, sum_out, sum_in,
    wide_out, wide_in, summed_out, summed_in, thirds_ref,
    own_ref, piece_out, piece_in, rows_out, rows_in,
    m_ref, w_ref, mix_ref, codes_out, codes_in, mapped, turned,
    local_sems, sems, xs, xr, cross_sems,
):
    here = Place()
    line, tok = here.line, here.tok
    rows = init_v.shape[0]
    rank, cols = basis_ref.shape
    total_rank = rank * tok
    tokens = line * proj_out.shape[2]
    reducers, per_tile = part_out.shape[:2]

    acts_copy = pltpu.make_async_copy(acts_ref, turned_acts(full_ref, here), local_sems.at[0])
    init_copy = pltpu.make_async_copy(init_ref, init_v, local_sems.at[1])
    kept_copy = pltpu.make_async_copy(kept_hbm, kept_ref, local_sems.at[2])
    member_copy = pltpu.make_async_copy(member_hbm, member_ref, local_sems.at[3])
    for copy in (acts_copy, init_copy, kept_copy, member_copy):
        copy.start()
    line_to, plane_to = line_others(here), plane_others(here)
    greet_start([here.in_line(k) for k in line_to] + [here.in_plane(p) for p in plane_to])
    init_copy.wait()
    turned_init = init_v[...].T
    if tok > 1:
        wide = jnp.concatenate([turned_init, jnp.zeros((total_rank, 128 - rows), F32)], axis=1)
        init_out[...] = wide.astype(BF16).reshape(init_out.shape)
    else:
        basis_ref[...] = turned_init.astype(BF16)
    acts_copy.wait()
    greet_finish(line + tok - 2)

    acts_x = Gather(here, full_ref, xs, xr)
    acts_x.start()
    spread = Exchange(here.p, plane_to, here.in_plane, init_out, init_in, sems, 0)
    if tok > 1:
        spread.send_all()
        spread.keep()
    kept_copy.wait()
    member_copy.wait()
    same, member_masks = masks(member_ref, line, groups)
    linked = jnp.where(same, kept_ref[...].astype(F32), 0.0)
    mix_ref[...] = mixing(linked, rank)
    acts_x.finish()
    if tok > 1:
        spread.received()
        per = 128 // rows
        for c in range(tok // per):
            total = init_in[c * per].astype(F32)
            for d in range(1, per):
                total += pltpu.roll(init_in[c * per + d].astype(F32), d * rows, 1)
            basis_ref[:, c * 128 : c * 128 + 128] = total.astype(BF16)

    chunk = tokens // line
    per_step = 2 if line % 2 == 0 else 1
    steps = line // per_step

    def line_exchange(src, dst, which):
        return Exchange(here.k, line_to, here.in_line, src, dst, sems, which)

    reducing = here.k < reducers

    proj_x = line_exchange(proj_out, proj_in, 1)
    mixed_x = line_exchange(mixed_out, mixed_in, 2)
    part_x = line_exchange(part_out, part_in, 3)
    sum_x = line_exchange(sum_out, sum_in, 4)
    codes_x = line_exchange(codes_out, codes_in, 9)
    wide_x = line_exchange(wide_out, wide_in, 10)
    summed_x = line_exchange(summed_out, summed_in, 11)
    image_ref, mapped_image = image_all.at[0], image_all.at[1]
    mapped_x = Cross(here, mapped_image, cross_sems)

    def project(basis, finish, exchange):
        def body(d, carry):
            away = steps // 2 + (2 * (d % 2) - 1) * ((d + 1) // 2)
            u = (here.k // per_step + away) % steps
            proj = finish(
                lax.dot_general(
                    basis[...], tokens_at(full_ref, u, per_step * chunk),
                    (((1,), (1,)), ((), ())), preferred_element_type=F32,
                )
            )
            for v in range(per_step):
                c = u * per_step + v
                exchange.src[c] = proj[:, v * chunk : (v + 1) * chunk]

                @pl.when(c != here.k)
                def _():
                    exchange.send(c)

            return carry

        lax.fori_loop(0, steps, body, 0)
        exchange.keep()

    def acts():
        return full_ref[...].reshape(tokens, cols)

    project(basis_ref, lambda proj: proj.astype(BF16), proj_x)
    proj_x.received()
    stacked = proj_in[...].reshape(line * rank, chunk)
    mixed_out[...] = (
        jnp.dot(mix_ref[...], stacked, preferred_element_type=F32)
        .astype(BF16)
        .reshape(mixed_out.shape)
    )
    mixed_x.send_all()
    mixed_x.keep()
    mixed_x.received()
    mixed = jnp.concatenate([mixed_in[c] for c in range(line)], axis=1)
    own = jnp.dot(mixed, acts(), preferred_element_type=F32)
    own = own * (1.0 / tokens) + RIDGE * basis_ref[...].astype(F32)
    own_ref[...] = own
    chunks, split = piece_out.shape[0], tok // piece_out.shape[0]
    width = cols // chunks
    for c in range(chunks):
        piece_out[c] = own[:, c * width : (c + 1) * width]
    for to in plane_to:
        group_copy(
            piece_out.at[to // split], piece_in.at[here.p], sems, 12, here.in_plane(to)
        ).start()
    piece_in[here.p] = piece_out[here.p // split]
    thirds_ref[...] = thirds(own)
    project(thirds_ref, sum_thirds, wide_x)

    if tok > 1:
        arrived = piece_in.at[pl.ds(0, tok - 1)]
        piece_copy = group_copy(arrived, arrived, sems, 12, here.in_plane(plane_to[0]))
        piece_copy.wait_recv()
    kind, slot = here.p % split, here.p // split
    tile_at = 0
    for c in range(0, total_rank, LEAF):
        high = (total_rank - c) // tok
        mine = []
        for m in range(chunks):
            for r in range(0, high, 8):
                row = c + (split * m + kind) * high + r
                mine.append(piece_in[row // rank, pl.ds(pl.multiple_of(row % rank, 8), 8)])
        panel = piece_in[c // rank : (c + LEAF) // rank].reshape(LEAF, width)
        tile = dot_t(jnp.concatenate(mine, axis=0), panel)
        rows_out[:, tile_at : tile_at + high // 8] = tile.reshape(chunks, high // 8, 8, LEAF)
        tile_at += high // 8
    for d in sorted(range(1, chunks), key=lambda d: -min(d, chunks - d)):
        to = lax.rem(slot + d, chunks)
        group_copy(
            rows_out.at[to], rows_in.at[slot], sems, 13, here.in_plane(split * to + kind)
        ).start()
    rows_in[slot] = rows_out[slot]
    if tok > 1:
        arrived = rows_in.at[pl.ds(0, chunks - 1)]
        rows_copy = group_copy(arrived, arrived, sems, 13, here.in_plane(plane_to[0]))
        rows_copy.wait_recv()
    part_out[...] = jnp.sum(rows_in[...], axis=0).reshape(part_out.shape)

    def iteration(turn, carry):
        gram_at = gram_ref.at[turn]

        @pl.when(turn > 0)
        def _():
            whole = image_ref[...].reshape(total_rank, cols)
            tiles = []
            for c in range(0, total_rank, LEAF):
                high = (total_rank - c) // tok
                mine = [eight_rows(image_ref, c + here.p * high + r) for r in range(0, high, 8)]
                tile = dot_t(jnp.concatenate(mine, axis=0), whole[c : c + LEAF])
                tiles.append(tile.reshape(high // 8, 8, LEAF))
            part_out[...] = jnp.concatenate(tiles, axis=0).reshape(part_out.shape)

        for to in line_to:

            @pl.when(to < reducers)
            def _():
                part_x.send(to)

        @pl.when(turn == 0)
        def _():
            wide_x.received()
            split = thirds(wide_in[...].reshape(line * rank, chunk), axis=1)
            product = jnp.dot(mix_ref[...], split, preferred_element_type=F32)
            summed_out[...] = sum_thirds(product, axis=1).reshape(summed_out.shape)
            summed_x.send_all()
            summed_x.keep()

        @pl.when(turn == ITERS - 1)
        def _():
            own = full_ref[here.y, here.x].reshape(tokens // tok, cols).astype(F32)
            mapped[...] = dot_t(own, image_ref[...].reshape(total_rank, cols))

        @pl.when(reducing)
        def _():
            part_x.keep()
            part_x.received()
            totals = [
                jnp.sum(part_in[...] * mask[:, None], axis=0) for mask in member_masks
            ]
            for i in range(line):
                mine = member_masks[0][i][None] * totals[0]
                for g in range(1, groups):
                    mine += member_masks[g][i][None] * totals[g]
                sum_out[i] = mine
            sum_x.send_all()
            sum_x.keep()
            sum_x.received(reducers - 1)

        @pl.when(jnp.logical_not(reducing))
        def _():
            sum_x.received(reducers)

        gram_at[here.p] = sum_in[...].reshape(gram_ref.shape[2:])
        front = total_rank // tok // 8
        spans = [(0, front), (front, gram_ref.shape[2] - front)]

        def gram_copy(n, ref, to):
            return group_copy(ref, ref, sems, 5 + 2 * turn + n, here.in_plane(to))

        def gram_whole(n):
            return gram_copy(n, gram_at.at[pl.ds(0, tok - 1), pl.ds(*spans[n])], plane_to[0])

        if tok > 1:
            for n in (0, 1):
                for to in plane_to:
                    gram_copy(n, gram_at.at[here.p, pl.ds(*spans[n])], to).start()

        @pl.when(turn == 0)
        def _():
            summed_x.received()
            mixed = jnp.concatenate([summed_in[c] for c in range(line)], axis=1)
            product = sum_thirds(jnp.dot(thirds(mixed), acts(), preferred_element_type=F32))
            own = product * (1.0 / tokens) + RIDGE * own_ref[...]
            mapped_image[here.y, here.x] = own.reshape(image_all.shape[3:])
            mapped_x.start()

        def panels(n):
            if tok > 1:
                gram_whole(n).wait_recv()
            first = 0
            for c in range(0, total_rank, LEAF):
                count = (total_rank - c) // tok // 8
                if (c > 0) == (n > 0):
                    panel = gram_at[:, first : first + count].reshape(total_rank - c, LEAF)
                    m_ref[c:, c : c + LEAF] = panel * (1.0 / group_cols)
                first += count

        panels(0)

        def more(b):
            if b == 0:
                panels(1)
                return

            @pl.when(turn == 0)
            def _():
                mapped_x.middle()

        @pl.when(reducing)
        def _():
            part_x.sent(reducers - 1)
            sum_x.sent()

        @pl.when(jnp.logical_not(reducing))
        def _():
            part_x.sent(reducers)

        factor_inverse(m_ref, w_ref, more)
        if tok > 1:
            for n in (0, 1):
                gram_whole(n).wait_send()

        @pl.when(turn == 0)
        def _():
            mapped_x.finish()
            source = mapped_image[...].reshape(total_rank, cols)
            upper = total_rank // 2
            image_ref[...] = jnp.concatenate(
                [dot3(w_ref[:upper, :upper], source[:upper]), dot3(w_ref[upper:, :], source)], axis=0
            ).reshape(image_all.shape[1:])

        return carry

    lax.fori_loop(0, ITERS, iteration, 0)

    codes = dot_t(mapped[...], w_ref[...]).reshape(line, -1, total_rank)
    half = total_rank // 2
    codes_out[...] = jnp.concatenate([codes[:, :, :half], codes[:, :, half:]], axis=1).astype(BF16)
    codes_x.send_all()
    codes_x.keep()
    wide = turned.shape[0]
    per = wide // rows
    at = pl.multiple_of(here.p // per * wide, wide)
    part = image_all[0, :, :, :, :, pl.ds(at, wide)].reshape(total_rank, wide)
    turned[...] = dot(w_ref[...], part).T
    bases_ref[...] = turned[pl.ds(pl.multiple_of(here.p % per * rows, rows), rows), :]
    for exchange in (acts_x, proj_x, mixed_x, wide_x, summed_x, mapped_x):
        exchange.sent()
    if tok > 1:
        spread.sent()
        piece_copy.wait_send()
        rows_copy.wait_send()
    codes_x.received()
    scale = 1.0 / math.sqrt(group_cols)
    few = latent_ref.shape[0]
    for g in range(groups):
        for c in range(0, half, 128 if half % 128 == 0 else half):
            size = min(128, half)
            mask = member_masks[g][:, :1, :size]
            total = jnp.sum(codes_in[:, :, c : c + size].astype(F32) * mask, axis=0) * scale
            for h in (0, 1):
                at = g * total_rank + h * half + c
                latent_ref[:, at : at + size] = total[h * few : (h + 1) * few].astype(BF16)
    codes_x.sent()


def turned_acts(full_ref, here):
    return full_ref.at[here.y, here.x]


def greet_start(devices):
    barrier = pltpu.get_barrier_semaphore()
    for device in devices:
        pl.semaphore_signal(barrier, inc=1, device_id=device, device_id_type=MESH)


def greet_finish(count):
    pl.semaphore_wait(pltpu.get_barrier_semaphore(), count)


def per_device(acts, init_basis, kept, member):
    tok = lax.axis_size("tok")
    line = lax.axis_size("gr") * lax.axis_size("gc")
    side = math.isqrt(tok)
    groups = kept.shape[0] // GBLK
    rows, total_rank = init_basis.shape[1:]
    shard, cols = acts.shape
    tokens = shard * tok
    rank = total_rank // tok
    group_cols = GBLK * rows * tok
    tiles = sum((total_rank - c) // tok // 8 for c in range(0, total_rank, LEAF))
    reducers = max(d for d in range(1, line + 1) if tiles % d == 0)
    per_tile = tiles // reducers
    chunks = max(1, tok // 2)
    pieces = (line, rank, tokens // line)
    init_pieces = (tok, rank, 128)
    codes = (line, shard // line * 2, total_rank // 2)
    bases, latent = pl.pallas_call(
        functools.partial(whole_kernel, groups, group_cols),
        out_shape=(
            jax.ShapeDtypeStruct((rows, total_rank), F32),
            jax.ShapeDtypeStruct((shard // line, groups * total_rank), BF16),
        ),
        in_specs=[pl.BlockSpec(memory_space=pl.ANY)] * 4,
        out_specs=(vmem(), vmem()),
        scratch_shapes=[
            pltpu.VMEM(kept.shape, kept.dtype),
            pltpu.VMEM((1, kept.shape[0]), member.dtype),
            pltpu.VMEM((side, side, 4, shard // 4, cols), BF16),
            pltpu.VMEM((2, side, side, 4, rank // 4, cols), F32),
            pltpu.VMEM((ITERS, tok, tiles, 8, LEAF), F32),
            pltpu.VMEM((rank, cols), BF16),
            pltpu.VMEM((rows, total_rank), F32),
            pltpu.VMEM(init_pieces, BF16),
            pltpu.VMEM(init_pieces, BF16),
            pltpu.VMEM(pieces, BF16),
            pltpu.VMEM(pieces, BF16),
            pltpu.VMEM(pieces, BF16),
            pltpu.VMEM(pieces, BF16),
            pltpu.VMEM((reducers, per_tile, 8, LEAF), F32),
            pltpu.VMEM((line, per_tile, 8, LEAF), F32),
            pltpu.VMEM((line, per_tile, 8, LEAF), F32),
            pltpu.VMEM((reducers, per_tile, 8, LEAF), F32),
            pltpu.VMEM(pieces, F32),
            pltpu.VMEM(pieces, F32),
            pltpu.VMEM(pieces, F32),
            pltpu.VMEM(pieces, F32),
            pltpu.VMEM((3 * rank, cols), BF16),
            pltpu.VMEM((rank, cols), F32),
            pltpu.VMEM((chunks, rank, cols // chunks), F32),
            pltpu.VMEM((tok, rank, cols // chunks), F32),
            pltpu.VMEM((chunks, tiles, 8, LEAF), F32),
            pltpu.VMEM((chunks, tiles, 8, LEAF), F32),
            pltpu.VMEM((total_rank, total_rank), F32),
            pltpu.VMEM((total_rank, total_rank), F32),
            pltpu.VMEM((line * rank, line * rank), BF16),
            pltpu.VMEM(codes, BF16),
            pltpu.VMEM(codes, BF16),
            pltpu.VMEM((shard, total_rank), F32),
            pltpu.VMEM((max(rows, 128), total_rank), F32),
            pltpu.SemaphoreType.DMA((4,)),
            pltpu.SemaphoreType.DMA((2, 14)),
            pltpu.SemaphoreType.DMA((2,)),
            pltpu.SemaphoreType.DMA((2, 20)),
            pltpu.SemaphoreType.DMA((2, 4)),
        ],
        compiler_params=params(0),
    )(acts.reshape(4, shard // 4, cols), init_basis[0], kept, member.reshape(1, -1))
    return bases[None], latent


def solution(mesh):
    placed = (P("tok", ("gr", "gc")), P(("gr", "gc"), "tok", None), P(), P())
    return jax.shard_map(
        per_device,
        mesh=mesh,
        in_specs=placed,
        out_specs=(P(("gr", "gc"), "tok", None), P(("tok", "gr", "gc"), None)),
        check_vma=False,
    )
```
